128 devices in a mesh: section: 2 (over core), fsdp: 16 (over z, y), replica: 4 (over x).
Axes of the slice: x: 4, y: 4, z: 4, core: 2. Of those that a mesh axis runs over, the one named last changes fastest.
Arguments:
- pipe_ends: bfloat16 [2, 2, 4, 2048, 768], P('section', None, 'replica', 'fsdp'), may hold values from -6 to 6
- seq_lengths: int32 [2, 4, 4], P(None, 'replica'), may hold values from 1 to 2048, as said below
- norm1_gain: bfloat16 [2, 768], P('section', 'fsdp'), may hold values from 0.5 to 1.5
- norm1_bias: bfloat16 [2, 768], P('section', 'fsdp'), may hold values from -1 to 1
- norm2_gain: bfloat16 [2, 768], P('section', 'fsdp'), may hold values from 0.5 to 1.5
- norm2_bias: bfloat16 [2, 768], P('section', 'fsdp'), may hold values from -1 to 1
- qkv_weight: bfloat16 [2, 768, 2304], P('section', 'fsdp'), may hold values from -0.21875 to 0.21875
- qkv_bias: bfloat16 [2, 3, 768], P('section', None, 'fsdp'), may hold values from -1 to 1
- out_weight: bfloat16 [2, 768, 768], P('section', 'fsdp'), may hold values from -1.5 to 1.5
- out_bias: bfloat16 [2, 768], P('section', 'fsdp'), may hold values from -1 to 1
- up_weight: bfloat16 [2, 768, 3072], P('section', 'fsdp'), may hold values from -0.21875 to 0.21875
- up_bias: bfloat16 [2, 3072], P('section', 'fsdp'), may hold values from -1 to 1
- down_weight: bfloat16 [2, 3072, 768], P('section', 'fsdp'), may hold values from -0.109375 to 0.109375
- down_bias: bfloat16 [2, 768], P('section', 'fsdp'), may hold values from -1 to 1
Outputs:
- layer_out: bfloat16 [2, 2, 4, 2048, 768], P('section', None, 'replica', 'fsdp')
- input_grad: bfloat16 [2, 2, 4, 2048, 768], P('section', None, 'replica', 'fsdp')
- norm1_gain_grad: float32 [2, 768], P('section', 'fsdp')
- norm1_bias_grad: float32 [2, 768], P('section', 'fsdp')
- norm2_gain_grad: float32 [2, 768], P('section', 'fsdp')
- norm2_bias_grad: float32 [2, 768], P('section', 'fsdp')
- qkv_weight_grad: float32 [2, 768, 2304], P('section', 'fsdp')
- qkv_bias_grad: float32 [2, 3, 768], P('section', None, 'fsdp')
- out_weight_grad: float32 [2, 768, 768], P('section', 'fsdp')
- out_bias_grad: float32 [2, 768], P('section', 'fsdp')
- up_weight_grad: float32 [2, 768, 3072], P('section', 'fsdp')
- up_bias_grad: float32 [2, 3072], P('section', 'fsdp')
- down_weight_grad: float32 [2, 3072, 768], P('section', 'fsdp')
- down_bias_grad: float32 [2, 768], P('section', 'fsdp')
The draws below stay inside these ranges and needn't reach their ends.
Inputs may be any that keep to these rules, and one draw needn't show every extreme that they name: `seq_lengths`: in each micro-batch and group the 4 lengths sum to 2048; the sequence at a place drawn from the seed starts within the first 128 tokens and ends within the last 128; each other one is at most (127) // 3 long.
All inputs are finite; a program needn't handle non-finite values.
Results may differ from the reference program's by a relative error of at most 0.02.
Values may be sent and summed in bfloat16 or wider, within the bound.
No kernel may reach another device: no remote copies, remote signals or barrier semaphores. Data moves between devices by JAX's collectives and lax.ppermute only.
A program may use at most 256 MiB of HBM per device.

```python
import jax
import jax.numpy as jnp
from jax import lax

D = 768
HEADS = 12
FF = 3072
HEAD_DIM = 64
MICRO = 2
NSEQ = 4
GROUP = 2048
N_FSDP = 16
N_REPLICA = 4


def draw_seq_lengths(key, part):
    key = jax.random.fold_in(key, 11)
    short_key, place_key = jax.random.split(key)
    short_most = (GROUP // N_FSDP - 1) // (NSEQ - 1)
    short_len = jax.random.randint(short_key, (MICRO, N_REPLICA, NSEQ), 1, short_most + 1)
    longest = jax.random.randint(place_key, (MICRO, N_REPLICA, 1), 0, NSEQ)
    chosen = jnp.arange(NSEQ)[None, None, :] == longest
    others = jnp.sum(jnp.where(chosen, 0, short_len), axis=2, keepdims=True)
    return jnp.where(chosen, GROUP - others, short_len).astype(jnp.int32)


def level_of(own_key, shape, shards, low, top_value):
    gain = 1.0
    for axis_at, blocks in shards:
        draws = jax.random.uniform(jax.random.fold_in(jax.random.fold_in(own_key, 6), axis_at), (blocks,), jnp.float32, low / len(shards), top_value / len(shards))
        gain = gain * jnp.repeat(jnp.exp(draws), shape[axis_at] // blocks).reshape((-1,) + (1,) * (len(shape) - 1 - axis_at))
    return gain


def gaussian(stream_key, dims, deviation, most, pieces=(), kind=jnp.bfloat16):
    factor_of = level_of(stream_key, dims, pieces, -0.22, 0.18) if pieces else 1.0
    entries = jax.random.normal(stream_key, dims, jnp.float32) * deviation * factor_of
    return jnp.minimum(jnp.maximum(entries, -most), most).astype(kind)


def setup_inputs(seed: int = 0) -> dict:
    keys = jax.random.split(jax.random.key(seed), 15)
    return {
        "pipe_ends": gaussian(keys[0], (2, MICRO, N_REPLICA, GROUP, D), 1.0, 6.0, ((0, 2), (2, 4), (3, 16))),
        "seq_lengths": draw_seq_lengths(jax.random.fold_in(keys[14], 71), 0),
        "norm1_gain": jnp.clip(1.0 + 0.1 * jax.random.normal(keys[2], (2, D), jnp.float32), 0.5, 1.5).astype(jnp.bfloat16),
        "norm1_bias": gaussian(keys[3], (2, D), 0.2, 1.0, ((0, 2), (1, 16))),
        "norm2_gain": jnp.clip(1.0 + 0.1 * jax.random.normal(keys[4], (2, D), jnp.float32), 0.5, 1.5).astype(jnp.bfloat16),
        "norm2_bias": gaussian(keys[5], (2, D), 0.2, 1.0, ((0, 2), (1, 16))),
        "qkv_weight": gaussian(keys[6], (2, D, 3 * D), D ** -0.5, 0.21875, ((0, 2), (1, 16))),
        "qkv_bias": gaussian(keys[7], (2, 3, D), 0.2, 1.0, ((0, 2), (2, 16))),
        "out_weight": gaussian(keys[8], (2, D, D), (D // 48) ** -0.5, 1.5, ((0, 2), (1, 16))),
        "out_bias": gaussian(keys[9], (2, D), 0.2, 1.0, ((0, 2), (1, 16))),
        "up_weight": gaussian(keys[10], (2, D, FF), D ** -0.5, 0.21875, ((0, 2), (1, 16))),
        "up_bias": gaussian(keys[11], (2, FF), 0.2, 1.0, ((0, 2), (1, 16))),
        "down_weight": gaussian(keys[12], (2, FF, D), FF ** -0.5, 0.109375, ((0, 2), (1, 16))),
        "down_bias": gaussian(keys[13], (2, D), 0.2, 1.0, ((0, 2), (1, 16))),
    }


@jax.custom_vjp
def low(v):
    return lax.optimization_barrier(v.astype(jnp.bfloat16)).astype(jnp.float32)

@jax.custom_vjp
def low_back(v):
    return v

def low_keep(v):
    return (low(v), None)

def low_pass(kept, grad):
    return (grad,)

def back_keep(v):
    return (v, None)

def back_low(kept, grad):
    return (low(grad),)
low.defvjp(low_keep, low_pass)
low_back.defvjp(back_keep, back_low)
EPSILON = 1e-05
NEG_FILL = -1e+30
HIGH = lax.Precision.HIGHEST

def rotate(heads_in, cos_table, sin_table):
    cos_three = cos_table[:, None, :]
    sin_three = sin_table[:, None, :]
    lower = heads_in[:, :, 0:8]
    upper = heads_in[:, :, 8:16]
    return jnp.concatenate([lower * cos_three - upper * sin_three, upper * cos_three + lower * sin_three, heads_in[:, :, 16:]], axis=2)

def layout(global_rows, seq_lens):
    lengths = seq_lens.astype(jnp.int32)
    finish = jnp.cumsum(lengths).astype(jnp.int32)
    passed = global_rows[:, None] >= finish[None, :]
    segment = lax.optimization_barrier(jnp.sum(passed.astype(jnp.int32), axis=1)).astype(jnp.int32)
    seq_begin = lax.optimization_barrier(jnp.sum(jnp.where(passed, lengths[None, :], 0), axis=1)).astype(jnp.int32)
    return (segment, (global_rows - seq_begin).astype(jnp.int32))

def rotary_tables(positions):
    inv_freq = 10000.0 ** (-jnp.arange(8, dtype=jnp.float32) / 8.0)
    angles = positions.astype(jnp.float32)[:, None] * inv_freq[None, :]
    return (jnp.cos(angles), jnp.sin(angles))

def normalize(tok_rows, gain_vec, bias_vec):
    row_mean = lax.optimization_barrier(jnp.mean(tok_rows, axis=-1, keepdims=True))
    centered = tok_rows - row_mean
    row_var = lax.optimization_barrier(jnp.mean(centered * centered, axis=-1, keepdims=True))
    return centered * lax.rsqrt(row_var + EPSILON) * gain_vec + bias_vec

def attend(queries, keys_all, values_all, segment, block_rows):
    row_count = queries.shape[0]
    key_rows = jnp.arange(row_count, dtype=jnp.int32)

    def one_block(block_start):
        query_part = lax.dynamic_slice_in_dim(queries, block_start, block_rows, 0)
        query_rows = block_start + jnp.arange(block_rows, dtype=jnp.int32)
        query_seg = lax.dynamic_slice_in_dim(segment, block_start, block_rows, 0)
        allowed = (segment[None, :] == query_seg[:, None]) & (key_rows[None, :] <= query_rows[:, None])
        scores = low_back(jnp.einsum('qhd,khd->hqk', query_part, keys_all, precision=HIGH) * 0.125)
        masked = jnp.where(allowed[None], scores, NEG_FILL)
        row_top = lax.optimization_barrier(jnp.max(masked, axis=2, keepdims=True))
        exp_vals = jnp.exp(masked - row_top)
        attn_probs = exp_vals / lax.optimization_barrier(jnp.sum(exp_vals, axis=2, keepdims=True))
        return jnp.einsum('hqk,khd->qhd', low(attn_probs), values_all, precision=HIGH)
    starts = (jnp.arange(row_count // block_rows) * block_rows).astype(jnp.int32)
    blocks_out = lax.map(jax.checkpoint(one_block), starts)
    return blocks_out.reshape(row_count, -1)

def run_layer(tok_rows, weights, cos_table, sin_table, segment):
    gain_attn, bias_attn, gain_mlp, bias_mlp, w_qkv, b_qkv, w_out, b_out, w_up, b_up, w_down, b_down = weights
    row_count = tok_rows.shape[0]
    attn_in = low(normalize(tok_rows, gain_attn, bias_attn))
    qkv = low_back(jnp.dot(attn_in, w_qkv, precision=HIGH) + b_qkv.reshape(-1)).reshape(row_count, 3, HEADS, HEAD_DIM)
    queries = low(rotate(qkv[:, 0], cos_table, sin_table))
    keys_all = low(rotate(qkv[:, 1], cos_table, sin_table))
    values_all = low(qkv[:, 2])
    attn_mid = low(low_back(attend(queries, keys_all, values_all, segment, min(512, row_count))))
    attn_out = jnp.dot(attn_mid, w_out, precision=HIGH) + b_out
    mlp_in = low(normalize(tok_rows, gain_mlp, bias_mlp))
    up_proj = low_back(jnp.dot(mlp_in, w_up, precision=HIGH) + b_up)
    hidden = low(jax.nn.gelu(up_proj, approximate=False))
    return tok_rows + attn_out + jnp.dot(hidden, w_down, precision=HIGH) + b_down

def reference(pipe_ends, seq_lengths, norm1_gain, norm1_bias, norm2_gain, norm2_bias, qkv_weight, qkv_bias, out_weight, out_bias, up_weight, up_bias, down_weight, down_bias):
    params = [weight.astype(jnp.float32) for weight in (norm1_gain, norm1_bias, norm2_gain, norm2_bias, qkv_weight, qkv_bias, out_weight, out_bias, up_weight, up_bias, down_weight, down_bias)]
    early_params = tuple((weight[0] for weight in params))
    late_params = tuple((weight[1] for weight in params))
    groups = MICRO * N_REPLICA
    inputs = pipe_ends[0].astype(jnp.float32).reshape(groups, GROUP, D)
    cotangent = pipe_ends[1].astype(jnp.float32).reshape(groups, GROUP, D)
    lengths = seq_lengths.reshape(groups, NSEQ).astype(jnp.int32)
    all_rows = jnp.arange(GROUP, dtype=jnp.int32)

    def geometry(group_lens):
        segment, positions = layout(all_rows, group_lens)
        cos_table, sin_table = rotary_tables(positions)
        return (segment, cos_table, sin_table)
    segments, cosines, sines = lax.map(geometry, lengths)

    def full_pass(first_in, boundary_shift, first_weights, second_weights):

        def per_group(group_item):
            tok_rows, shift_rows, segment, cos_table, sin_table = group_item
            early_out = run_layer(tok_rows, first_weights, cos_table, sin_table, segment)
            boundary = low(low_back(early_out)) + shift_rows
            late_out = run_layer(boundary, second_weights, cos_table, sin_table, segment)
            return (early_out, late_out)
        return lax.map(jax.checkpoint(per_group), (first_in, boundary_shift, segments, cosines, sines))
    (early_all, late_all), pull_back = jax.vjp(full_pass, inputs, jnp.zeros_like(inputs), early_params, late_params)
    grad_inputs, grad_boundary, early_grads, late_grads = pull_back((jnp.zeros_like(early_all), cotangent))
    out_shape = (MICRO, N_REPLICA, GROUP, D)
    layer_out = jnp.stack([early_all.reshape(out_shape), late_all.reshape(out_shape)]).astype(jnp.bfloat16)
    input_grad = jnp.stack([grad_inputs.reshape(out_shape), grad_boundary.reshape(out_shape)]).astype(jnp.bfloat16)
    gradients = [jnp.stack([early_part, late_part]).astype(jnp.float32) for early_part, late_part in zip(early_grads, late_grads)]
    return (layer_out, input_grad, gradients[0], gradients[1], gradients[2], gradients[3], gradients[4], gradients[5], gradients[6], gradients[7], gradients[8], gradients[9], gradients[10], gradients[11])
```

```python
import jax
import jax.numpy as jnp
import numpy as np
from jax import lax
from jax.experimental import pallas as pl
from jax.experimental.pallas import tpu as pltpu
from jax.sharding import PartitionSpec as P

HEADS = 12
HEAD_DIM = 64
EPSILON = 1e-05
NEG_FILL = -1e30
WIDTH = 768
RING = 4
OWN_ROWS = 48
PACK = 64
LANES = 256
SPOT = 192
BF = jnp.bfloat16
F32 = jnp.float32
CORES = ("section", "fsdp")


def flat(core, a, b):
    return core * RING * RING + (a % RING) * RING + b % RING


def moves(step):
    return [
        (flat(core, a, b), step(core, a, b))
        for core in range(2)
        for a in range(RING)
        for b in range(RING)
        if step(core, a, b) is not None
    ]


def along_weights(by):
    return moves(lambda core, a, b: flat(core, a + by, b) if core == 0 else flat(core, a, b + by))


def along_tokens(by):
    return moves(lambda core, a, b: flat(core, a, b + by) if core == 0 else flat(core, a + by, b))


def send(value, pairs):
    return lax.ppermute(value, CORES, pairs)


def gathered_weights_axis(block):
    return [block] + [send(block, along_weights(-by)) for by in (1, 3, 2)]


ORDER = (0, 1, 3, 2)


def in_order(blocks):
    found = dict(zip(ORDER, blocks))
    return [found[i] for i in range(RING)]


def vmem_call(body, out_shapes, flops, scalars, *arrays):
    return pl.pallas_call(
        body,
        out_shape=out_shapes,
        in_specs=[pl.BlockSpec(memory_space=pltpu.SMEM)] * len(scalars)
        + [pl.BlockSpec(memory_space=pltpu.VMEM)] * len(arrays),
        out_specs=jax.tree.map(lambda _: pl.BlockSpec(memory_space=pltpu.VMEM), out_shapes),
        compiler_params=pltpu.CompilerParams(vmem_limit_bytes=56 * 1024 * 1024),
        cost_estimate=pl.CostEstimate(flops=flops, bytes_accessed=4_000_000, transcendentals=0),
    )(*scalars, *arrays)


def mm(left, right):
    return lax.dot_general(left, right, (((1,), (0,)), ((), ())), preferred_element_type=F32)


def mm_nt(left, right):
    return lax.dot_general(left, right, (((1,), (1,)), ((), ())), preferred_element_type=F32)


def mm_tn(left, right):
    return lax.dot_general(left, right, (((0,), (0,)), ((), ())), preferred_element_type=F32)


def order_body(dest_ref, b0, b1, b2, b3, w_ref, beta_ref):
    total = jnp.zeros((1, WIDTH), F32)
    for e, block in enumerate((b0, b1, b2, b3)):
        for d in range(RING):
            at = pl.multiple_of(dest_ref[e * RING + d] * OWN_ROWS, 16)
            w_ref[pl.ds(at, OWN_ROWS), :] = block[d * PACK : d * PACK + OWN_ROWS, :]
            extra = block[d * PACK + OWN_ROWS : (d + 1) * PACK, :].astype(F32)
            total = total + extra[0:1, :] + extra[1:2, :]
    beta_ref[...] = jnp.broadcast_to(total, beta_ref.shape)


def order_columns_split(dest, blocks):
    return vmem_call(
        order_body,
        (jax.ShapeDtypeStruct((WIDTH, WIDTH), BF), jax.ShapeDtypeStruct((8, WIDTH), F32)),
        1_000_000,
        (dest,),
        *blocks,
    )


def order_rows_body(dest_ref, b0, b1, b2, b3, out_ref, down_ref, beta_ref):
    total = jnp.zeros((1, WIDTH), F32)
    for e, block in enumerate((b0, b1, b2, b3)):
        at_out = pl.multiple_of(dest_ref[e] * OWN_ROWS, 16)
        at_down = pl.multiple_of(dest_ref[e] * SPOT, 16)
        out_ref[pl.ds(at_out, OWN_ROWS), :] = block[0:OWN_ROWS, :]
        down_ref[pl.ds(at_down, SPOT), :] = block[OWN_ROWS : OWN_ROWS + SPOT, :]
        extra = block[OWN_ROWS + SPOT :, :].astype(F32)
        total = total + extra[0:1, :] + extra[1:2, :]
    out_ref[SPOT:, :] = jnp.zeros((LANES - SPOT, WIDTH), BF)
    beta_ref[...] = jnp.broadcast_to(total, beta_ref.shape)


def order_rows_split(dest, blocks):
    return vmem_call(
        order_rows_body,
        (
            jax.ShapeDtypeStruct((LANES, WIDTH), BF),
            jax.ShapeDtypeStruct((WIDTH, WIDTH), BF),
            jax.ShapeDtypeStruct((8, WIDTH), F32),
        ),
        1_000_000,
        (dest,),
        *blocks,
    )


def cut_body(dest_ref, m_ref, s_ref, o0, o1, o2, o3):
    row = lax.broadcasted_iota(jnp.int32, (PACK - OWN_ROWS, WIDTH), 0)
    extra = jnp.where(row == 0, s_ref[0:1, :], 0.0).astype(BF)
    for e, out in enumerate((o0, o1, o2, o3)):
        for d in range(RING):
            at = pl.multiple_of(dest_ref[e * RING + d] * OWN_ROWS, 16)
            out[d * PACK : d * PACK + OWN_ROWS, :] = m_ref[pl.ds(at, OWN_ROWS), :].astype(BF)
            out[d * PACK + OWN_ROWS : (d + 1) * PACK, :] = extra


def cut_columns_split(dest, total, sums):
    shape = jax.ShapeDtypeStruct((LANES, WIDTH), BF)
    return vmem_call(cut_body, (shape,) * RING, 1_000_000, (dest,), total, sums)


def cut_rows_body(dest_ref, out_grad, down_grad, s_ref, o0, o1, o2, o3):
    row = lax.broadcasted_iota(jnp.int32, (PACK - OWN_ROWS, WIDTH), 0)
    extra = jnp.where(row == 0, s_ref[0:1, :], 0.0).astype(BF)
    for e, out in enumerate((o0, o1, o2, o3)):
        at_out = pl.multiple_of(dest_ref[e] * OWN_ROWS, 16)
        at_down = pl.multiple_of(dest_ref[e] * SPOT, 16)
        out[0:OWN_ROWS, :] = out_grad[pl.ds(at_out, OWN_ROWS), :].astype(BF)
        out[OWN_ROWS : OWN_ROWS + SPOT, :] = down_grad[pl.ds(at_down, SPOT), :].astype(BF)
        out[OWN_ROWS + SPOT :, :] = extra


def cut_rows_split(dest, out_grad, down_grad, sums):
    shape = jax.ShapeDtypeStruct((LANES, WIDTH), BF)
    return vmem_call(
        cut_rows_body, (shape,) * RING, 1_000_000, (dest,), out_grad, down_grad, sums
    )


def head_mask(value, head):
    lane = lax.broadcasted_iota(jnp.int32, value.shape, 1)
    return jnp.where((lane >= head * HEAD_DIM) & (lane < (head + 1) * HEAD_DIM), value, 0)


def allowed_pairs(starts_ref, info, e, rows):
    part = rows // RING
    pieces = []
    for d in range(RING):
        base = lax.broadcasted_iota(jnp.int32, (part, rows), 0) + starts_ref[e * RING + d]
        pieces.append(jnp.where((base >= info[0:1, :]) & (base <= info[1:2, :]), 0.0, NEG_FILL))
    return jnp.concatenate(pieces, axis=0)


def attend_body(starts_ref, info_ref, q_ref, kv0, kv1, kv2, kv3, mid_ref, lse_ref):
    rows = q_ref.shape[0]
    info = info_ref[...]
    q = q_ref[...]
    masked_q = [head_mask(q, h) for h in range(3)]
    tops, sums, accs = [None] * 3, [None] * 3, [None] * 3
    for e, kv in enumerate((kv0, kv1, kv2, kv3)):
        bias = allowed_pairs(starts_ref, info, e, rows)
        keys = kv[:, :LANES]
        values_t = kv[:, LANES:].T
        for h in range(3):
            scores = mm_nt(keys, masked_q[h]) + bias
            top = jnp.max(scores, axis=0, keepdims=True)
            if e:
                top = jnp.maximum(tops[h], top)
            probs = jnp.exp(scores - top)
            total = jnp.sum(probs, axis=0, keepdims=True)
            part = mm(values_t[h * HEAD_DIM : (h + 1) * HEAD_DIM, :], probs.astype(BF))
            if e:
                shrink = jnp.exp(tops[h] - top)
                total = total + sums[h] * shrink
                part = part + accs[h] * shrink
            tops[h], sums[h], accs[h] = top, total, part
    mids = [accs[h] / sums[h] for h in range(3)] + [jnp.zeros((HEAD_DIM, rows), F32)]
    mid_ref[...] = jnp.concatenate(mids, axis=0).T.astype(BF)
    for h in range(3):
        lse_ref[h : h + 1, :] = tops[h] + jnp.log(sums[h])
    lse_ref[3:, :] = jnp.zeros((5, rows), F32)


def attend(starts, info, q, kvs):
    rows = q.shape[0]
    return vmem_call(
        attend_body,
        (jax.ShapeDtypeStruct((rows, LANES), BF), jax.ShapeDtypeStruct((8, rows), F32)),
        6_000_000_000,
        (starts,),
        info,
        q,
        *kvs,
    )


def attend_back_body(
    starts_ref, info_ref, q_ref, do_ref, mid_ref, lse_ref, kv0, kv1, kv2, kv3, dq_ref, g0, g1, g2, g3
):
    rows = q_ref.shape[0]
    info = info_ref[...]
    q, do = q_ref[...], do_ref[...]
    lse = lse_ref[...]
    lane = lax.broadcasted_iota(jnp.int32, (8, LANES), 1)
    head = lax.broadcasted_iota(jnp.int32, (8, LANES), 0)
    pick = jnp.where(lane // HEAD_DIM == head, 1.0, 0.0)
    products = do.astype(F32) * mid_ref[...].astype(F32)
    delta = lax.dot_general(
        pick,
        products,
        (((1,), (1,)), ((), ())),
        precision=lax.Precision.HIGHEST,
        preferred_element_type=F32,
    )
    masked_q = [head_mask(q, h) for h in range(3)]
    masked_do = [head_mask(do, h) for h in range(3)]
    dq = [None] * 3
    for e, (kv, grad) in enumerate(zip((kv0, kv1, kv2, kv3), (g0, g1, g2, g3))):
        bias = allowed_pairs(starts_ref, info, e, rows)
        keys = kv[:, :LANES]
        keys_t = keys.T
        values = kv[:, LANES:]
        dk = jnp.zeros((rows, LANES), F32)
        dv = jnp.zeros((rows, LANES), F32)
        for h in range(3):
            scores = mm_nt(keys, masked_q[h]) + bias
            probs = jnp.exp(scores - lse[h : h + 1, :])
            dprobs = mm_nt(values, masked_do[h])
            dscores = (probs * (dprobs - delta[h : h + 1, :])).astype(BF)
            dv = dv + mm(probs.astype(BF), masked_do[h])
            dk = dk + mm(dscores, masked_q[h])
            part = mm(keys_t[h * HEAD_DIM : (h + 1) * HEAD_DIM, :], dscores)
            dq[h] = part if e == 0 else dq[h] + part
        grad[:, :LANES] = dk.astype(BF)
        grad[:, LANES:] = dv.astype(BF)
    dq_ref[...] = jnp.concatenate(dq + [jnp.zeros((HEAD_DIM, rows), F32)], axis=0).T


def attend_back(starts, info, q, do, mid, lse, kvs):
    rows = q.shape[0]
    grad = jax.ShapeDtypeStruct((rows, 2 * LANES), BF)
    return vmem_call(
        attend_back_body,
        (jax.ShapeDtypeStruct((rows, LANES), F32),) + (grad,) * RING,
        16_000_000_000,
        (starts,),
        info,
        q,
        do,
        mid,
        lse,
        *kvs,
    )


def rotate(value, tables):
    cos, below, above = tables
    return (
        value * cos
        + jnp.roll(value, -8, axis=1) * below
        + jnp.roll(value, 8, axis=1) * above
    )


def rotate_back(value, tables):
    cos, below, above = tables
    return (
        value * cos
        - jnp.roll(value, -8, axis=1) * below
        - jnp.roll(value, 8, axis=1) * above
    )


def unit_rows_of(rows):
    centered = rows - jnp.mean(rows, axis=-1, keepdims=True)
    inv_std = lax.rsqrt(jnp.mean(centered * centered, axis=-1, keepdims=True) + EPSILON)
    return centered * inv_std, inv_std


def gelu_slope(up_proj, cdf):
    density = jnp.exp(-0.5 * up_proj * up_proj) * 0.3989422804014327
    return cdf + up_proj * density


def forward_layer(tok_rows, weights, geometry):
    (w_qkv, beta_qkv), (w_up, beta_up), (w_out, w_down, beta_out) = weights
    starts, info, tables = geometry
    own = tok_rows.shape[0]
    unit, inv_std = unit_rows_of(tok_rows)
    x_all = jnp.concatenate(in_order(gathered_weights_axis(unit.astype(BF))), axis=0)
    qkv = mm(x_all, w_qkv) + beta_qkv[0:1]
    q = (rotate(qkv[:, :LANES], tables) * 0.125).astype(BF)
    k = rotate(qkv[:, LANES : 2 * LANES], tables).astype(BF)
    kv = jnp.concatenate([k, qkv[:, 2 * LANES :].astype(BF)], axis=1)
    kvs = in_order([kv] + [send(kv, along_tokens(-by)) for by in (1, 3, 2)])
    up_proj = mm(x_all, w_up) + beta_up[0:1]
    cdf = 0.5 * (1.0 + lax.erf(up_proj * 0.7071067811865476))
    hidden = (up_proj * cdf).astype(BF)
    slope = gelu_slope(up_proj, cdf).astype(BF)
    mlp = mm(hidden, w_down) + beta_out[0:1]
    mid, lse = attend(starts, info, q, kvs)
    partial = mm(mid, w_out) + mlp
    total = tok_rows + partial[:own]
    for by in (1, 3, 2):
        part = partial[by * own : (by + 1) * own].astype(BF)
        total = total + send(part, along_weights(by)).astype(F32)
    return total, (unit, inv_std, x_all, q, kvs, hidden, slope, mid, lse)


def backward_layer(grad_rows, weights, stored, geometry, dest, dest_rows):
    (w_qkv, unused), (w_up, unused), (w_out, w_down, unused) = weights
    starts, info, tables = geometry
    unit, inv_std, x_all, q, kvs, hidden, slope, mid, lse = stored
    own = grad_rows.shape[0]
    g_all = jnp.concatenate(in_order(gathered_weights_axis(grad_rows)), axis=0)
    do = mm_nt(g_all, w_out).astype(BF)
    dq, *dkvs = attend_back(starts, info, q, do, mid, lse, kvs)
    dkv = dkvs[0].astype(F32)
    for by in (1, 3, 2):
        dkv = dkv + send(dkvs[by], along_tokens(by)).astype(F32)
    grad_up = (mm_nt(g_all, w_down) * slope.astype(F32)).astype(BF)
    dx_up = mm_nt(grad_up, w_up)
    down_grad = mm_tn(hidden, g_all)
    out_grad = mm_tn(mid, g_all)
    sum_g = jnp.sum(g_all.astype(F32), axis=0, keepdims=True)
    rows_cut = cut_rows_split(dest_rows, out_grad, down_grad, sum_g)
    up_grad = mm_tn(x_all, grad_up)
    sum_up = jnp.sum(grad_up.astype(F32), axis=0, keepdims=True)
    up_cut = cut_columns_split(dest, up_grad, sum_up)
    grad_qkv = jnp.concatenate(
        [
            rotate_back(dq * 0.125, tables).astype(BF),
            rotate_back(dkv[:, :LANES], tables).astype(BF),
            dkv[:, LANES:].astype(BF),
        ],
        axis=1,
    )
    dx = mm_nt(grad_qkv, w_qkv) + dx_up
    total = dx[:own]
    for by in (1, 3, 2):
        part = dx[by * own : (by + 1) * own].astype(BF)
        total = total + send(part, along_weights(by)).astype(F32)
    qkv_grad = mm_tn(x_all, grad_qkv)
    sum_qkv = jnp.sum(grad_qkv.astype(F32), axis=0, keepdims=True)
    qkv_cut = cut_columns_split(dest, qkv_grad, sum_qkv)
    grad_in = grad_rows.astype(F32) + inv_std * (
        total
        - jnp.mean(total, axis=-1, keepdims=True)
        - unit * jnp.mean(total * unit, axis=-1, keepdims=True)
    )
    return grad_in, (qkv_cut, up_cut, rows_cut)


def over_tokens(cut):
    total = cut[0].astype(F32)
    for by in (1, 3, 2):
        total = total + send(cut[by], along_tokens(by)).astype(F32)
    return total.astype(BF)


def over_weights(total, tp):
    blocks = total.reshape(RING, PACK, WIDTH)

    def block_for(by):
        return lax.dynamic_index_in_dim(blocks, (tp + by) % RING, 0, keepdims=False)

    parts = [block_for(0)] + [send(block_for(by), along_weights(by)) for by in (1, 3, 2)]
    stacked = jnp.stack(in_order(parts))
    return jnp.stack(
        [
            lax.dynamic_index_in_dim(stacked, (tp - j) % RING, 0, keepdims=False)
            for j in range(RING)
        ]
    )


def to_core(value, core):
    return send(value, moves(lambda s, a, b: flat(core, a, b) if s != core else None))


def over_replicas(value, core):
    rest = lax.axis_size("replica")
    low = value.astype(BF)
    total = low.astype(F32)
    for by in range(1, rest):
        pairs = [(core * rest + i, core * rest + (i + by) % rest) for i in range(rest)]
        total = total + lax.ppermute(low, ("section", "replica"), pairs).astype(F32)
    return total


def hi_lo_rows(row):
    hi = row.astype(BF)
    lo = (row - hi.astype(F32)).astype(BF)
    return jnp.concatenate([hi, lo, jnp.zeros((14, row.shape[1]), BF)], axis=0)


def on_device(
    pipe_ends,
    seq_lengths,
    norm1_gain,
    norm1_bias,
    norm2_gain,
    norm2_bias,
    qkv_weight,
    qkv_bias,
    out_weight,
    out_bias,
    up_weight,
    up_bias,
    down_weight,
    down_bias,
):
    core = lax.axis_index("section")
    first = core == 0
    place = lax.axis_index("fsdp")
    a_at, b_at = place // RING, place % RING
    tp = jnp.where(first, a_at, b_at)
    sq = jnp.where(first, b_at, a_at)
    rows_dev = pipe_ends.shape[3]

    def block_of(weight_at, token_at):
        weight_at, token_at = weight_at % RING, token_at % RING
        return jnp.where(first, RING * weight_at + token_at, RING * token_at + weight_at)

    ring = jnp.arange(RING, dtype=jnp.int32)
    dest = block_of(tp + ring[None, :], sq + ring[:, None]).reshape(-1).astype(jnp.int32)
    dest_cut = block_of(ring[None, :] + 0 * ring[:, None], sq + ring[:, None])
    dest_cut = dest_cut.reshape(-1).astype(jnp.int32)
    dest_rows = ((sq + ring) % RING).astype(jnp.int32)

    gain1 = norm1_gain[0].astype(F32)
    bias1 = norm1_bias[0].astype(F32)
    gain2 = norm2_gain[0].astype(F32)
    bias2 = norm2_bias[0].astype(F32)
    own_qkv = qkv_weight[0].astype(F32)
    own_up = up_weight[0].astype(F32)
    spot = (jnp.arange(RING * RING) == place)[:, None]

    def spread(piece):
        return jnp.where(spot, piece[None, :], 0.0).reshape(1, -1)

    qkv_row = jnp.sum(bias1[:, None] * own_qkv, axis=0, keepdims=True) + jnp.concatenate(
        [spread(qkv_bias[0, i].astype(F32)) for i in range(3)], axis=1
    )
    up_row = jnp.sum(bias2[:, None] * own_up, axis=0, keepdims=True) + spread(
        up_bias[0].astype(F32)
    )
    out_row = spread(out_bias[0].astype(F32) + down_bias[0].astype(F32))
    pack_qkv = jnp.concatenate([(gain1[:, None] * own_qkv).astype(BF), hi_lo_rows(qkv_row)])
    pack_up = jnp.concatenate([(gain2[:, None] * own_up).astype(BF), hi_lo_rows(up_row)])
    pack_down = jnp.concatenate([down_weight[0], hi_lo_rows(out_row)])
    pack_qkv = pack_qkv.reshape(PACK, 3, RING, SPOT).transpose(2, 0, 1, 3)
    pack_qkv = jnp.pad(pack_qkv, ((0, 0), (0, 0), (0, 0), (0, LANES - SPOT)))
    pack_qkv = pack_qkv.reshape(RING, PACK, WIDTH)
    pack_up = pack_up.reshape(PACK, RING, RING, SPOT)
    up_by_a = pack_up.transpose(1, 0, 2, 3).reshape(RING, PACK, WIDTH)
    up_by_b = pack_up.transpose(2, 0, 1, 3).reshape(RING, PACK, WIDTH)
    swap = moves(lambda s, a, b: flat(1 - s, a, b))

    def both(own, other):
        return jnp.where(first, own, other), jnp.where(first, other, own)

    qkv_layers = both(pack_qkv, send(pack_qkv, swap))
    other_ends = send(
        jnp.where(first, pipe_ends[0, 1, 0], pipe_ends[0, 0, 0]), swap
    )
    own_end = jnp.where(first, pipe_ends[0, 0, 0], pipe_ends[0, 1, 0])
    tokens_in = jnp.where(first, own_end, other_ends)
    cotangent = jnp.where(first, other_ends, own_end)

    lens = lax.dynamic_index_in_dim(seq_lengths[:, 0], core, 0, keepdims=False)
    starts = (dest * rows_dev).astype(jnp.int32)
    rows_at = (starts[:RING, None] + jnp.arange(rows_dev, dtype=jnp.int32)[None, :]).reshape(-1)
    finish = jnp.cumsum(lens)
    begin = jnp.sum(
        jnp.where(rows_at[None, :] >= finish[:, None], lens[:, None], 0), axis=0
    ).astype(jnp.int32)
    info = jnp.concatenate(
        [begin[None, :], rows_at[None, :], jnp.zeros((6, rows_at.shape[0]), jnp.int32)], axis=0
    )
    lane = np.arange(LANES)
    in_head = lane % HEAD_DIM
    turned = (in_head < 16) & (lane < SPOT)
    inv_freq = (10000.0 ** (-(in_head % 8) / 8.0)).astype(np.float32)
    angles = (rows_at - begin).astype(F32)[:, None] * jnp.where(turned, inv_freq, 0.0)[None, :]
    cos, sin = jnp.cos(angles), jnp.sin(angles)
    tables = (
        cos,
        jnp.where((in_head < 8)[None, :], -sin, 0.0),
        jnp.where((in_head >= 8)[None, :], sin, 0.0),
    )
    geometry = (starts, info, tables)

    def columns_split(layer_pack):
        def block_for(by):
            return lax.dynamic_index_in_dim(layer_pack, (tp + by) % RING, 0, keepdims=False)

        parts = [block_for(0)] + [
            send(block_for(-by), along_weights(-by)) for by in (1, 3, 2)
        ]
        rows = jnp.concatenate(in_order(parts), axis=0)
        return order_columns_split(
            dest, in_order([rows] + [send(rows, along_tokens(-by)) for by in (1, 3, 2)])
        )

    def rows_split(layer_pack):
        return order_rows_split(
            dest_rows,
            in_order([layer_pack] + [send(layer_pack, along_tokens(-by)) for by in (1, 3, 2)]),
        )

    own_up_pack = jnp.where(first, up_by_a, up_by_b)
    sent_up_pack = jnp.where(first, up_by_b, up_by_a)
    up_layers = both(own_up_pack, send(sent_up_pack, swap))
    down_layers = both(pack_down, send(pack_down, swap))
    turn = moves(lambda s, a, b: flat(1, b, a) if s == 0 else flat(0, a, b))
    stay = moves(lambda s, a, b: None if s == 0 else flat(s, b, a))
    out_other = send(out_weight[0], turn)
    out_turned = send(out_weight[0], stay)
    out_layers = jnp.where(first, out_weight[0], out_other), jnp.where(first, out_other, out_turned)

    layers = [
        (
            columns_split(qkv_layers[i]),
            columns_split(up_layers[i]),
            rows_split(jnp.concatenate([out_layers[i], down_layers[i]], axis=0)),
        )
        for i in range(2)
    ]

    out0, stored0 = forward_layer(tokens_in.astype(F32), layers[0], geometry)
    low0 = out0.astype(BF)
    out1, stored1 = forward_layer(low0.astype(F32), layers[1], geometry)
    low1 = out1.astype(BF)
    grad1, cuts1 = backward_layer(
        cotangent, layers[1], stored1, geometry, dest_cut, dest_rows
    )
    grad1 = grad1.astype(BF)
    grad0, cuts0 = backward_layer(grad1, layers[0], stored0, geometry, dest_cut, dest_rows)
    grad0 = grad0.astype(BF)

    def swapped_rows(early, late):
        other = send(jnp.where(first, late, early), swap)
        mine = jnp.where(first, early, late)
        stacked = jnp.stack([jnp.where(first, mine, other), jnp.where(first, other, mine)])
        return stacked[None, :, None]

    layer_out = swapped_rows(low0, low1)
    input_grad = swapped_rows(grad0, grad1)

    def reduced(cuts, layer):
        qkv_cut, up_cut, rows_cut = cuts
        up_part = over_weights(over_tokens(up_cut), tp)
        up_part = up_part.reshape(RING, PACK, RING, SPOT)
        up_part = jnp.where(
            first, up_part.transpose(1, 0, 2, 3), up_part.transpose(1, 2, 0, 3)
        ).reshape(PACK, -1)
        rows_part = over_tokens(rows_cut)
        out_part = jnp.where(first, rows_part[:OWN_ROWS], send(rows_part[:OWN_ROWS], stay))
        rows_part = jnp.concatenate([out_part, rows_part[OWN_ROWS:]], axis=0)
        qkv_part = over_weights(over_tokens(qkv_cut), tp)
        qkv_part = qkv_part.reshape(RING, PACK, 3, LANES)[..., :SPOT]
        qkv_part = qkv_part.transpose(1, 2, 0, 3).reshape(PACK, -1)
        result = []
        for part in (qkv_part, up_part, rows_part):
            joined = part.astype(F32) + to_core(part, layer).astype(F32)
            result.append(over_replicas(joined, layer))
        return result

    sums1 = reduced(cuts1, 1)
    sums0 = reduced(cuts0, 0)
    m_qkv, m_up, m_rows = [jnp.where(first, one, two) for one, two in zip(sums0, sums1)]
    s_qkv, s_up, s_g = m_qkv[OWN_ROWS], m_up[OWN_ROWS], m_rows[OWN_ROWS + SPOT]
    m_qkv, m_up = m_qkv[:OWN_ROWS], m_up[:OWN_ROWS]

    def own_piece(row, parts):
        pieces = row.reshape(parts, RING * RING, -1)
        return lax.dynamic_index_in_dim(pieces, place, 1, keepdims=False)

    bias_grad = own_piece(s_g, 1)
    gradients = (
        jnp.sum(own_qkv * m_qkv, axis=1),
        jnp.sum(own_qkv * s_qkv[None, :], axis=1),
        jnp.sum(own_up * m_up, axis=1),
        jnp.sum(own_up * s_up[None, :], axis=1),
        gain1[:, None] * m_qkv + bias1[:, None] * s_qkv[None, :],
        own_piece(s_qkv, 3),
        m_rows[:OWN_ROWS],
        bias_grad[0],
        gain2[:, None] * m_up + bias2[:, None] * s_up[None, :],
        own_piece(s_up, 1)[0],
        m_rows[OWN_ROWS : OWN_ROWS + SPOT],
        bias_grad[0],
    )
    return (layer_out, input_grad) + tuple(grad[None] for grad in gradients)


def solution(mesh):
    tokens = P("section", None, "replica", "fsdp", None)
    vector = P("section", "fsdp")
    matrix = P("section", "fsdp", None)
    three = P("section", None, "fsdp")
    params = (
        vector,
        vector,
        vector,
        vector,
        matrix,
        three,
        matrix,
        vector,
        matrix,
        vector,
        matrix,
        vector,
    )
    return jax.shard_map(
        on_device,
        mesh=mesh,
        in_specs=(tokens, P(None, "replica", None)) + params,
        out_specs=(tokens, tokens) + params,
        check_vma=False,
    )
```

```python
import jax
import jax.numpy as jnp
import numpy as np
from jax import lax
from jax.experimental import pallas as pl
from jax.experimental.pallas import tpu as pltpu
from jax.sharding import PartitionSpec as P

HEADS = 12
HEAD_DIM = 64
EPSILON = 1e-05
NEG_FILL = -1e30
WIDTH = 768
RING = 4
OWN_ROWS = 48
PACK = 64
LANES = 256
SPOT = 192
BF = jnp.bfloat16
F32 = jnp.float32
CORES = ("section", "fsdp")


def flat(core, a, b):
    return core * RING * RING + (a % RING) * RING + b % RING


def moves(step):
    return [
        (flat(core, a, b), step(core, a, b))
        for core in range(2)
        for a in range(RING)
        for b in range(RING)
        if step(core, a, b) is not None
    ]


def along_weights(by):
    return moves(lambda core, a, b: flat(core, a + by, b) if core == 0 else flat(core, a, b + by))


def along_tokens(by):
    return moves(lambda core, a, b: flat(core, a, b + by) if core == 0 else flat(core, a + by, b))


def token_groups():
    return [[flat(0, a, b) for b in range(RING)] for a in range(RING)] + [
        [flat(1, a, b) for a in range(RING)] for b in range(RING)
    ]


def send(value, pairs):
    return lax.ppermute(value, CORES, pairs)


def gather_tokens_axis(block):
    return lax.all_gather(block, CORES, axis=0, tiled=True, axis_index_groups=token_groups())


def scatter_tokens_axis(total):
    return lax.psum_scatter(
        total, CORES, scatter_dimension=0, tiled=True, axis_index_groups=token_groups()
    )


def gathered_weights_axis(block):
    return [block] + [send(block, along_weights(-by)) for by in (1, 3, 2)]


ORDER = (0, 1, 3, 2)


def turned(blocks, by):
    rows = blocks[0].shape[0]
    twice = jnp.concatenate(list(blocks) + list(blocks), axis=0)
    return lax.dynamic_slice_in_dim(twice, ((RING - by) % RING) * rows, RING * rows, 0)


def in_order(blocks):
    found = dict(zip(ORDER, blocks))
    return [found[i] for i in range(RING)]


def after(value, *others):
    return lax.optimization_barrier((value,) + others)[0]


def vmem_call(body, out_shapes, flops, scalars, *arrays):
    specs, operands = [], []
    for item in arrays:
        array, column = item if isinstance(item, tuple) else (item, None)
        block = array.shape if column is None else (array.shape[0], WIDTH)
        place = (0,) * array.ndim if column is None else (0, column)
        specs.append(pl.BlockSpec(block, lambda i, place=place: place))
        operands.append(array)
    return pl.pallas_call(
        body,
        grid=(1,),
        out_shape=out_shapes,
        in_specs=[pl.BlockSpec(memory_space=pltpu.SMEM)] * len(scalars) + specs,
        out_specs=jax.tree.map(
            lambda shape: pl.BlockSpec(shape.shape, lambda i, n=len(shape.shape): (0,) * n),
            out_shapes,
        ),
        compiler_params=pltpu.CompilerParams(vmem_limit_bytes=56 * 1024 * 1024),
        cost_estimate=pl.CostEstimate(flops=flops, bytes_accessed=4_000_000, transcendentals=0),
    )(*scalars, *operands)


def like(shape, dtype):
    return jax.ShapeDtypeStruct(shape, dtype)


def mm(left, right):
    return lax.dot_general(left, right, (((1,), (0,)), ((), ())), preferred_element_type=F32)


def mm_nt(left, right):
    return lax.dot_general(left, right, (((1,), (1,)), ((), ())), preferred_element_type=F32)


def mm_tn(left, right):
    return lax.dot_general(left, right, (((0,), (0,)), ((), ())), preferred_element_type=F32)


def bias_rows(bias, weight, row):
    row = row + jnp.sum(bias * weight, axis=0, keepdims=True)
    high = row.astype(BF)
    low = (row - high.astype(F32)).astype(BF)
    return jnp.concatenate(
        [high, low, jnp.zeros((PACK - OWN_ROWS - 2, row.shape[1]), BF)], axis=0
    )


def pack_qkv_body(gain_ref, bias_ref, row_ref, weight_ref, out_ref):
    weight = weight_ref[...].astype(F32)
    scaled = (weight * gain_ref[...]).astype(BF)
    whole = jnp.concatenate([scaled, bias_rows(bias_ref[...], weight, row_ref[...])], axis=0)
    spare = jnp.zeros((PACK, LANES - SPOT), BF)
    for t in range(RING):
        for i in range(3):
            at = i * WIDTH + t * SPOT
            part = jnp.concatenate([whole[:, at : at + SPOT], spare], axis=1)
            out_ref[t, :, i * LANES : (i + 1) * LANES] = part


def pack_up_body(first_ref, gain_ref, bias_ref, row_ref, weight_ref, own_ref, sent_ref):
    weight = weight_ref[...].astype(F32)
    scaled = (weight * gain_ref[...]).astype(BF)
    whole = jnp.concatenate([scaled, bias_rows(bias_ref[...], weight, row_ref[...])], axis=0)
    first = first_ref[0] == 1
    for t in range(RING):
        by_a = whole[:, t * WIDTH : (t + 1) * WIDTH]
        by_b = jnp.concatenate(
            [whole[:, a * WIDTH + t * SPOT : a * WIDTH + (t + 1) * SPOT] for a in range(RING)],
            axis=1,
        )
        own_ref[t] = jnp.where(first, by_a, by_b)
        sent_ref[t] = jnp.where(first, by_b, by_a)


def out_rows(rows):
    parts = [rows[j * LANES : j * LANES + OWN_ROWS, :] for j in range(RING)]
    return jnp.concatenate(parts + [jnp.zeros((LANES - SPOT, WIDTH), BF)], axis=0)


def down_rows(rows):
    parts = [rows[j * LANES + OWN_ROWS : j * LANES + OWN_ROWS + SPOT, :] for j in range(RING)]
    return jnp.concatenate(parts, axis=0)


def out_bias_row(rows):
    total = jnp.zeros((1, WIDTH), F32)
    for j in range(RING):
        extra = rows[j * LANES + OWN_ROWS + SPOT : (j + 1) * LANES, :].astype(F32)
        total = total + extra[0:1, :] + extra[1:2, :]
    return total


def rotate(value, cos, below, above):
    lanes = value.shape[1]
    return (
        value * cos
        + pltpu.roll(value, lanes - 8, 1) * below
        + pltpu.roll(value, 8, 1) * above
    )


def rotate_back(value, cos, below, above):
    return rotate(value, cos, -below, -above)


def project_body(x0, x1, x2, x3, perm, ones, w, cos, below, above, x_ref, q_ref, kv_ref):
    x = jnp.concatenate([x0[...], x1[...], x2[...], x3[...]], axis=0)
    x_all = (mm(x, perm[...]) + ones[...]).astype(BF)
    x_ref[...] = x_all
    qkv = mm(x_all, w[...])
    tables = cos[...], below[...], above[...]
    q_ref[...] = (rotate(qkv[:, :LANES], *tables) * 0.125).astype(BF)
    kv_ref[:, :LANES] = rotate(qkv[:, LANES : 2 * LANES], *tables).astype(BF)
    kv_ref[:, LANES:] = qkv[:, 2 * LANES :].astype(BF)


def mlp_body(x_ref, w_up, rows, hidden_ref, slope_ref, out_ref):
    up_proj = mm(x_ref[...], w_up[...])
    cdf = 0.5 * (1.0 + lax.erf(up_proj * 0.7071067811865476))
    hidden = (up_proj * cdf).astype(BF)
    hidden_ref[...] = hidden
    density = jnp.exp(-0.5 * up_proj * up_proj) * 0.3989422804014327
    slope_ref[...] = (cdf + up_proj * density).astype(BF)
    out_ref[...] = mm(hidden, down_rows(rows)) + out_bias_row(rows)


def head_mask(value, head):
    lane = lax.broadcasted_iota(jnp.int32, value.shape, 1)
    return jnp.where((lane >= head * HEAD_DIM) & (lane < (head + 1) * HEAD_DIM), value, 0)


def allowed_pairs(starts_ref, info, e, rows):
    part = rows // RING
    pieces = []
    for d in range(RING):
        base = lax.broadcasted_iota(jnp.int32, (part, rows), 0) + starts_ref[e * RING + d]
        pieces.append(jnp.where((base >= info[0:1, :]) & (base <= info[1:2, :]), 0.0, NEG_FILL))
    return jnp.concatenate(pieces, axis=0)


def attend_body(
    starts_ref, info_ref, q_ref, kv0, kv1, kv2, kv3, rows_ref, mlp_ref, mid_ref, lse_ref, own, p1, p2, p3
):
    rows = q_ref.shape[0]
    info = info_ref[...]
    q = q_ref[...]
    masked_q = [head_mask(q, h) for h in range(3)]
    tops, sums, accs = [None] * 3, [None] * 3, [None] * 3
    for e, kv in enumerate((kv0, kv1, kv2, kv3)):
        bias = allowed_pairs(starts_ref, info, e, rows)
        keys = kv[:, :LANES]
        values_t = kv[:, LANES:].T
        for h in range(3):
            scores = mm_nt(keys, masked_q[h]) + bias
            top = jnp.max(scores, axis=0, keepdims=True)
            if e:
                top = jnp.maximum(tops[h], top)
            probs = jnp.exp(scores - top)
            total = jnp.sum(probs, axis=0, keepdims=True)
            part = mm(values_t[h * HEAD_DIM : (h + 1) * HEAD_DIM, :], probs.astype(BF))
            if e:
                shrink = jnp.exp(tops[h] - top)
                total = total + sums[h] * shrink
                part = part + accs[h] * shrink
            tops[h], sums[h], accs[h] = top, total, part
    mids = [accs[h] / sums[h] for h in range(3)] + [jnp.zeros((HEAD_DIM, rows), F32)]
    mid = jnp.concatenate(mids, axis=0).T.astype(BF)
    mid_ref[...] = mid
    for h in range(3):
        lse_ref[h : h + 1, :] = tops[h] + jnp.log(sums[h])
    lse_ref[3:, :] = jnp.zeros((5, rows), F32)
    partial = mm(mid, out_rows(rows_ref)) + mlp_ref[...]
    block = rows // RING
    own[...] = partial[:block]
    for i, part in enumerate((p1, p2, p3)):
        part[...] = partial[(i + 1) * block : (i + 2) * block].astype(BF)


def attend_back_body(
    starts_ref, info_ref, q_ref, a0, a1, a2, a3, rows_ref, mid_ref, lse_ref, cos, below, above,
    kv0, kv1, kv2, kv3, g_ref, dq_ref, g0, g1, g2, g3
):
    rows = q_ref.shape[0]
    info = info_ref[...]
    q = q_ref[...]
    g_all = jnp.concatenate([a0[...], a1[...], a2[...], a3[...]], axis=0)
    g_ref[...] = g_all
    do = mm_nt(g_all, out_rows(rows_ref)).astype(BF)
    lse = lse_ref[...]
    lane = lax.broadcasted_iota(jnp.int32, (8, LANES), 1)
    head = lax.broadcasted_iota(jnp.int32, (8, LANES), 0)
    pick = jnp.where(lane // HEAD_DIM == head, 1.0, 0.0)
    products = do.astype(F32) * mid_ref[...].astype(F32)
    delta = lax.dot_general(
        pick,
        products,
        (((1,), (1,)), ((), ())),
        precision=lax.Precision.HIGHEST,
        preferred_element_type=F32,
    )
    masked_q = [head_mask(q, h) for h in range(3)]
    masked_do = [head_mask(do, h) for h in range(3)]
    dq = [None] * 3
    for e, (kv, grad) in enumerate(zip((kv0, kv1, kv2, kv3), (g0, g1, g2, g3))):
        bias = allowed_pairs(starts_ref, info, e, rows)
        keys = kv[:, :LANES]
        keys_t = keys.T
        values = kv[:, LANES:]
        dk = jnp.zeros((rows, LANES), F32)
        dv = jnp.zeros((rows, LANES), F32)
        for h in range(3):
            scores = mm_nt(keys, masked_q[h]) + bias
            probs = jnp.exp(scores - lse[h : h + 1, :])
            dprobs = mm_nt(values, masked_do[h])
            dscores = (probs * (dprobs - delta[h : h + 1, :])).astype(BF)
            dv = dv + mm(probs.astype(BF), masked_do[h])
            dk = dk + mm(dscores, masked_q[h])
            part = mm(keys_t[h * HEAD_DIM : (h + 1) * HEAD_DIM, :], dscores)
            dq[h] = part if e == 0 else dq[h] + part
        grad[:, :LANES] = dk.astype(BF)
        grad[:, LANES:] = dv.astype(BF)
    dq_all = jnp.concatenate(dq + [jnp.zeros((HEAD_DIM, rows), F32)], axis=0).T * 0.125
    dq_ref[...] = rotate_back(dq_all, cos[...], below[...], above[...]).astype(BF)


def mlp_back_body(g_ref, slope, hidden, mid, x_ref, w_up, rows, dx_ref, early_ref):
    g_all = g_ref[...]
    grad_up = (mm_nt(g_all, down_rows(rows)) * slope[...].astype(F32)).astype(BF)
    dx_ref[...] = mm_nt(grad_up, w_up[...])
    early_ref[:, :WIDTH] = mm_tn(x_ref[...], grad_up).astype(BF)
    down_grad = mm_tn(hidden[...], g_all).astype(BF)
    out_grad = mm_tn(mid[...], g_all).astype(BF)
    sums = jnp.sum(g_all.astype(F32), axis=0, keepdims=True)
    sums = jnp.broadcast_to(sums, (PACK - OWN_ROWS, WIDTH)).astype(BF)
    for j in range(RING):
        at = j * LANES
        early_ref[at : at + OWN_ROWS, WIDTH:] = out_grad[j * OWN_ROWS : (j + 1) * OWN_ROWS]
        early_ref[at + OWN_ROWS : at + OWN_ROWS + SPOT, WIDTH:] = down_grad[
            j * SPOT : (j + 1) * SPOT
        ]
        early_ref[at + OWN_ROWS + SPOT : at + LANES, WIDTH:] = sums


def qkv_back_body(
    dq, g0, g1, g2, g3, cos, below, above, w_qkv, dx_up, perm, grad_ref, d0, d1, d2, d3
):
    dkv = g0[...].astype(F32)
    for part in (g1, g2, g3):
        dkv = dkv + part[...].astype(F32)
    dk = rotate_back(dkv[:, :LANES], cos[...], below[...], above[...])
    grad = jnp.concatenate([dq[...], dk.astype(BF), dkv[:, LANES:].astype(BF)], axis=1)
    grad_ref[...] = grad
    dx = (mm_nt(grad, w_qkv[...]) + dx_up[...]).astype(BF)
    dx = mm_nt(dx, perm[...]).astype(BF)
    block = dx.shape[0] // RING
    for i, part in enumerate((d0, d1, d2, d3)):
        part[...] = dx[i * block : (i + 1) * block]


def unit_rows_of(rows):
    centered = rows - jnp.mean(rows, axis=-1, keepdims=True)
    inv_std = lax.rsqrt(jnp.mean(centered * centered, axis=-1, keepdims=True) + EPSILON)
    return centered * inv_std, inv_std


def forward_layer(tok_rows, xs, weights, geometry, order, then):
    w_qkv, w_up, w_rows = weights
    starts, info, tables = geometry
    own = tok_rows.shape[0]
    rows = RING * own
    x_all, q, kv = vmem_call(
        project_body,
        (
            like((rows, RING * LANES), BF),
            like((rows, LANES), BF),
            like((rows, 2 * LANES), BF),
        ),
        1_600_000_000,
        (),
        *xs,
        *order,
        w_qkv,
        *tables,
    )
    kvs = in_order([kv] + [send(kv, along_tokens(-by)) for by in (1, 3, 2)])
    w_up, w_rows = then(kvs, w_up, w_rows)
    hidden, slope, mlp = vmem_call(
        mlp_body,
        (like((rows, WIDTH), BF), like((rows, WIDTH), BF), like((rows, WIDTH), F32)),
        2_000_000_000,
        (),
        x_all,
        w_up,
        w_rows,
    )
    mid, lse, mine, *parts = vmem_call(
        attend_body,
        (
            like((rows, LANES), BF),
            like((8, rows), F32),
            like((own, WIDTH), F32),
            like((own, WIDTH), BF),
            like((own, WIDTH), BF),
            like((own, WIDTH), BF),
        ),
        6_000_000_000,
        (starts,),
        info,
        q,
        *kvs,
        w_rows,
        mlp,
    )
    total = tok_rows + mine
    for by in (1, 3, 2):
        total = total + send(parts[by - 1], along_weights(by)).astype(F32)
    return total, (x_all, q, kvs, hidden, slope, mid, lse)


def backward_layer(grad_rows, gs, unit, inv_std, weights, stored, geometry, order, meanwhile):
    w_qkv, w_up, w_rows = weights
    starts, info, tables = geometry
    x_all, q, kvs, hidden, slope, mid, lse = stored
    own = grad_rows.shape[0]
    rows = RING * own
    g_all, dq, *dkvs = vmem_call(
        attend_back_body,
        (like((rows, WIDTH), BF), like((rows, LANES), BF))
        + (like((rows, 2 * LANES), BF),) * RING,
        16_000_000_000,
        (starts,),
        info,
        q,
        *gs,
        w_rows,
        mid,
        lse,
        *tables,
        *kvs,
    )
    received = [send(dkvs[by], along_tokens(by)) for by in (1, 3, 2)]
    dx_up, early = vmem_call(
        mlp_back_body,
        (like((rows, RING * LANES), F32), like((RING * LANES, 2 * WIDTH), BF)),
        4_000_000_000,
        (),
        g_all,
        slope,
        hidden,
        mid,
        x_all,
        w_up,
        w_rows,
    )
    early = scatter_tokens_axis(early)
    dkv_own, extra = meanwhile(dkvs[0])
    grad_qkv, *dxs = vmem_call(
        qkv_back_body,
        (like((rows, WIDTH), BF),) + (like((own, WIDTH), BF),) * RING,
        2_000_000_000,
        (),
        dq,
        dkv_own,
        *received,
        *tables,
        w_qkv,
        dx_up,
        order[0],
    )
    total = dxs[0].astype(F32)
    for by in (1, 3, 2):
        total = total + send(dxs[by], along_weights(by)).astype(F32)
    qkv_cut = mm_tn(x_all, grad_qkv).astype(BF)
    grad_in = grad_rows.astype(F32) + inv_std * (
        total
        - jnp.mean(total, axis=-1, keepdims=True)
        - unit * jnp.mean(total * unit, axis=-1, keepdims=True)
    )
    return grad_in, early, qkv_cut, extra


def over_tokens(cut, sq):
    def block_for(by):
        return lax.dynamic_slice_in_dim(cut, ((sq + by) % RING) * LANES, LANES, 0)

    total = block_for(0).astype(F32)
    for by in (1, 3, 2):
        total = total + send(block_for(by), along_tokens(by)).astype(F32)
    return total.astype(BF)


def over_weights(total, tp):
    parts = [total[:PACK]] + [
        send(total[by * PACK : (by + 1) * PACK], along_weights(by)) for by in (1, 3, 2)
    ]
    near = in_order(parts)
    return turned([near[0], near[3], near[2], near[1]], tp)


def to_core(value, core):
    return send(value, moves(lambda s, a, b: flat(core, a, b) if s != core else None))


def over_replicas(low, core):
    rest = lax.axis_size("replica")
    total = low.astype(F32)
    for by in range(1, rest):
        pairs = [(core * rest + i, core * rest + (i + by) % rest) for i in range(rest)]
        total = total + lax.ppermute(low, ("section", "replica"), pairs).astype(F32)
    return total


def on_device(
    pipe_ends,
    seq_lengths,
    norm1_gain,
    norm1_bias,
    norm2_gain,
    norm2_bias,
    qkv_weight,
    qkv_bias,
    out_weight,
    out_bias,
    up_weight,
    up_bias,
    down_weight,
    down_bias,
):
    core = lax.axis_index("section")
    first = core == 0
    place = lax.axis_index("fsdp")
    a_at, b_at = place // RING, place % RING
    tp = jnp.where(first, a_at, b_at)
    sq = jnp.where(first, b_at, a_at)
    rows_dev = pipe_ends.shape[3]

    def block_of(weight_at, token_at):
        weight_at, token_at = weight_at % RING, token_at % RING
        return jnp.where(first, RING * weight_at + token_at, RING * token_at + weight_at)

    ring = jnp.arange(RING, dtype=jnp.int32)
    dest = block_of(tp + ring[None, :], sq + ring[:, None]).reshape(-1).astype(jnp.int32)
    kept = block_of(tp + ring[None, :], ring[:, None]).reshape(-1).astype(jnp.int32)
    spare = jnp.arange(PACK, dtype=jnp.int32)[None, :]
    feature = jnp.where(spare < OWN_ROWS, kept[:, None] * OWN_ROWS + spare, -1).reshape(1, -1)
    perm = (jnp.arange(WIDTH, dtype=jnp.int32)[:, None] == feature).astype(BF)
    ones = np.tile((np.arange(PACK) // 2 == OWN_ROWS // 2).astype(np.float32), RING * RING)
    order = (perm, ones[None, :])

    gain1 = norm1_gain[0].astype(F32)
    bias1 = norm1_bias[0].astype(F32)
    gain2 = norm2_gain[0].astype(F32)
    bias2 = norm2_bias[0].astype(F32)
    own_qkv = qkv_weight[0].astype(F32)
    own_up = up_weight[0].astype(F32)
    spot = (jnp.arange(RING * RING) == place)[:, None]

    def spread(piece):
        return jnp.where(spot, piece[None, :], 0.0).reshape(1, -1)

    qkv_row = jnp.concatenate([spread(qkv_bias[0, i].astype(F32)) for i in range(3)], axis=1)
    up_row = spread(up_bias[0].astype(F32))
    out_row = spread(out_bias[0].astype(F32) + down_bias[0].astype(F32))
    pack = like((RING, PACK, WIDTH), BF)
    pack_qkv = vmem_call(
        pack_qkv_body, pack, 1_000_000, (), gain1[:, None], bias1[:, None], qkv_row, qkv_weight[0]
    )
    own_up_pack, sent_up_pack = vmem_call(
        pack_up_body,
        (pack, pack),
        1_000_000,
        (first.astype(jnp.int32)[None],),
        gain2[:, None],
        bias2[:, None],
        up_row,
        up_weight[0],
    )
    out_high = out_row.astype(BF)
    out_low = (out_row - out_high.astype(F32)).astype(BF)
    pack_down = jnp.concatenate(
        [down_weight[0], out_high, out_low, jnp.zeros((PACK - OWN_ROWS - 2, WIDTH), BF)], axis=0
    )
    swap = moves(lambda s, a, b: flat(1 - s, a, b))

    def both(own, other):
        return jnp.where(first, own, other), jnp.where(first, other, own)

    qkv_layers = both(pack_qkv, send(pack_qkv, swap))
    other_ends = send(
        jnp.where(first, pipe_ends[0, 1, 0], pipe_ends[0, 0, 0]), swap
    )
    own_end = jnp.where(first, pipe_ends[0, 0, 0], pipe_ends[0, 1, 0])
    tokens_in = jnp.where(first, own_end, other_ends)
    cotangent = jnp.where(first, other_ends, own_end)

    lens = lax.dynamic_index_in_dim(seq_lengths[:, 0], core, 0, keepdims=False)
    starts = (dest * rows_dev).astype(jnp.int32)
    rows_at = (starts[:RING, None] + jnp.arange(rows_dev, dtype=jnp.int32)[None, :]).reshape(-1)
    finish = jnp.cumsum(lens)
    begin = jnp.sum(
        jnp.where(rows_at[None, :] >= finish[:, None], lens[:, None], 0), axis=0
    ).astype(jnp.int32)
    info = jnp.concatenate(
        [begin[None, :], rows_at[None, :], jnp.zeros((6, rows_at.shape[0]), jnp.int32)], axis=0
    )
    lane = np.arange(LANES)
    in_head = lane % HEAD_DIM
    rotary = (in_head < 16) & (lane < SPOT)
    inv_freq = (10000.0 ** (-(in_head % 8) / 8.0)).astype(np.float32)
    angles = (rows_at - begin).astype(F32)[:, None] * jnp.where(rotary, inv_freq, 0.0)[None, :]
    cos, sin = jnp.cos(angles), jnp.sin(angles)
    tables = (
        cos,
        jnp.where((in_head < 8)[None, :], -sin, 0.0),
        jnp.where((in_head >= 8)[None, :], sin, 0.0),
    )
    geometry = (starts, info, tables)

    def to_columns(pack):
        def block_for(by):
            return lax.dynamic_index_in_dim(pack, (tp + by) % RING, 0, keepdims=False)

        parts = [block_for(0)] + [
            send(block_for(-by), along_weights(-by)) for by in (1, 3, 2)
        ]
        return jnp.concatenate(in_order(parts), axis=0)

    up_layers = both(own_up_pack, send(sent_up_pack, swap))
    down_layers = both(pack_down, send(pack_down, swap))
    turn = moves(lambda s, a, b: flat(1, b, a) if s == 0 else flat(0, a, b))
    stay = moves(lambda s, a, b: None if s == 0 else flat(s, b, a))
    out_other = send(out_weight[0], turn)
    out_turned = send(out_weight[0], stay)
    out_layers = jnp.where(first, out_weight[0], out_other), jnp.where(first, out_other, out_turned)
    row_packs = [jnp.concatenate([out_layers[i], down_layers[i]], axis=0) for i in range(2)]

    unit0, inv_std0 = unit_rows_of(tokens_in.astype(F32))
    ends = jnp.concatenate([unit0.astype(BF), cotangent], axis=1)
    qkv0 = to_columns(qkv_layers[0])
    ends = in_order(gathered_weights_axis(ends))
    xs0 = [end[:, :WIDTH] for end in ends]
    gs1 = [end[:, WIDTH:] for end in ends]
    qkv0 = turned(
        in_order([qkv0] + [send(qkv0, along_tokens(-by)) for by in (1, 3, 2)]), sq
    )
    rest = jnp.concatenate([up_layers[0], qkv_layers[1], up_layers[1]], axis=2)
    rest = to_columns(after(rest, qkv0))
    mlp0 = gather_tokens_axis(jnp.concatenate([rest[:, :WIDTH], row_packs[0]], axis=1))
    weights0 = (qkv0, (mlp0, 0), (mlp0, 1))
    later = jnp.concatenate([rest[:, WIDTH:], row_packs[1]], axis=1)

    out0, stored0 = forward_layer(
        tokens_in.astype(F32), xs0, weights0, geometry, order, lambda kvs, *rest: rest
    )
    all1 = gather_tokens_axis(after(later, *stored0[2]))
    weights1 = ((all1, 0), (all1, 1), (all1, 2))
    low0 = out0.astype(BF)
    unit1, inv_std1 = unit_rows_of(low0.astype(F32))
    xs1 = in_order(gathered_weights_axis(unit1.astype(BF)))
    out1, stored1 = forward_layer(
        low0.astype(F32), xs1, weights1, geometry, order, lambda kvs, *rest: rest
    )
    low1 = out1.astype(BF)

    def up_swapped(value):
        value = value.reshape(RING, PACK, RING, SPOT)
        return value.transpose(2, 1, 0, 3).reshape(RING * PACK, WIDTH)

    def rows_turned(rows):
        out_part = jnp.where(first, rows[:OWN_ROWS], send(rows[:OWN_ROWS], stay))
        return jnp.concatenate([out_part, rows[OWN_ROWS:]], axis=0)

    def joined(part, layer):
        return (part.astype(F32) + to_core(part, layer).astype(F32)).astype(BF)

    def joined_up(part, layer):
        return joined(jnp.where(first, part, up_swapped(part)), layer)

    grad1, early1, late1, unused = backward_layer(
        cotangent,
        gs1,
        unit1,
        inv_std1,
        weights1,
        stored1,
        geometry,
        order,
        lambda value: (value, None),
    )
    grad1 = grad1.astype(BF)
    scattered1 = scatter_tokens_axis(late1)
    gs0 = in_order(gathered_weights_axis(grad1))

    def finish_second(value):
        columns1 = over_weights(
            jnp.concatenate([scattered1, early1[:, :WIDTH]], axis=1), tp
        )
        value, columns1 = lax.optimization_barrier((value, columns1))
        whole = jnp.concatenate(
            [
                joined(columns1[:, :WIDTH], 1),
                joined_up(columns1[:, WIDTH:], 1),
                joined(rows_turned(early1[:, WIDTH:]), 1),
            ],
            axis=1,
        )
        return value, lax.psum(whole, "replica").astype(F32)

    grad0, early0, late0, sums1 = backward_layer(
        grad1, gs0, unit0, inv_std0, weights0, stored0, geometry, order, finish_second
    )
    grad0 = grad0.astype(BF)
    late0 = over_tokens(late0, sq)
    up0 = over_weights(early0[:, :WIDTH], tp)
    late0, up0 = lax.optimization_barrier((late0, up0))
    early_sums0 = jnp.concatenate(
        [joined_up(up0, 0), joined(rows_turned(early0[:, WIDTH:]), 0)], axis=1
    )
    early_sums0 = over_replicas(early_sums0, 0)
    late_sums0 = over_replicas(joined(over_weights(late0, tp), 0), 0)

    def swapped_rows(early, late):
        other = send(jnp.where(first, late, early), swap)
        mine = jnp.where(first, early, late)
        stacked = jnp.stack([jnp.where(first, mine, other), jnp.where(first, other, mine)])
        return stacked[None, :, None]

    layer_out = swapped_rows(low0, low1)
    input_grad = swapped_rows(grad0, grad1)

    m_qkv = jnp.where(first, late_sums0, sums1[:, :WIDTH])
    m_up = jnp.where(first, early_sums0[:, :WIDTH], sums1[:, WIDTH : 2 * WIDTH])
    m_rows = jnp.where(first, early_sums0[:, WIDTH:], sums1[:, 2 * WIDTH :])
    m_qkv = m_qkv.reshape(RING, PACK, 3, LANES)[..., :SPOT].transpose(1, 2, 0, 3).reshape(PACK, -1)
    m_up = m_up.reshape(RING, PACK, WIDTH).transpose(1, 0, 2).reshape(PACK, -1)
    s_qkv, s_up, s_g = m_qkv[OWN_ROWS], m_up[OWN_ROWS], m_rows[OWN_ROWS + SPOT]
    m_qkv, m_up = m_qkv[:OWN_ROWS], m_up[:OWN_ROWS]

    def own_piece(row, parts):
        pieces = row.reshape(parts, RING * RING, -1)
        return lax.dynamic_index_in_dim(pieces, place, 1, keepdims=False)

    bias_grad = own_piece(s_g, 1)
    gradients = (
        jnp.sum(own_qkv * m_qkv, axis=1),
        jnp.sum(own_qkv * s_qkv[None, :], axis=1),
        jnp.sum(own_up * m_up, axis=1),
        jnp.sum(own_up * s_up[None, :], axis=1),
        gain1[:, None] * m_qkv + bias1[:, None] * s_qkv[None, :],
        own_piece(s_qkv, 3),
        m_rows[:OWN_ROWS],
        bias_grad[0],
        gain2[:, None] * m_up + bias2[:, None] * s_up[None, :],
        own_piece(s_up, 1)[0],
        m_rows[OWN_ROWS : OWN_ROWS + SPOT],
        bias_grad[0],
    )
    return (layer_out, input_grad) + tuple(grad[None] for grad in gradients)


def solution(mesh):
    tokens = P("section", None, "replica", "fsdp", None)
    vector = P("section", "fsdp")
    matrix = P("section", "fsdp", None)
    three = P("section", None, "fsdp")
    params = (
        vector,
        vector,
        vector,
        vector,
        matrix,
        three,
        matrix,
        vector,
        matrix,
        vector,
        matrix,
        vector,
    )
    return jax.shard_map(
        on_device,
        mesh=mesh,
        in_specs=(tokens, P(None, "replica", None)) + params,
        out_specs=(tokens, tokens) + params,
        check_vma=False,
    )
```

```python
import jax
import jax.numpy as jnp
import numpy as np
from jax import lax
from jax.experimental import pallas as pl
from jax.experimental.pallas import tpu as pltpu
from jax.sharding import PartitionSpec as P

HEADS = 12
HEAD_DIM = 64
EPSILON = 1e-05
NEG_FILL = -1e30
WIDTH = 768
RING = 4
OWN_ROWS = 48
PACK = 64
LANES = 256
SPOT = 192
BF = jnp.bfloat16
F32 = jnp.float32
CORES = ("section", "fsdp")


def flat(core, a, b):
    return core * RING * RING + (a % RING) * RING + b % RING


def moves(step):
    return [
        (flat(core, a, b), step(core, a, b))
        for core in range(2)
        for a in range(RING)
        for b in range(RING)
        if step(core, a, b) is not None
    ]


def along_weights(by):
    return moves(lambda core, a, b: flat(core, a + by, b) if core == 0 else flat(core, a, b + by))


def along_tokens(by):
    return moves(lambda core, a, b: flat(core, a, b + by) if core == 0 else flat(core, a + by, b))


def token_groups():
    return [[flat(0, a, b) for b in range(RING)] for a in range(RING)] + [
        [flat(1, a, b) for a in range(RING)] for b in range(RING)
    ]


def send(value, pairs):
    return lax.ppermute(value, CORES, pairs)


def gather_tokens_axis(block):
    return lax.all_gather(block, CORES, axis=0, tiled=True, axis_index_groups=token_groups())


def scatter_tokens_axis(total):
    return lax.psum_scatter(
        total, CORES, scatter_dimension=0, tiled=True, axis_index_groups=token_groups()
    )


def gathered_weights_axis(block):
    return [block] + [send(block, along_weights(-by)) for by in (1, 3, 2)]


ORDER = (0, 1, 3, 2)


def turned(blocks, by):
    rows = blocks[0].shape[0]
    twice = jnp.concatenate(list(blocks) + list(blocks), axis=0)
    return lax.dynamic_slice_in_dim(twice, ((RING - by) % RING) * rows, RING * rows, 0)


def in_order(blocks):
    found = dict(zip(ORDER, blocks))
    return [found[i] for i in range(RING)]


def after(value, *others):
    return lax.optimization_barrier((value,) + others)[0]


def vmem_call(body, out_shapes, flops, scalars, *arrays):
    specs, operands = [], []
    for item in arrays:
        array, column = item if isinstance(item, tuple) else (item, None)
        block = array.shape if column is None else (array.shape[0], WIDTH)
        place = (0,) * array.ndim if column is None else (0, column)
        specs.append(pl.BlockSpec(block, lambda i, place=place: place))
        operands.append(array)
    return pl.pallas_call(
        body,
        grid=(1,),
        out_shape=out_shapes,
        in_specs=[pl.BlockSpec(memory_space=pltpu.SMEM)] * len(scalars) + specs,
        out_specs=jax.tree.map(
            lambda shape: pl.BlockSpec(shape.shape, lambda i, n=len(shape.shape): (0,) * n),
            out_shapes,
        ),
        compiler_params=pltpu.CompilerParams(vmem_limit_bytes=56 * 1024 * 1024),
        cost_estimate=pl.CostEstimate(flops=flops, bytes_accessed=4_000_000, transcendentals=0),
    )(*scalars, *operands)


def like(shape, dtype):
    return jax.ShapeDtypeStruct(shape, dtype)


def mm(left, right):
    return lax.dot_general(left, right, (((1,), (0,)), ((), ())), preferred_element_type=F32)


def mm_nt(left, right):
    return lax.dot_general(left, right, (((1,), (1,)), ((), ())), preferred_element_type=F32)


def mm_tn(left, right):
    return lax.dot_general(left, right, (((0,), (0,)), ((), ())), preferred_element_type=F32)


def bias_rows(bias, weight, row):
    row = row + jnp.sum(bias * weight, axis=0, keepdims=True)
    high = row.astype(BF)
    low = (row - high.astype(F32)).astype(BF)
    return jnp.concatenate(
        [high, low, jnp.zeros((PACK - OWN_ROWS - 2, row.shape[1]), BF)], axis=0
    )


def pack_qkv_body(gain_ref, bias_ref, row_ref, weight_ref, out_ref):
    weight = weight_ref[...].astype(F32)
    scaled = (weight * gain_ref[...]).astype(BF)
    whole = jnp.concatenate([scaled, bias_rows(bias_ref[...], weight, row_ref[...])], axis=0)
    spare = jnp.zeros((PACK, LANES - SPOT), BF)
    for t in range(RING):
        for i in range(3):
            at = i * WIDTH + t * SPOT
            part = jnp.concatenate([whole[:, at : at + SPOT], spare], axis=1)
            out_ref[t, :, i * LANES : (i + 1) * LANES] = part


def pack_up_body(first_ref, gain_ref, bias_ref, row_ref, weight_ref, own_ref, sent_ref):
    weight = weight_ref[...].astype(F32)
    scaled = (weight * gain_ref[...]).astype(BF)
    whole = jnp.concatenate([scaled, bias_rows(bias_ref[...], weight, row_ref[...])], axis=0)
    first = first_ref[0] == 1
    for t in range(RING):
        by_a = whole[:, t * WIDTH : (t + 1) * WIDTH]
        by_b = jnp.concatenate(
            [whole[:, a * WIDTH + t * SPOT : a * WIDTH + (t + 1) * SPOT] for a in range(RING)],
            axis=1,
        )
        own_ref[t] = jnp.where(first, by_a, by_b)
        sent_ref[t] = jnp.where(first, by_b, by_a)


def out_rows(rows):
    parts = [rows[j * LANES : j * LANES + OWN_ROWS, :] for j in range(RING)]
    return jnp.concatenate(parts + [jnp.zeros((LANES - SPOT, WIDTH), BF)], axis=0)


def down_rows(rows):
    parts = [rows[j * LANES + OWN_ROWS : j * LANES + OWN_ROWS + SPOT, :] for j in range(RING)]
    return jnp.concatenate(parts, axis=0)


def out_bias_row(rows):
    total = jnp.zeros((1, WIDTH), F32)
    for j in range(RING):
        extra = rows[j * LANES + OWN_ROWS + SPOT : (j + 1) * LANES, :].astype(F32)
        total = total + extra[0:1, :] + extra[1:2, :]
    return total


def rotate(value, cos, sin):
    cos = jnp.concatenate([cos, cos], axis=1)
    sin = jnp.concatenate([sin, sin], axis=1)
    lanes = value.shape[1]
    lane = lax.broadcasted_iota(jnp.int32, value.shape, 1)
    other = jnp.where(
        (lane & (HEAD_DIM - 1)) < 8,
        -pltpu.roll(value, lanes - 8, 1),
        pltpu.roll(value, 8, 1),
    )
    return value * cos + other * sin


def places(feature):
    row = lax.broadcasted_iota(jnp.int32, (WIDTH, feature.shape[1]), 0)
    return jnp.where(row == feature[0:1, :], 1.0, 0.0).astype(BF)


def project_body(x0, x1, x2, x3, feature, ones, w, cos, sin, x_ref, q_ref, kv_ref):
    x = jnp.concatenate([x0[...], x1[...], x2[...], x3[...]], axis=0)
    x_all = (mm(x, places(feature)) + ones[...]).astype(BF)
    x_ref[...] = x_all
    qkv = mm(x_all, w[...])
    tables = cos[...], sin[...]
    q_ref[...] = (rotate(qkv[:, :LANES], *tables) * 0.125).astype(BF)
    kv_ref[:, :LANES] = rotate(qkv[:, LANES : 2 * LANES], *tables).astype(BF)
    kv_ref[:, LANES:] = qkv[:, 2 * LANES :].astype(BF)


def store_parts(partial, outs):
    block = partial.shape[0] // len(outs)
    for i, out in enumerate(outs):
        out[...] = partial[i * block : (i + 1) * block].astype(out.dtype)


def mlp_body(x_ref, w_up, rows, *refs):
    given = 0 if len(refs) == 3 else 1
    mids, (hidden_ref, slope_ref), outs = refs[:given], refs[given : given + 2], refs[given + 2 :]
    up_proj = mm(x_ref[...], w_up[...])
    cdf = 0.5 * (1.0 + lax.erf(up_proj * 0.7071067811865476))
    hidden = (up_proj * cdf).astype(BF)
    hidden_ref[...] = hidden
    density = jnp.exp(-0.5 * up_proj * up_proj) * 0.3989422804014327
    slope_ref[...] = (cdf + up_proj * density).astype(BF)
    partial = mm(hidden, down_rows(rows)) + out_bias_row(rows)
    for mid in mids:
        partial = partial + mm(mid[...], out_rows(rows))
    store_parts(partial, outs)


def head_mask(value, head):
    lane = lax.broadcasted_iota(jnp.int32, value.shape, 1)
    return jnp.where((lane >= head * HEAD_DIM) & (lane < (head + 1) * HEAD_DIM), value, 0)


def allowed_pairs(starts_ref, info, e, rows):
    part = rows // RING
    pieces = []
    for d in range(RING):
        base = lax.broadcasted_iota(jnp.int32, (part, rows), 0) + starts_ref[e * RING + d]
        pieces.append(jnp.where((base >= info[0:1, :]) & (base <= info[1:2, :]), 0.0, NEG_FILL))
    return jnp.concatenate(pieces, axis=0)


def attend_body(starts_ref, info_ref, q_ref, kv0, kv1, kv2, kv3, *refs):
    given = 0 if len(refs) == 2 else 2
    others, (mid_ref, lse_ref), outs = refs[:given], refs[given : given + 2], refs[given + 2 :]
    rows = q_ref.shape[0]
    info = info_ref[...]
    q = q_ref[...]
    masked_q = [head_mask(q, h) for h in range(3)]
    tops, sums, accs = [None] * 3, [None] * 3, [None] * 3
    for e, kv in enumerate((kv0, kv1, kv2, kv3)):
        bias = allowed_pairs(starts_ref, info, e, rows)
        keys = kv[:, :LANES]
        values_t = kv[:, LANES:].T
        for h in range(3):
            scores = mm_nt(keys, masked_q[h]) + bias
            top = jnp.max(scores, axis=0, keepdims=True)
            if e:
                top = jnp.maximum(tops[h], top)
            probs = jnp.exp(scores - top)
            total = jnp.sum(probs, axis=0, keepdims=True)
            part = mm(values_t[h * HEAD_DIM : (h + 1) * HEAD_DIM, :], probs.astype(BF))
            if e:
                shrink = jnp.exp(tops[h] - top)
                total = total + sums[h] * shrink
                part = part + accs[h] * shrink
            tops[h], sums[h], accs[h] = top, total, part
    mids = [accs[h] / sums[h] for h in range(3)] + [jnp.zeros((HEAD_DIM, rows), F32)]
    mid = jnp.concatenate(mids, axis=0).T.astype(BF)
    mid_ref[...] = mid
    for h in range(3):
        lse_ref[h : h + 1, :] = tops[h] + jnp.log(sums[h])
    lse_ref[3:, :] = jnp.zeros((5, rows), F32)
    if others:
        rows_ref, mlp_ref = others
        store_parts(mm(mid, out_rows(rows_ref)) + mlp_ref[...], outs)


def attend_back_body(
    starts_ref, info_ref, q_ref, a0, a1, a2, a3, rows_ref, mid_ref, lse_ref, cos, sin,
    kv0, kv1, kv2, kv3, dq_ref, g0, g1, g2, g3
):
    rows = q_ref.shape[0]
    info = info_ref[...]
    q = q_ref[...]
    g_all = jnp.concatenate([a0[...], a1[...], a2[...], a3[...]], axis=0)
    do = mm_nt(g_all, out_rows(rows_ref)).astype(BF)
    lse = lse_ref[...]
    lane = lax.broadcasted_iota(jnp.int32, (8, LANES), 1)
    head = lax.broadcasted_iota(jnp.int32, (8, LANES), 0)
    pick = jnp.where(lane // HEAD_DIM == head, 1.0, 0.0)
    products = do.astype(F32) * mid_ref[...].astype(F32)
    delta = lax.dot_general(
        pick,
        products,
        (((1,), (1,)), ((), ())),
        precision=lax.Precision.HIGHEST,
        preferred_element_type=F32,
    )
    masked_q = [head_mask(q, h) for h in range(3)]
    masked_do = [head_mask(do, h) for h in range(3)]
    dq = [None] * 3
    for e, (kv, grad) in enumerate(zip((kv0, kv1, kv2, kv3), (g0, g1, g2, g3))):
        bias = allowed_pairs(starts_ref, info, e, rows)
        keys = kv[:, :LANES]
        keys_t = keys.T
        values = kv[:, LANES:]
        dk = jnp.zeros((rows, LANES), F32)
        dv = jnp.zeros((rows, LANES), F32)
        for h in range(3):
            scores = mm_nt(keys, masked_q[h]) + bias
            probs = jnp.exp(scores - lse[h : h + 1, :])
            dprobs = mm_nt(values, masked_do[h])
            dscores = (probs * (dprobs - delta[h : h + 1, :])).astype(BF)
            dv = dv + mm(probs.astype(BF), masked_do[h])
            dk = dk + mm(dscores, masked_q[h])
            part = mm(keys_t[h * HEAD_DIM : (h + 1) * HEAD_DIM, :], dscores)
            dq[h] = part if e == 0 else dq[h] + part
        grad[:, :LANES] = dk.astype(BF)
        grad[:, LANES:] = dv.astype(BF)
    dq_all = jnp.concatenate(dq + [jnp.zeros((HEAD_DIM, rows), F32)], axis=0).T * 0.125
    dq_ref[...] = rotate(dq_all, cos[...], -sin[...]).astype(BF)


def mlp_back_body(a0, a1, a2, a3, slope, hidden, mid, x_ref, w_up, rows, dx_ref, early_ref):
    g_all = jnp.concatenate([a0[...], a1[...], a2[...], a3[...]], axis=0)
    grad_up = (mm_nt(g_all, down_rows(rows)) * slope[...].astype(F32)).astype(BF)
    dx_ref[...] = mm_nt(grad_up, w_up[...])
    early_ref[:, :WIDTH] = mm_tn(x_ref[...], grad_up).astype(BF)
    down_grad = mm_tn(hidden[...], g_all).astype(BF)
    out_grad = mm_tn(mid[...], g_all).astype(BF)
    sums = jnp.sum(g_all.astype(F32), axis=0, keepdims=True)
    sums = jnp.broadcast_to(sums, (PACK - OWN_ROWS, WIDTH)).astype(BF)
    for j in range(RING):
        at = j * LANES
        early_ref[at : at + OWN_ROWS, WIDTH:] = out_grad[j * OWN_ROWS : (j + 1) * OWN_ROWS]
        early_ref[at + OWN_ROWS : at + OWN_ROWS + SPOT, WIDTH:] = down_grad[
            j * SPOT : (j + 1) * SPOT
        ]
        early_ref[at + OWN_ROWS + SPOT : at + LANES, WIDTH:] = sums


def qkv_back_body(
    dq, g0, g1, g2, g3, cos, sin, w_qkv, dx_up, feature, grad_ref, d0, d1, d2, d3
):
    dkv = g0[...].astype(F32)
    for part in (g1, g2, g3):
        dkv = dkv + part[...].astype(F32)
    dk = rotate(dkv[:, :LANES], cos[...], -sin[...])
    grad = jnp.concatenate([dq[...], dk.astype(BF), dkv[:, LANES:].astype(BF)], axis=1)
    grad_ref[...] = grad
    dx = (mm_nt(grad, w_qkv[...]) + dx_up[...]).astype(BF)
    store_parts(mm_nt(dx, places(feature)), (d0, d1, d2, d3))


def finish_body(first_ref, p0, p1, p2, p3, sums, gain1, bias1, gain2, bias2,
                w_qkv, w_up, gain1_ref, bias1_ref, gain2_ref, bias2_ref, qkv_ref, out_ref, up_ref, down_ref,
                s_qkv_ref, s_up_ref, s_g_ref):
    first = first_ref[0] == 1

    def total(low, high):
        value = p0[:, low:high].astype(F32)
        for part in (p1, p2, p3):
            value = value + part[:, low:high].astype(F32)
        return jnp.where(first, value, sums[:, low:high].astype(F32))

    m = total(0, WIDTH)
    m_qkv = jnp.concatenate(
        [
            m[t * PACK : (t + 1) * PACK, i * LANES : i * LANES + SPOT]
            for i in range(3)
            for t in range(RING)
        ],
        axis=1,
    )
    m = total(WIDTH, 2 * WIDTH)
    m_up = jnp.concatenate([m[t * PACK : (t + 1) * PACK] for t in range(RING)], axis=1)
    rows = sums[:, 2 * WIDTH :].astype(F32)
    out_ref[...] = rows[:OWN_ROWS]
    down_ref[...] = rows[OWN_ROWS : OWN_ROWS + SPOT]
    s_g_ref[...] = rows[OWN_ROWS + SPOT : OWN_ROWS + SPOT + 8]
    for m, w_ref, gain, bias, gain_ref, bias_ref, grad_ref, s_ref in (
        (m_qkv, w_qkv, gain1, bias1, gain1_ref, bias1_ref, qkv_ref, s_qkv_ref),
        (m_up, w_up, gain2, bias2, gain2_ref, bias2_ref, up_ref, s_up_ref),
    ):
        ends = m[OWN_ROWS : OWN_ROWS + 1]
        m = m[:OWN_ROWS]
        weight = w_ref[...].astype(F32)
        gain_ref[...] = jnp.sum(weight * m, axis=1, keepdims=True)
        bias_ref[...] = jnp.sum(weight * ends, axis=1, keepdims=True)
        grad_ref[...] = gain[...] * m + bias[...] * ends
        s_ref[...] = jnp.broadcast_to(ends, s_ref.shape)


def unit_rows_of(rows):
    centered = rows - jnp.mean(rows, axis=-1, keepdims=True)
    inv_std = lax.rsqrt(jnp.mean(centered * centered, axis=-1, keepdims=True) + EPSILON)
    return centered * inv_std, inv_std


def forward_layer(tok_rows, xs, weights, geometry, order, mlp_first):
    w_qkv, w_up, w_rows = weights
    starts, info, tables = geometry
    own = tok_rows.shape[0]
    rows = RING * own
    x_all, q, kv = vmem_call(
        project_body,
        (
            like((rows, RING * LANES), BF),
            like((rows, LANES), BF),
            like((rows, 2 * LANES), BF),
        ),
        1_600_000_000,
        (),
        *xs,
        *order,
        w_qkv,
        *tables,
    )
    kvs = in_order([kv] + [send(kv, along_tokens(-by)) for by in (1, 3, 2)])
    whole = (like((rows, WIDTH), F32),)
    cut = (like((own, WIDTH), F32),) + (like((own, WIDTH), BF),) * (RING - 1)

    def mlp(attended, outs):
        return vmem_call(
            mlp_body,
            (like((rows, WIDTH), BF), like((rows, WIDTH), BF)) + outs,
            2_000_000_000,
            (),
            x_all,
            w_up,
            w_rows,
            *attended,
        )

    def attention(others, outs):
        return vmem_call(
            attend_body,
            (like((rows, LANES), BF), like((8, rows), F32)) + outs,
            6_000_000_000,
            (starts,),
            info,
            q,
            *kvs,
            *others,
        )

    if mlp_first:
        hidden, slope, partial = mlp((), whole)
        mid, lse, *parts = attention((w_rows, partial), cut)
    else:
        mid, lse = attention((), ())
        hidden, slope, *parts = mlp((mid,), cut)
    total = tok_rows + parts[0]
    for by in (1, 3, 2):
        total = total + send(parts[by], along_weights(by)).astype(F32)
    return total, (x_all, q, kvs, hidden, slope, mid, lse)


def backward_layer(
    grad_rows, gs, unit, inv_std, weights, stored, geometry, order, sq, tie, meanwhile=None
):
    w_qkv, w_up, w_rows = weights
    starts, info, tables = geometry
    x_all, q, kvs, hidden, slope, mid, lse = stored
    own = grad_rows.shape[0]
    rows = RING * own

    def mlp_back(gs):
        return vmem_call(
            mlp_back_body,
            (like((rows, RING * LANES), F32), like((RING * LANES, 2 * WIDTH), BF)),
            4_000_000_000,
            (),
            *gs,
            slope,
            hidden,
            mid,
            x_all,
            w_up,
            w_rows,
        )

    def attention_back(gs):
        return vmem_call(
            attend_back_body,
            (like((rows, LANES), BF),) + (like((rows, 2 * LANES), BF),) * RING,
            16_000_000_000,
            (starts,),
            info,
            q,
            *gs,
            w_rows,
            mid,
            lse,
            *tables,
            *kvs,
        )

    if meanwhile is None:
        dq, *dkvs = attention_back(gs)
        received = [send(dkvs[by], along_tokens(by)) for by in (1, 3, 2)]
        dx_up, early = mlp_back([after(gs[0], tie)] + gs[1:])
        early = scatter_tokens_axis(after(early, *received))
        dkv_own, extra = dkvs[0], None
    else:
        dx_up, early = mlp_back(gs)
        early = scatter_tokens_axis(early)
        dq, *dkvs = attention_back([after(gs[0], dx_up)] + gs[1:])
        received = [send(dkvs[by], along_tokens(by)) for by in (1, 3, 2)]
        extra = meanwhile(*received)
        dkv_own = dkvs[0]
    grad_qkv, *dxs = vmem_call(
        qkv_back_body,
        (like((rows, WIDTH), BF),) + (like((own, WIDTH), BF),) * RING,
        2_000_000_000,
        (),
        dq,
        dkv_own,
        *received,
        *tables,
        w_qkv,
        dx_up,
        order[0],
    )
    qkv_cut = mm_tn(x_all, grad_qkv).astype(BF)
    if meanwhile is not None:
        qkv_cut = over_tokens(qkv_cut, sq)
        dxs = [dxs[0]] + [after(part, qkv_cut) for part in dxs[1:]]
    total = dxs[0].astype(F32)
    for by in (1, 3, 2):
        total = total + send(dxs[by], along_weights(by)).astype(F32)
    grad_in = grad_rows.astype(F32) + inv_std * (
        total
        - jnp.mean(total, axis=-1, keepdims=True)
        - unit * jnp.mean(total * unit, axis=-1, keepdims=True)
    )
    return grad_in, early, qkv_cut, extra


def over_tokens(cut, sq):
    def block_for(by):
        return lax.dynamic_slice_in_dim(cut, ((sq + by) % RING) * LANES, LANES, 0)

    total = block_for(0).astype(F32)
    for by in (1, 3, 2):
        total = total + send(block_for(by), along_tokens(by)).astype(F32)
    return total.astype(BF)


def over_weights(total, tp):
    parts = [total[:PACK]] + [
        send(total[by * PACK : (by + 1) * PACK], along_weights(by)) for by in (1, 3, 2)
    ]
    near = in_order(parts)
    return turned([near[0], near[3], near[2], near[1]], tp)


def to_core(value, core):
    return send(value, moves(lambda s, a, b: flat(core, a, b) if s != core else None))


def over_replicas(low, core):
    rest = lax.axis_size("replica")
    parts = [low]
    for by in range(1, rest):
        pairs = [(core * rest + i, core * rest + (i + by) % rest) for i in range(rest)]
        parts.append(lax.ppermute(low, ("section", "replica"), pairs))
    return parts


def on_device(
    pipe_ends,
    seq_lengths,
    norm1_gain,
    norm1_bias,
    norm2_gain,
    norm2_bias,
    qkv_weight,
    qkv_bias,
    out_weight,
    out_bias,
    up_weight,
    up_bias,
    down_weight,
    down_bias,
):
    core = lax.axis_index("section")
    first = core == 0
    place = lax.axis_index("fsdp")
    a_at, b_at = place // RING, place % RING
    tp = jnp.where(first, a_at, b_at)
    sq = jnp.where(first, b_at, a_at)
    rows_dev = pipe_ends.shape[3]

    def block_of(weight_at, token_at):
        weight_at, token_at = weight_at % RING, token_at % RING
        return jnp.where(first, RING * weight_at + token_at, RING * token_at + weight_at)

    ring = jnp.arange(RING, dtype=jnp.int32)
    dest = block_of(tp + ring[None, :], sq + ring[:, None]).reshape(-1).astype(jnp.int32)
    kept = block_of(tp + ring[None, :], ring[:, None]).reshape(-1).astype(jnp.int32)
    spare = jnp.arange(PACK, dtype=jnp.int32)[None, :]
    feature = jnp.where(spare < OWN_ROWS, kept[:, None] * OWN_ROWS + spare, -1).reshape(1, -1)
    ones = np.tile((np.arange(PACK) // 2 == OWN_ROWS // 2).astype(np.float32), RING * RING)
    order = (jnp.broadcast_to(feature, (8, RING * LANES)), ones[None, :])

    gain1 = norm1_gain[0].astype(F32)
    bias1 = norm1_bias[0].astype(F32)
    gain2 = norm2_gain[0].astype(F32)
    bias2 = norm2_bias[0].astype(F32)
    spot = (jnp.arange(RING * RING) == place)[:, None]

    def spread(piece):
        return jnp.where(spot, piece[None, :], 0.0).reshape(1, -1)

    qkv_row = jnp.concatenate([spread(qkv_bias[0, i].astype(F32)) for i in range(3)], axis=1)
    up_row = spread(up_bias[0].astype(F32))
    out_row = spread(out_bias[0].astype(F32) + down_bias[0].astype(F32))
    pack = like((RING, PACK, WIDTH), BF)
    pack_qkv = vmem_call(
        pack_qkv_body, pack, 1_000_000, (), gain1[:, None], bias1[:, None], qkv_row, qkv_weight[0]
    )
    own_up_pack, sent_up_pack = vmem_call(
        pack_up_body,
        (pack, pack),
        1_000_000,
        (first.astype(jnp.int32)[None],),
        gain2[:, None],
        bias2[:, None],
        up_row,
        up_weight[0],
    )
    out_high = out_row.astype(BF)
    out_low = (out_row - out_high.astype(F32)).astype(BF)
    pack_down = jnp.concatenate(
        [down_weight[0], out_high, out_low, jnp.zeros((PACK - OWN_ROWS - 2, WIDTH), BF)], axis=0
    )
    swap = moves(lambda s, a, b: flat(1 - s, a, b))

    def both(own, other):
        return jnp.where(first, own, other), jnp.where(first, other, own)

    qkv_layers = both(pack_qkv, send(pack_qkv, swap))
    other_ends = send(
        jnp.where(first, pipe_ends[0, 1, 0], pipe_ends[0, 0, 0]), swap
    )
    own_end = jnp.where(first, pipe_ends[0, 0, 0], pipe_ends[0, 1, 0])
    tokens_in = jnp.where(first, own_end, other_ends)
    cotangent = jnp.where(first, other_ends, own_end)

    lens = lax.dynamic_index_in_dim(seq_lengths[:, 0], core, 0, keepdims=False)
    starts = (dest * rows_dev).astype(jnp.int32)
    rows_at = (starts[:RING, None] + jnp.arange(rows_dev, dtype=jnp.int32)[None, :]).reshape(-1)
    finish = jnp.cumsum(lens)
    begin = jnp.sum(
        jnp.where(rows_at[None, :] >= finish[:, None], lens[:, None], 0), axis=0
    ).astype(jnp.int32)
    info = jnp.concatenate(
        [begin[None, :], rows_at[None, :], jnp.zeros((6, rows_at.shape[0]), jnp.int32)], axis=0
    )
    in_head = np.arange(2 * HEAD_DIM) % HEAD_DIM
    inv_freq = (10000.0 ** (-(in_head % 8) / 8.0)).astype(np.float32)
    inv_freq = np.where(in_head < 16, inv_freq, np.float32(0))
    angles = (rows_at - begin).astype(F32)[:, None] * inv_freq[None, :]
    tables = (jnp.cos(angles), jnp.sin(angles))
    geometry = (starts, info, tables)

    def to_columns(pack):
        def block_for(by):
            return lax.dynamic_index_in_dim(pack, (tp + by) % RING, 0, keepdims=False)

        parts = [block_for(0)] + [
            send(block_for(-by), along_weights(-by)) for by in (1, 3, 2)
        ]
        return jnp.concatenate(in_order(parts), axis=0)

    up_layers = both(own_up_pack, send(sent_up_pack, swap))
    down_layers = both(pack_down, send(pack_down, swap))
    turn = moves(lambda s, a, b: flat(1, b, a) if s == 0 else flat(0, a, b))
    stay = moves(lambda s, a, b: None if s == 0 else flat(s, b, a))
    out_other = send(out_weight[0], turn)
    out_turned = send(out_weight[0], stay)
    out_layers = jnp.where(first, out_weight[0], out_other), jnp.where(first, out_other, out_turned)
    row_packs = [jnp.concatenate([out_layers[i], down_layers[i]], axis=0) for i in range(2)]

    unit0, inv_std0 = unit_rows_of(tokens_in.astype(F32))
    xs0 = in_order(gathered_weights_axis(unit0.astype(BF)))
    columns0 = to_columns(jnp.concatenate([qkv_layers[0], up_layers[0]], axis=2))
    columns0 = after(columns0, *xs0)
    qkv0 = columns0[:, :WIDTH]
    qkv0 = turned(
        in_order([qkv0] + [send(qkv0, along_tokens(-by)) for by in (1, 3, 2)]), sq
    )
    mlp0 = gather_tokens_axis(
        after(jnp.concatenate([columns0[:, WIDTH:], row_packs[0]], axis=1), qkv0)
    )
    weights0 = (qkv0, (mlp0, 0), (mlp0, 1))

    out0, stored0 = forward_layer(
        tokens_in.astype(F32), xs0, weights0, geometry, order, False
    )
    gs1 = in_order(gathered_weights_axis(after(cotangent, stored0[1])))
    columns1 = jnp.concatenate([qkv_layers[1], up_layers[1]], axis=2)
    columns1 = to_columns(after(columns1, stored0[5]))
    all1 = gather_tokens_axis(jnp.concatenate([columns1, row_packs[1]], axis=1))
    weights1 = ((all1, 0), (all1, 1), (all1, 2))
    low0 = out0.astype(BF)
    unit1, inv_std1 = unit_rows_of(low0.astype(F32))
    xs1 = in_order(gathered_weights_axis(unit1.astype(BF)))
    out1, stored1 = forward_layer(
        low0.astype(F32), xs1, weights1, geometry, order, True
    )
    low1 = out1.astype(BF)

    def up_swapped(value):
        value = value.reshape(RING, PACK, RING, SPOT)
        return value.transpose(2, 1, 0, 3).reshape(RING * PACK, WIDTH)

    def rows_turned(rows):
        out_part = jnp.where(first, rows[:OWN_ROWS], send(rows[:OWN_ROWS], stay))
        return jnp.concatenate([out_part, rows[OWN_ROWS:]], axis=0)

    def joined(part, layer):
        return (part.astype(F32) + to_core(part, layer).astype(F32)).astype(BF)

    def joined_up(part, layer):
        return joined(jnp.where(first, part, up_swapped(part)), layer)

    grad1, early1, late1, unused = backward_layer(
        cotangent,
        gs1,
        unit1,
        inv_std1,
        weights1,
        stored1,
        geometry,
        order,
        sq,
        low1,
    )
    grad1 = grad1.astype(BF)
    scattered1 = scatter_tokens_axis(after(late1, grad1))
    gs0 = in_order(gathered_weights_axis(grad1))

    def swapped_rows(early, late):
        other = send(jnp.where(first, late, early), swap)
        mine = jnp.where(first, early, late)
        stacked = jnp.stack([jnp.where(first, mine, other), jnp.where(first, other, mine)])
        return stacked[None, :, None]

    layer_out = swapped_rows(low0, low1)
    gs0[0] = after(gs0[0], early1, layer_out)

    def finish_second(*received):
        columns = jnp.concatenate([scattered1, early1[:, :WIDTH]], axis=1)
        columns = over_weights(after(columns, *received), tp)
        return [
            joined(columns[:, :WIDTH], 1),
            joined_up(columns[:, WIDTH:], 1),
            joined(rows_turned(early1[:, WIDTH:]), 1),
        ]

    grad0, early0, late0, whole1 = backward_layer(
        grad1, gs0, unit0, inv_std0, weights0, stored0, geometry, order, sq, None, finish_second
    )
    grad0 = grad0.astype(BF)
    rows0 = joined(rows_turned(early0[:, WIDTH:]), 0)
    sent = jnp.concatenate(whole1[:2] + [jnp.where(first, rows0, whole1[2])], axis=1)
    sums = lax.psum(sent, "replica")
    columns0 = jnp.concatenate([late0, early0[:, :WIDTH]], axis=1)
    columns0 = over_weights(after(columns0, rows0, *whole1), tp)
    columns0 = over_replicas(
        jnp.concatenate(
            [joined(columns0[:, :WIDTH], 0), joined_up(columns0[:, WIDTH:], 0)], axis=1
        ),
        0,
    )

    input_grad = swapped_rows(grad0, grad1)

    column = like((OWN_ROWS, 1), F32)
    gain1_grad, bias1_grad, gain2_grad, bias2_grad, qkv_grad, out_grad, up_grad, down_grad, *totals = vmem_call(
        finish_body,
        (
            column,
            column,
            column,
            column,
            like((OWN_ROWS, 3 * WIDTH), F32),
            like((OWN_ROWS, WIDTH), F32),
            like((OWN_ROWS, RING * WIDTH), F32),
            like((SPOT, WIDTH), F32),
            like((8, 3 * WIDTH), F32),
            like((8, RING * WIDTH), F32),
            like((8, WIDTH), F32),
        ),
        10_000_000,
        (first.astype(jnp.int32)[None],),
        *columns0,
        sums,
        gain1[:, None],
        bias1[:, None],
        gain2[:, None],
        bias2[:, None],
        qkv_weight[0],
        up_weight[0],
    )

    def own_piece(rows, parts):
        pieces = rows[0].reshape(parts, RING * RING, -1)
        return lax.dynamic_index_in_dim(pieces, place, 1, keepdims=False)

    s_qkv, s_up, s_g = totals
    bias_grad = own_piece(s_g, 1)[0]
    gradients = (
        gain1_grad[:, 0],
        bias1_grad[:, 0],
        gain2_grad[:, 0],
        bias2_grad[:, 0],
        qkv_grad,
        own_piece(s_qkv, 3),
        out_grad,
        bias_grad,
        up_grad,
        own_piece(s_up, 1)[0],
        down_grad,
        bias_grad,
    )
    return (layer_out, input_grad) + tuple(grad[None] for grad in gradients)


def solution(mesh):
    tokens = P("section", None, "replica", "fsdp", None)
    vector = P("section", "fsdp")
    matrix = P("section", "fsdp", None)
    three = P("section", None, "fsdp")
    params = (
        vector,
        vector,
        vector,
        vector,
        matrix,
        three,
        matrix,
        vector,
        matrix,
        vector,
        matrix,
        vector,
    )
    return jax.shard_map(
        on_device,
        mesh=mesh,
        in_specs=(tokens, P(None, "replica", None)) + params,
        out_specs=(tokens, tokens) + params,
        check_vma=False,
    )
```

```python
import jax
import jax.numpy as jnp
import numpy as np
from jax import lax
from jax.experimental import pallas as pl
from jax.experimental.pallas import tpu as pltpu
from jax.sharding import PartitionSpec as P

HEADS = 12
HEAD_DIM = 64
EPSILON = 1e-05
NEG_FILL = -1e30
WIDTH = 768
RING = 4
OWN_ROWS = 48
PACK = 64
LANES = 256
SPOT = 192
BF = jnp.bfloat16
F32 = jnp.float32
CORES = ("section", "fsdp")


def flat(core, a, b):
    return core * RING * RING + (a % RING) * RING + b % RING


def moves(step):
    return [
        (flat(core, a, b), step(core, a, b))
        for core in range(2)
        for a in range(RING)
        for b in range(RING)
        if step(core, a, b) is not None
    ]


def along_weights(by):
    return moves(lambda core, a, b: flat(core, a + by, b) if core == 0 else flat(core, a, b + by))


def along_tokens(by):
    return moves(lambda core, a, b: flat(core, a, b + by) if core == 0 else flat(core, a + by, b))


def token_groups():
    return [[flat(0, a, b) for b in range(RING)] for a in range(RING)] + [
        [flat(1, a, b) for a in range(RING)] for b in range(RING)
    ]


def send(value, pairs):
    return lax.ppermute(value, CORES, pairs)


def gather_tokens_axis(block):
    return lax.all_gather(block, CORES, axis=0, tiled=True, axis_index_groups=token_groups())


def scatter_tokens_axis(total):
    return lax.psum_scatter(
        total, CORES, scatter_dimension=0, tiled=True, axis_index_groups=token_groups()
    )


def gathered_weights_axis(block):
    return [block] + [send(block, along_weights(-by)) for by in (1, 3, 2)]


ORDER = (0, 1, 3, 2)


def turned(blocks, by):
    rows = blocks[0].shape[0]
    twice = jnp.concatenate(list(blocks) + list(blocks), axis=0)
    return lax.dynamic_slice_in_dim(twice, ((RING - by) % RING) * rows, RING * rows, 0)


def in_order(blocks):
    found = dict(zip(ORDER, blocks))
    return [found[i] for i in range(RING)]


def after(value, *others):
    return lax.optimization_barrier((value,) + others)[0]


def vmem_call(body, out_shapes, flops, scalars, *arrays, steps=1):
    specs, operands = [], []
    for item in arrays:
        array, column = item if isinstance(item, tuple) else (item, None)
        block = array.shape if column is None else (array.shape[0], WIDTH)
        place = (0,) * array.ndim if column is None else (0, column)
        specs.append(pl.BlockSpec(block, lambda i, place=place: place))
        operands.append(array)
    return pl.pallas_call(
        body,
        grid=(steps,),
        out_shape=out_shapes,
        in_specs=[pl.BlockSpec(memory_space=pltpu.SMEM)] * len(scalars) + specs,
        out_specs=pl.BlockSpec(
            (out_shapes.shape[0], out_shapes.shape[1] // steps), lambda i: (0, steps - 1 - i)
        )
        if steps > 1
        else jax.tree.map(
            lambda shape: pl.BlockSpec(shape.shape, lambda i, n=len(shape.shape): (0,) * n),
            out_shapes,
        ),
        compiler_params=pltpu.CompilerParams(vmem_limit_bytes=56 * 1024 * 1024),
        cost_estimate=pl.CostEstimate(flops=flops, bytes_accessed=4_000_000, transcendentals=0),
    )(*scalars, *operands)


def like(shape, dtype):
    return jax.ShapeDtypeStruct(shape, dtype)


def mm(left, right):
    return lax.dot_general(left, right, (((1,), (0,)), ((), ())), preferred_element_type=F32)


def mm_nt(left, right):
    return lax.dot_general(left, right, (((1,), (1,)), ((), ())), preferred_element_type=F32)


def mm_exact(left, right):
    return lax.dot_general(
        left,
        right,
        (((1,), (1,)), ((), ())),
        precision=lax.Precision.HIGHEST,
        preferred_element_type=F32,
    )


def mm_tn(left, right):
    return lax.dot_general(left, right, (((0,), (0,)), ((), ())), preferred_element_type=F32)


def bias_rows(bias, weight, row):
    row = row + jnp.sum(bias * weight, axis=0, keepdims=True)
    high = row.astype(BF)
    low = (row - high.astype(F32)).astype(BF)
    return jnp.concatenate(
        [high, low, jnp.zeros((PACK - OWN_ROWS - 2, row.shape[1]), BF)], axis=0
    )


def pack_qkv_body(gain_ref, bias_ref, row_ref, weight_ref, out_ref):
    weight = weight_ref[...].astype(F32)
    scaled = (weight * gain_ref[...]).astype(BF)
    whole = jnp.concatenate([scaled, bias_rows(bias_ref[...], weight, row_ref[...])], axis=0)
    spare = jnp.zeros((PACK, LANES - SPOT), BF)
    for t in range(RING):
        for i in range(3):
            at = i * WIDTH + t * SPOT
            part = jnp.concatenate([whole[:, at : at + SPOT], spare], axis=1)
            out_ref[t, :, i * LANES : (i + 1) * LANES] = part


def pack_up_body(first_ref, gain_ref, bias_ref, row_ref, weight_ref, own_ref, sent_ref):
    weight = weight_ref[...].astype(F32)
    scaled = (weight * gain_ref[...]).astype(BF)
    whole = jnp.concatenate([scaled, bias_rows(bias_ref[...], weight, row_ref[...])], axis=0)
    first = first_ref[0] == 1
    for t in range(RING):
        by_a = whole[:, t * WIDTH : (t + 1) * WIDTH]
        by_b = jnp.concatenate(
            [whole[:, a * WIDTH + t * SPOT : a * WIDTH + (t + 1) * SPOT] for a in range(RING)],
            axis=1,
        )
        own_ref[t] = jnp.where(first, by_a, by_b)
        sent_ref[t] = jnp.where(first, by_b, by_a)


def out_rows(rows):
    parts = [rows[j * LANES : j * LANES + OWN_ROWS, :] for j in range(RING)]
    return jnp.concatenate(parts + [jnp.zeros((LANES - SPOT, WIDTH), BF)], axis=0)


def down_rows(rows):
    parts = [rows[j * LANES + OWN_ROWS : j * LANES + OWN_ROWS + SPOT, :] for j in range(RING)]
    return jnp.concatenate(parts, axis=0)


def out_bias_row(rows):
    total = jnp.zeros((1, WIDTH), F32)
    for j in range(RING):
        extra = rows[j * LANES + OWN_ROWS + SPOT : (j + 1) * LANES, :].astype(F32)
        total = total + extra[0:1, :] + extra[1:2, :]
    return total


def rotate(value, cos, sin):
    cos = jnp.concatenate([cos, cos], axis=1)
    sin = jnp.concatenate([sin, sin], axis=1)
    lanes = value.shape[1]
    lane = lax.broadcasted_iota(jnp.int32, value.shape, 1)
    other = jnp.where(
        (lane & (HEAD_DIM - 1)) < 8,
        -pltpu.roll(value, lanes - 8, 1),
        pltpu.roll(value, 8, 1),
    )
    return value * cos + other * sin


def places(feature):
    row = lax.broadcasted_iota(jnp.int32, (WIDTH, feature.shape[1]), 0)
    return jnp.where(row == feature[0:1, :], 1.0, 0.0).astype(BF)


def project_body(x0, x1, x2, x3, feature, ones, w, cos, sin, x_ref, q_ref, kv_ref):
    x = jnp.concatenate([x0[...], x1[...], x2[...], x3[...]], axis=0)
    x_all = (mm(x, places(feature)) + ones[...]).astype(BF)
    x_ref[...] = x_all
    qkv = mm(x_all, w[...])
    tables = cos[...], sin[...]
    q_ref[...] = (rotate(qkv[:, :LANES], *tables) * 0.125).astype(BF)
    kv_ref[:, :LANES] = rotate(qkv[:, LANES : 2 * LANES], *tables).astype(BF)
    kv_ref[:, LANES:] = qkv[:, 2 * LANES :].astype(BF)


def store_parts(partial, outs):
    block = partial.shape[0] // len(outs)
    for i, out in enumerate(outs):
        out[...] = partial[i * block : (i + 1) * block].astype(out.dtype)


def mlp_body(x_ref, w_up, rows, *refs):
    given = 0 if len(refs) == 3 else 1
    mids, (hidden_ref, slope_ref), outs = refs[:given], refs[given : given + 2], refs[given + 2 :]
    up_proj = mm(x_ref[...], w_up[...])
    cdf = 0.5 * (1.0 + lax.erf(up_proj * 0.7071067811865476))
    hidden = (up_proj * cdf).astype(BF)
    hidden_ref[...] = hidden
    density = jnp.exp(-0.5 * up_proj * up_proj) * 0.3989422804014327
    slope_ref[...] = (cdf + up_proj * density).astype(BF)
    partial = mm(hidden, down_rows(rows)) + out_bias_row(rows)
    for mid in mids:
        partial = partial + mm(mid[...], out_rows(rows))
    store_parts(partial, outs)


def head_mask(value, head):
    lane = lax.broadcasted_iota(jnp.int32, value.shape, 1)
    return jnp.where((lane >= head * HEAD_DIM) & (lane < (head + 1) * HEAD_DIM), value, 0)


def allowed_pairs(starts_ref, info, e, rows):
    part = rows // RING
    pieces = []
    for d in range(RING):
        base = lax.broadcasted_iota(jnp.int32, (part, rows), 0) + starts_ref[e * RING + d]
        pieces.append(jnp.where((base >= info[0:1, :]) & (base <= info[1:2, :]), 0.0, NEG_FILL))
    return jnp.concatenate(pieces, axis=0)


def attend_body(starts_ref, info_ref, q_ref, kv0, kv1, kv2, kv3, *refs):
    given = 0 if len(refs) == 2 else 2
    others, (mid_ref, lse_ref), outs = refs[:given], refs[given : given + 2], refs[given + 2 :]
    rows = q_ref.shape[0]
    info = info_ref[...]
    q = q_ref[...]
    masked_q = [head_mask(q, h) for h in range(3)]
    tops, sums, accs = [None] * 3, [None] * 3, [None] * 3
    for e, kv in enumerate((kv0, kv1, kv2, kv3)):
        bias = allowed_pairs(starts_ref, info, e, rows)
        keys = kv[:, :LANES]
        values_t = kv[:, LANES:].T
        for h in range(3):
            scores = mm_nt(keys, masked_q[h]) + bias
            top = jnp.max(scores, axis=0, keepdims=True)
            if e:
                top = jnp.maximum(tops[h], top)
            probs = jnp.exp(scores - top)
            total = jnp.sum(probs, axis=0, keepdims=True)
            part = mm(values_t[h * HEAD_DIM : (h + 1) * HEAD_DIM, :], probs.astype(BF))
            if e:
                shrink = jnp.exp(tops[h] - top)
                total = total + sums[h] * shrink
                part = part + accs[h] * shrink
            tops[h], sums[h], accs[h] = top, total, part
    mids = [accs[h] / sums[h] for h in range(3)] + [jnp.zeros((HEAD_DIM, rows), F32)]
    mid = jnp.concatenate(mids, axis=0).T.astype(BF)
    mid_ref[...] = mid
    for h in range(3):
        lse_ref[h : h + 1, :] = tops[h] + jnp.log(sums[h])
    lse_ref[3:, :] = jnp.zeros((5, rows), F32)
    if others:
        rows_ref, mlp_ref = others
        store_parts(mm(mid, out_rows(rows_ref)) + mlp_ref[...], outs)


def attend_back_body(
    starts_ref, info_ref, q_ref, a0, a1, a2, a3, rows_ref, mid_ref, lse_ref, cos, sin,
    kv0, kv1, kv2, kv3, dq_ref, g0, g1, g2, g3
):
    rows = q_ref.shape[0]
    info = info_ref[...]
    q = q_ref[...]
    g_all = jnp.concatenate([a0[...], a1[...], a2[...], a3[...]], axis=0)
    do = mm_nt(g_all, out_rows(rows_ref)).astype(BF)
    lse = lse_ref[...]
    lane = lax.broadcasted_iota(jnp.int32, (8, LANES), 1)
    head = lax.broadcasted_iota(jnp.int32, (8, LANES), 0)
    pick = jnp.where(lane // HEAD_DIM == head, 1.0, 0.0)
    products = do.astype(F32) * mid_ref[...].astype(F32)
    delta = lax.dot_general(
        pick,
        products,
        (((1,), (1,)), ((), ())),
        precision=lax.Precision.HIGHEST,
        preferred_element_type=F32,
    )
    masked_q = [head_mask(q, h) for h in range(3)]
    masked_do = [head_mask(do, h) for h in range(3)]
    dq = [None] * 3
    for e, (kv, grad) in enumerate(zip((kv0, kv1, kv2, kv3), (g0, g1, g2, g3))):
        bias = allowed_pairs(starts_ref, info, e, rows)
        keys = kv[:, :LANES]
        keys_t = keys.T
        values = kv[:, LANES:]
        dk = jnp.zeros((rows, LANES), F32)
        dv = jnp.zeros((rows, LANES), F32)
        for h in range(3):
            scores = mm_nt(keys, masked_q[h]) + bias
            probs = jnp.exp(scores - lse[h : h + 1, :])
            dprobs = mm_nt(values, masked_do[h])
            dscores = (probs * (dprobs - delta[h : h + 1, :])).astype(BF)
            dv = dv + mm(probs.astype(BF), masked_do[h])
            dk = dk + mm(dscores, masked_q[h])
            part = mm(keys_t[h * HEAD_DIM : (h + 1) * HEAD_DIM, :], dscores)
            dq[h] = part if e == 0 else dq[h] + part
        grad[:, :LANES] = dk.astype(BF)
        grad[:, LANES:] = dv.astype(BF)
    dq_all = jnp.concatenate(dq + [jnp.zeros((HEAD_DIM, rows), F32)], axis=0).T * 0.125
    dq_ref[...] = rotate(dq_all, cos[...], -sin[...]).astype(BF)


def mlp_back_body(a0, a1, a2, a3, slope, w_up, rows, grad_ref, dx_ref):
    g_all = jnp.concatenate([a0[...], a1[...], a2[...], a3[...]], axis=0)
    grad_up = (mm_nt(g_all, down_rows(rows)) * slope[...].astype(F32)).astype(BF)
    grad_ref[...] = grad_up
    dx_ref[...] = mm_nt(grad_up, w_up[...])


def weight_grads_body(a0, a1, a2, a3, hidden, mid, x_ref, grad_qkv, grad_up, out_ref):
    step = pl.program_id(0)

    @pl.when(step == 0)
    def rows_part():
        g_all = jnp.concatenate([a0[...], a1[...], a2[...], a3[...]], axis=0)
        down_grad = mm_tn(hidden[...], g_all).astype(BF)
        out_grad = mm_tn(mid[...], g_all).astype(BF)
        sums = jnp.sum(g_all.astype(F32), axis=0, keepdims=True)
        sums = jnp.broadcast_to(sums, (PACK - OWN_ROWS, WIDTH)).astype(BF)
        for j in range(RING):
            at = j * LANES
            out_ref[at : at + OWN_ROWS, :] = out_grad[j * OWN_ROWS : (j + 1) * OWN_ROWS]
            out_ref[at + OWN_ROWS : at + OWN_ROWS + SPOT, :] = down_grad[j * SPOT : (j + 1) * SPOT]
            out_ref[at + OWN_ROWS + SPOT : at + LANES, :] = sums

    @pl.when(step == 1)
    def up_part():
        out_ref[...] = mm_tn(x_ref[...], grad_up[...]).astype(BF)

    @pl.when(step == 2)
    def qkv_part():
        out_ref[...] = mm_tn(x_ref[...], grad_qkv[...]).astype(BF)


def qkv_back_body(
    dq, g0, g1, g2, g3, cos, sin, w_qkv, dx_up, feature, grad_ref, d0, d1, d2, d3
):
    dkv = g0[...].astype(F32)
    for part in (g1, g2, g3):
        dkv = dkv + part[...].astype(F32)
    dk = rotate(dkv[:, :LANES], cos[...], -sin[...])
    grad = jnp.concatenate([dq[...], dk.astype(BF), dkv[:, LANES:].astype(BF)], axis=1)
    grad_ref[...] = grad
    dx = (mm_nt(grad, w_qkv[...]) + dx_up[...]).astype(BF)
    store_parts(mm_nt(dx, places(feature)), (d0, d1, d2, d3))


def finish_body(first_ref, p0, p1, p2, p3, sums, gain1, bias1, gain2, bias2,
                w_qkv, w_up, gain1_ref, bias1_ref, gain2_ref, bias2_ref, qkv_ref, out_ref, up_ref, down_ref,
                s_qkv_ref, s_up_ref, s_g_ref):
    first = first_ref[0] == 1

    def total(low, high):
        value = p0[:, low:high].astype(F32)
        for part in (p1, p2, p3):
            value = value + part[:, low:high].astype(F32)
        return jnp.where(first, value, sums[:, low:high].astype(F32))

    m = total(0, WIDTH)
    m_qkv = jnp.concatenate(
        [
            m[t * PACK : (t + 1) * PACK, i * LANES : i * LANES + SPOT]
            for i in range(3)
            for t in range(RING)
        ],
        axis=1,
    )
    m = total(WIDTH, 2 * WIDTH)
    m_up = jnp.concatenate([m[t * PACK : (t + 1) * PACK] for t in range(RING)], axis=1)
    rows = total(2 * WIDTH, 3 * WIDTH)
    out_ref[...] = rows[:OWN_ROWS]
    down_ref[...] = rows[OWN_ROWS : OWN_ROWS + SPOT]
    s_g_ref[...] = rows[OWN_ROWS + SPOT : OWN_ROWS + SPOT + 8]
    for m, w_ref, gain, bias, gain_ref, bias_ref, grad_ref, s_ref in (
        (m_qkv, w_qkv, gain1, bias1, gain1_ref, bias1_ref, qkv_ref, s_qkv_ref),
        (m_up, w_up, gain2, bias2, gain2_ref, bias2_ref, up_ref, s_up_ref),
    ):
        ends = m[OWN_ROWS : OWN_ROWS + 1]
        m = m[:OWN_ROWS]
        weight = w_ref[...].astype(F32)
        all_ones = jnp.ones((8, m.shape[1]), F32)
        gain_ref[...] = mm_exact(all_ones, weight * m)
        bias_ref[...] = mm_exact(all_ones, weight * ends)
        grad_ref[...] = gain[...] * m + bias[...] * ends
        s_ref[...] = jnp.broadcast_to(ends, s_ref.shape)


def unit_rows_of(rows):
    centered = rows - jnp.mean(rows, axis=-1, keepdims=True)
    inv_std = lax.rsqrt(jnp.mean(centered * centered, axis=-1, keepdims=True) + EPSILON)
    return centered * inv_std, inv_std


def forward_layer(tok_rows, xs, weights, geometry, order, mlp_first):
    w_qkv, w_up, w_rows = weights
    starts, info, tables = geometry
    own = tok_rows.shape[0]
    rows = RING * own
    x_all, q, kv = vmem_call(
        project_body,
        (
            like((rows, RING * LANES), BF),
            like((rows, LANES), BF),
            like((rows, 2 * LANES), BF),
        ),
        1_600_000_000,
        (),
        *xs,
        *order,
        w_qkv,
        *tables,
    )
    kvs = in_order([kv] + [send(kv, along_tokens(-by)) for by in (1, 3, 2)])
    whole = (like((rows, WIDTH), F32),)
    cut = (like((own, WIDTH), F32),) + (like((own, WIDTH), BF),) * (RING - 1)

    def mlp(attended, outs):
        return vmem_call(
            mlp_body,
            (like((rows, WIDTH), BF), like((rows, WIDTH), BF)) + outs,
            2_000_000_000,
            (),
            x_all,
            w_up,
            w_rows,
            *attended,
        )

    def attention(others, outs):
        return vmem_call(
            attend_body,
            (like((rows, LANES), BF), like((8, rows), F32)) + outs,
            6_000_000_000,
            (starts,),
            info,
            q,
            *kvs,
            *others,
        )

    if mlp_first:
        hidden, slope, partial = mlp((), whole)
        mid, lse, *parts = attention((w_rows, partial), cut)
    else:
        mid, lse = attention((), ())
        hidden, slope, *parts = mlp((mid,), cut)
    total = tok_rows + parts[0]
    for by in (1, 3, 2):
        total = total + send(parts[by], along_weights(by)).astype(F32)
    return total, (x_all, q, kvs, hidden, slope, mid, lse)


def backward_layer(
    grad_rows, gs, unit, inv_std, weights, stored, geometry, order, tie, window=(), ahead=()
):
    w_qkv, w_up, w_rows = weights
    starts, info, tables = geometry
    x_all, q, kvs, hidden, slope, mid, lse = stored
    own = grad_rows.shape[0]
    rows = RING * own

    def attention_back(gs):
        return vmem_call(
            attend_back_body,
            (like((rows, LANES), BF),) + (like((rows, 2 * LANES), BF),) * RING,
            16_000_000_000,
            (starts,),
            info,
            q,
            *gs,
            w_rows,
            mid,
            lse,
            *tables,
            *kvs,
        )

    dq, *dkvs = attention_back(gs)
    received = [send(dkvs[by], along_tokens(by)) for by in (1, 3, 2)]
    grad_up, dx_up = vmem_call(
        mlp_back_body,
        (like((rows, WIDTH), BF), like((rows, RING * LANES), F32)),
        1_600_000_000,
        (),
        *([after(gs[0], *tie)] + gs[1:]),
        slope,
        w_up,
        w_rows,
    )
    grad_qkv, *dxs = vmem_call(
        qkv_back_body,
        (like((rows, WIDTH), BF),) + (like((own, WIDTH), BF),) * RING,
        2_000_000_000,
        (),
        dq,
        after(dkvs[0], *window),
        *received,
        *tables,
        w_qkv,
        dx_up,
        order[0],
    )
    total = dxs[0].astype(F32)
    for by in (1, 3, 2):
        total = total + send(dxs[by], along_weights(by)).astype(F32)
    grad_in = grad_rows.astype(F32) + inv_std * (
        total
        - jnp.mean(total, axis=-1, keepdims=True)
        - unit * jnp.mean(total * unit, axis=-1, keepdims=True)
    )
    grad_in = grad_in.astype(BF)
    cuts = vmem_call(
        weight_grads_body,
        like((RING * LANES, 3 * WIDTH), BF),
        3_000_000_000,
        (),
        *gs,
        hidden,
        mid,
        x_all,
        after(grad_qkv, *(ahead or (grad_in,))),
        grad_up,
        steps=3,
    )
    return grad_in, scatter_tokens_axis(cuts)


def over_weights(total, tp):
    parts = [total[:PACK]] + [
        send(total[by * PACK : (by + 1) * PACK], along_weights(by)) for by in (1, 3, 2)
    ]
    near = in_order(parts)
    return turned([near[0], near[3], near[2], near[1]], tp)


def to_core(value, core):
    return send(value, moves(lambda s, a, b: flat(core, a, b) if s != core else None))


def over_replicas(low, core):
    rest = lax.axis_size("replica")
    parts = [low]
    for by in range(1, rest):
        pairs = [(core * rest + i, core * rest + (i + by) % rest) for i in range(rest)]
        parts.append(lax.ppermute(low, ("section", "replica"), pairs))
    return parts


def on_device(
    pipe_ends,
    seq_lengths,
    norm1_gain,
    norm1_bias,
    norm2_gain,
    norm2_bias,
    qkv_weight,
    qkv_bias,
    out_weight,
    out_bias,
    up_weight,
    up_bias,
    down_weight,
    down_bias,
):
    core = lax.axis_index("section")
    first = core == 0
    place = lax.axis_index("fsdp")
    a_at, b_at = place // RING, place % RING
    tp = jnp.where(first, a_at, b_at)
    sq = jnp.where(first, b_at, a_at)
    rows_dev = pipe_ends.shape[3]

    def block_of(weight_at, token_at):
        weight_at, token_at = weight_at % RING, token_at % RING
        return jnp.where(first, RING * weight_at + token_at, RING * token_at + weight_at)

    ring = jnp.arange(RING, dtype=jnp.int32)
    dest = block_of(tp + ring[None, :], sq + ring[:, None]).reshape(-1).astype(jnp.int32)
    kept = block_of(tp + ring[None, :], ring[:, None]).reshape(-1).astype(jnp.int32)
    spare = jnp.arange(PACK, dtype=jnp.int32)[None, :]
    feature = jnp.where(spare < OWN_ROWS, kept[:, None] * OWN_ROWS + spare, -1).reshape(1, -1)
    ones = np.tile((np.arange(PACK) // 2 == OWN_ROWS // 2).astype(np.float32), RING * RING)
    order = (jnp.broadcast_to(feature, (8, RING * LANES)), ones[None, :])

    gain1 = norm1_gain[0].astype(F32)
    bias1 = norm1_bias[0].astype(F32)
    gain2 = norm2_gain[0].astype(F32)
    bias2 = norm2_bias[0].astype(F32)
    spot = (jnp.arange(RING * RING) == place)[:, None]

    def spread(piece):
        return jnp.where(spot, piece[None, :], 0.0).reshape(1, -1)

    qkv_row = jnp.concatenate([spread(qkv_bias[0, i].astype(F32)) for i in range(3)], axis=1)
    up_row = spread(up_bias[0].astype(F32))
    out_row = spread(out_bias[0].astype(F32) + down_bias[0].astype(F32))
    pack = like((RING, PACK, WIDTH), BF)
    pack_qkv = vmem_call(
        pack_qkv_body, pack, 1_000_000, (), gain1[:, None], bias1[:, None], qkv_row, qkv_weight[0]
    )
    own_up_pack, sent_up_pack = vmem_call(
        pack_up_body,
        (pack, pack),
        1_000_000,
        (first.astype(jnp.int32)[None],),
        gain2[:, None],
        bias2[:, None],
        up_row,
        up_weight[0],
    )
    out_high = out_row.astype(BF)
    out_low = (out_row - out_high.astype(F32)).astype(BF)
    pack_down = jnp.concatenate(
        [down_weight[0], out_high, out_low, jnp.zeros((PACK - OWN_ROWS - 2, WIDTH), BF)], axis=0
    )
    swap = moves(lambda s, a, b: flat(1 - s, a, b))

    def both(own, other):
        return jnp.where(first, own, other), jnp.where(first, other, own)

    qkv_layers = both(pack_qkv, send(pack_qkv, swap))
    other_ends = send(
        jnp.where(first, pipe_ends[0, 1, 0], pipe_ends[0, 0, 0]), swap
    )
    own_end = jnp.where(first, pipe_ends[0, 0, 0], pipe_ends[0, 1, 0])
    tokens_in = jnp.where(first, own_end, other_ends)
    cotangent = jnp.where(first, other_ends, own_end)

    lens = lax.dynamic_index_in_dim(seq_lengths[:, 0], core, 0, keepdims=False)
    starts = (dest * rows_dev).astype(jnp.int32)
    rows_at = (starts[:RING, None] + jnp.arange(rows_dev, dtype=jnp.int32)[None, :]).reshape(-1)
    finish = jnp.cumsum(lens)
    begin = jnp.sum(
        jnp.where(rows_at[None, :] >= finish[:, None], lens[:, None], 0), axis=0
    ).astype(jnp.int32)
    info = jnp.concatenate(
        [begin[None, :], rows_at[None, :], jnp.zeros((6, rows_at.shape[0]), jnp.int32)], axis=0
    )
    in_head = np.arange(2 * HEAD_DIM) % HEAD_DIM
    inv_freq = (10000.0 ** (-(in_head % 8) / 8.0)).astype(np.float32)
    inv_freq = np.where(in_head < 16, inv_freq, np.float32(0))
    angles = (rows_at - begin).astype(F32)[:, None] * inv_freq[None, :]
    tables = (jnp.cos(angles), jnp.sin(angles))
    geometry = (starts, info, tables)

    def to_columns(pack):
        def block_for(by):
            return lax.dynamic_index_in_dim(pack, (tp + by) % RING, 0, keepdims=False)

        parts = [block_for(0)] + [
            send(block_for(-by), along_weights(-by)) for by in (1, 3, 2)
        ]
        return jnp.concatenate(in_order(parts), axis=0)

    up_layers = both(own_up_pack, send(sent_up_pack, swap))
    down_layers = both(pack_down, send(pack_down, swap))
    turn = moves(lambda s, a, b: flat(1, b, a) if s == 0 else flat(0, a, b))
    stay = moves(lambda s, a, b: None if s == 0 else flat(s, b, a))
    out_other = send(out_weight[0], turn)
    out_turned = send(out_weight[0], stay)
    out_layers = jnp.where(first, out_weight[0], out_other), jnp.where(first, out_other, out_turned)
    row_packs = [jnp.concatenate([out_layers[i], down_layers[i]], axis=0) for i in range(2)]

    unit0, inv_std0 = unit_rows_of(tokens_in.astype(F32))
    xs0 = in_order(gathered_weights_axis(unit0.astype(BF)))
    columns = to_columns(
        jnp.concatenate([qkv_layers[0], up_layers[0], qkv_layers[1], up_layers[1]], axis=2)
    )
    columns = after(columns, *xs0)
    qkv0 = columns[:, :WIDTH]
    qkv0 = turned(
        in_order([qkv0] + [send(qkv0, along_tokens(-by)) for by in (1, 3, 2)]), sq
    )
    mlp0 = gather_tokens_axis(
        jnp.concatenate([columns[:, WIDTH : 2 * WIDTH], row_packs[0]], axis=1)
    )
    weights0 = (qkv0, (mlp0, 0), (mlp0, 1))

    out0, stored0 = forward_layer(
        tokens_in.astype(F32), xs0, weights0, geometry, order, False
    )
    gs1 = in_order(gathered_weights_axis(after(cotangent, stored0[1])))
    later = jnp.concatenate([columns[:, 2 * WIDTH :], row_packs[1]], axis=1)
    all1 = gather_tokens_axis(after(later, *stored0[2]))
    weights1 = ((all1, 0), (all1, 1), (all1, 2))
    low0 = out0.astype(BF)
    unit1, inv_std1 = unit_rows_of(low0.astype(F32))
    xs1 = in_order(gathered_weights_axis(unit1.astype(BF)))
    out1, stored1 = forward_layer(
        low0.astype(F32), xs1, weights1, geometry, order, True
    )
    low1 = out1.astype(BF)

    def up_swapped(value):
        value = value.reshape(RING, PACK, RING, SPOT)
        return value.transpose(2, 1, 0, 3).reshape(RING * PACK, WIDTH)

    def rows_turned(rows):
        out_part = jnp.where(first, rows[:OWN_ROWS], send(rows[:OWN_ROWS], stay))
        return jnp.concatenate([out_part, rows[OWN_ROWS:]], axis=0)

    def joined(part, layer):
        return (part.astype(F32) + to_core(part, layer).astype(F32)).astype(BF)

    def joined_up(part, layer):
        return joined(jnp.where(first, part, up_swapped(part)), layer)

    grad1, scattered1 = backward_layer(
        cotangent,
        gs1,
        unit1,
        inv_std1,
        weights1,
        stored1,
        geometry,
        order,
        (low1,),
    )
    gs0 = in_order(gathered_weights_axis(grad1))

    def swapped_rows(early, late):
        other = send(jnp.where(first, late, early), swap)
        mine = jnp.where(first, early, late)
        stacked = jnp.stack([jnp.where(first, mine, other), jnp.where(first, other, mine)])
        return stacked[None, :, None]

    layer_out = swapped_rows(low0, low1)

    def to_owner(scattered, columns, layer):
        return jnp.concatenate(
            [
                joined(columns[:, :WIDTH], layer),
                joined_up(columns[:, WIDTH:], layer),
                joined(rows_turned(scattered[:, 2 * WIDTH :]), layer),
            ],
            axis=1,
        )

    columns1 = over_weights(scattered1[:, : 2 * WIDTH], tp)
    owned1 = to_owner(scattered1, columns1, 1)
    grad0, scattered0 = backward_layer(
        grad1,
        gs0,
        unit0,
        inv_std0,
        weights0,
        stored0,
        geometry,
        order,
        (),
        (columns1,),
        (owned1,),
    )
    parts1 = over_replicas(owned1, 1)
    total1 = parts1[0].astype(F32)
    for part in parts1[1:]:
        total1 = total1 + part.astype(F32)
    total1 = total1.astype(BF)
    input_grad = swapped_rows(grad0, grad1)
    scattered0 = after(scattered0, total1, input_grad)
    columns0 = over_weights(scattered0[:, : 2 * WIDTH], tp)
    parts0 = over_replicas(to_owner(scattered0, columns0, 0), 0)


    column = like((8, OWN_ROWS), F32)
    gain1_grad, bias1_grad, gain2_grad, bias2_grad, qkv_grad, out_grad, up_grad, down_grad, *totals = vmem_call(
        finish_body,
        (
            column,
            column,
            column,
            column,
            like((OWN_ROWS, 3 * WIDTH), F32),
            like((OWN_ROWS, WIDTH), F32),
            like((OWN_ROWS, RING * WIDTH), F32),
            like((SPOT, WIDTH), F32),
            like((8, 3 * WIDTH), F32),
            like((8, RING * WIDTH), F32),
            like((8, WIDTH), F32),
        ),
        10_000_000,
        (first.astype(jnp.int32)[None],),
        *parts0,
        total1,
        gain1[:, None],
        bias1[:, None],
        gain2[:, None],
        bias2[:, None],
        qkv_weight[0],
        up_weight[0],
    )

    def own_piece(rows, parts):
        pieces = rows[0].reshape(parts, RING * RING, -1)
        return lax.dynamic_index_in_dim(pieces, place, 1, keepdims=False)

    s_qkv, s_up, s_g = totals
    bias_grad = own_piece(s_g, 1)[0]
    gradients = (
        gain1_grad[0],
        bias1_grad[0],
        gain2_grad[0],
        bias2_grad[0],
        qkv_grad,
        own_piece(s_qkv, 3),
        out_grad,
        bias_grad,
        up_grad,
        own_piece(s_up, 1)[0],
        down_grad,
        bias_grad,
    )
    return (layer_out, input_grad) + tuple(grad[None] for grad in gradients)


def solution(mesh):
    tokens = P("section", None, "replica", "fsdp", None)
    vector = P("section", "fsdp")
    matrix = P("section", "fsdp", None)
    three = P("section", None, "fsdp")
    params = (
        vector,
        vector,
        vector,
        vector,
        matrix,
        three,
        matrix,
        vector,
        matrix,
        vector,
        matrix,
        vector,
    )
    return jax.shard_map(
        on_device,
        mesh=mesh,
        in_specs=(tokens, P(None, "replica", None)) + params,
        out_specs=(tokens, tokens) + params,
        check_vma=False,
    )
```

```python
import jax
import jax.numpy as jnp
import numpy as np
from jax import lax
from jax.experimental import pallas as pl
from jax.experimental.pallas import tpu as pltpu
from jax.sharding import PartitionSpec as P

HEADS = 12
HEAD_DIM = 64
EPSILON = 1e-05
NEG_FILL = -1e30
WIDTH = 768
RING = 4
OWN_ROWS = 48
PACK = 64
LANES = 256
SPOT = 192
BF = jnp.bfloat16
F32 = jnp.float32
CORES = ("section", "fsdp")


def flat(core, a, b):
    return core * RING * RING + (a % RING) * RING + b % RING


def moves(step):
    return [
        (flat(core, a, b), step(core, a, b))
        for core in range(2)
        for a in range(RING)
        for b in range(RING)
        if step(core, a, b) is not None
    ]


def along_weights(by):
    return moves(lambda core, a, b: flat(core, a + by, b) if core == 0 else flat(core, a, b + by))


def along_tokens(by):
    return moves(lambda core, a, b: flat(core, a, b + by) if core == 0 else flat(core, a + by, b))


def token_groups():
    return [[flat(0, a, b) for b in range(RING)] for a in range(RING)] + [
        [flat(1, a, b) for a in range(RING)] for b in range(RING)
    ]


def send(value, pairs):
    return lax.ppermute(value, CORES, pairs)


def gather_tokens_axis(block):
    return lax.all_gather(block, CORES, axis=0, tiled=True, axis_index_groups=token_groups())


def scatter_tokens_axis(total):
    return lax.psum_scatter(
        total, CORES, scatter_dimension=0, tiled=True, axis_index_groups=token_groups()
    )


def gathered_weights_axis(block):
    return [block] + [send(block, along_weights(-by)) for by in (1, 3, 2)]


ORDER = (0, 1, 3, 2)


def turned(blocks, by):
    rows = blocks[0].shape[0]
    twice = jnp.concatenate(list(blocks) + list(blocks), axis=0)
    return lax.dynamic_slice_in_dim(twice, ((RING - by) % RING) * rows, RING * rows, 0)


def in_order(blocks):
    found = dict(zip(ORDER, blocks))
    return [found[i] for i in range(RING)]


def after(value, *others):
    return lax.optimization_barrier((value,) + others)[0]


def vmem_call(body, out_shapes, flops, scalars, *arrays, steps=1):
    specs, operands = [], []
    for item in arrays:
        array, column = item if isinstance(item, tuple) else (item, None)
        block = array.shape if column is None else (array.shape[0], WIDTH)
        place = (0,) * array.ndim if column is None else (0, column)
        specs.append(pl.BlockSpec(block, lambda i, place=place: place))
        operands.append(array)
    return pl.pallas_call(
        body,
        grid=(steps,),
        out_shape=out_shapes,
        in_specs=[pl.BlockSpec(memory_space=pltpu.SMEM)] * len(scalars) + specs,
        out_specs=pl.BlockSpec(
            (out_shapes.shape[0], out_shapes.shape[1] // steps), lambda i: (0, steps - 1 - i)
        )
        if steps > 1
        else jax.tree.map(
            lambda shape: pl.BlockSpec(shape.shape, lambda i, n=len(shape.shape): (0,) * n),
            out_shapes,
        ),
        compiler_params=pltpu.CompilerParams(vmem_limit_bytes=56 * 1024 * 1024),
        cost_estimate=pl.CostEstimate(flops=flops, bytes_accessed=4_000_000, transcendentals=0),
    )(*scalars, *operands)


def like(shape, dtype):
    return jax.ShapeDtypeStruct(shape, dtype)


def mm(left, right):
    return lax.dot_general(left, right, (((1,), (0,)), ((), ())), preferred_element_type=F32)


def mm_nt(left, right):
    return lax.dot_general(left, right, (((1,), (1,)), ((), ())), preferred_element_type=F32)


def mm_exact(left, right):
    return lax.dot_general(
        left,
        right,
        (((1,), (1,)), ((), ())),
        precision=lax.Precision.HIGHEST,
        preferred_element_type=F32,
    )


def mm_tn(left, right):
    return lax.dot_general(left, right, (((0,), (0,)), ((), ())), preferred_element_type=F32)


def bias_rows(bias, weight, row):
    row = row + jnp.sum(bias * weight, axis=0, keepdims=True)
    high = row.astype(BF)
    low = (row - high.astype(F32)).astype(BF)
    return jnp.concatenate(
        [high, low, jnp.zeros((PACK - OWN_ROWS - 2, row.shape[1]), BF)], axis=0
    )


def as_column(row):
    size = row.shape[1]
    at = lax.broadcasted_iota(jnp.int32, (size, size), 0)
    lane = lax.broadcasted_iota(jnp.int32, (size, size), 1)
    return jnp.sum(jnp.where(at == lane, row, 0.0), axis=1, keepdims=True)


def spread(piece, place):
    size = piece.shape[1]
    whole = jnp.concatenate([piece] * (RING * RING), axis=1)
    lane = lax.broadcasted_iota(jnp.int32, whole.shape, 1)
    return jnp.where((lane >= place * size) & (lane < (place + 1) * size), whole, 0.0)


def pack_body(
    first_ref, place_ref, gain1, bias1, gain2, bias2, w_qkv, b_qkv, w_up, b_up, w_down, b_out, b_down,
    own_ref, sent_ref, down_ref
):
    first = first_ref[0] == 1
    place = place_ref[0]
    weight = w_qkv[...].astype(F32)
    scaled = (weight * as_column(gain1[...].astype(F32))).astype(BF)
    three = spread(b_qkv[...].astype(F32), place)
    row = jnp.concatenate([three[i : i + 1] for i in range(3)], axis=1)
    extra = bias_rows(as_column(bias1[...].astype(F32)), weight, row)
    whole = jnp.concatenate([scaled, extra], axis=0)
    spare = jnp.zeros((PACK, LANES - SPOT), BF)
    for t in range(RING):
        for i in range(3):
            at = i * WIDTH + t * SPOT
            part = jnp.concatenate([whole[:, at : at + SPOT], spare], axis=1)
            own_ref[t, :, i * LANES : (i + 1) * LANES] = part
            sent_ref[t, :, i * LANES : (i + 1) * LANES] = part
    weight = w_up[...].astype(F32)
    scaled = (weight * as_column(gain2[...].astype(F32))).astype(BF)
    extra = bias_rows(
        as_column(bias2[...].astype(F32)), weight, spread(b_up[...].astype(F32), place)
    )
    whole = jnp.concatenate([scaled, extra], axis=0)
    for t in range(RING):
        by_a = whole[:, t * WIDTH : (t + 1) * WIDTH]
        by_b = jnp.concatenate(
            [whole[:, a * WIDTH + t * SPOT : a * WIDTH + (t + 1) * SPOT] for a in range(RING)],
            axis=1,
        )
        own_ref[t, :, WIDTH:] = jnp.where(first, by_a, by_b)
        sent_ref[t, :, WIDTH:] = jnp.where(first, by_b, by_a)
    down_ref[:SPOT] = w_down[...]
    rows = [spread(b[...].astype(F32), place).astype(BF) for b in (b_out, b_down)]
    rows.append(jnp.zeros((PACK - OWN_ROWS - 2, WIDTH), BF))
    down_ref[SPOT:] = jnp.concatenate(rows, axis=0)


def out_rows(rows):
    parts = [rows[j * LANES : j * LANES + OWN_ROWS, :] for j in range(RING)]
    return jnp.concatenate(parts + [jnp.zeros((LANES - SPOT, WIDTH), BF)], axis=0)


def down_rows(rows):
    parts = [rows[j * LANES + OWN_ROWS : j * LANES + OWN_ROWS + SPOT, :] for j in range(RING)]
    return jnp.concatenate(parts, axis=0)


def out_bias_row(rows):
    total = jnp.zeros((1, WIDTH), F32)
    for j in range(RING):
        extra = rows[j * LANES + OWN_ROWS + SPOT : (j + 1) * LANES, :].astype(F32)
        total = total + extra[0:1, :] + extra[1:2, :]
    return total


def rotate(value, cos, sin):
    cos = jnp.concatenate([cos, cos], axis=1)
    sin = jnp.concatenate([sin, sin], axis=1)
    lanes = value.shape[1]
    lane = lax.broadcasted_iota(jnp.int32, value.shape, 1)
    other = jnp.where(
        (lane & (HEAD_DIM - 1)) < 8,
        -pltpu.roll(value, lanes - 8, 1),
        pltpu.roll(value, 8, 1),
    )
    return value * cos + other * sin


def places(feature):
    row = lax.broadcasted_iota(jnp.int32, (WIDTH, feature.shape[1]), 0)
    return jnp.where(row == feature[0:1, :], 1.0, 0.0).astype(BF)


def project_body(x0, x1, x2, x3, feature, ones, w, cos, sin, x_ref, q_ref, kv_ref):
    x = jnp.concatenate([x0[...], x1[...], x2[...], x3[...]], axis=0)
    x_all = (mm(x, places(feature)) + ones[...]).astype(BF)
    x_ref[...] = x_all
    qkv = mm(x_all, w[...])
    tables = cos[...], sin[...]
    q_ref[...] = (rotate(qkv[:, :LANES], *tables) * 0.125).astype(BF)
    kv_ref[:, :LANES] = rotate(qkv[:, LANES : 2 * LANES], *tables).astype(BF)
    kv_ref[:, LANES:] = qkv[:, 2 * LANES :].astype(BF)


def store_parts(partial, outs):
    block = partial.shape[0] // len(outs)
    for i, out in enumerate(outs):
        out[...] = partial[i * block : (i + 1) * block].astype(out.dtype)


def mlp_body(x_ref, w_up, rows, *refs):
    given = 0 if len(refs) == 3 else 1
    mids, (hidden_ref, slope_ref), outs = refs[:given], refs[given : given + 2], refs[given + 2 :]
    up_proj = mm(x_ref[...], w_up[...])
    cdf = 0.5 * (1.0 + lax.erf(up_proj * 0.7071067811865476))
    hidden = (up_proj * cdf).astype(BF)
    hidden_ref[...] = hidden
    density = jnp.exp(-0.5 * up_proj * up_proj) * 0.3989422804014327
    slope_ref[...] = (cdf + up_proj * density).astype(BF)
    partial = mm(hidden, down_rows(rows)) + out_bias_row(rows)
    for mid in mids:
        partial = partial + mm(mid[...], out_rows(rows))
    store_parts(partial, outs)


def head_mask(value, head):
    lane = lax.broadcasted_iota(jnp.int32, value.shape, 1)
    return jnp.where((lane >= head * HEAD_DIM) & (lane < (head + 1) * HEAD_DIM), value, 0)


def allowed_pairs(starts_ref, info, e, rows):
    part = rows // RING
    pieces = []
    for d in range(RING):
        base = lax.broadcasted_iota(jnp.int32, (part, rows), 0) + starts_ref[e * RING + d]
        pieces.append(jnp.where((base >= info[0:1, :]) & (base <= info[1:2, :]), 0.0, NEG_FILL))
    return jnp.concatenate(pieces, axis=0)


def attend_body(starts_ref, info_ref, q_ref, kv0, kv1, kv2, kv3, *refs):
    given = 0 if len(refs) == 2 else 2
    others, (mid_ref, lse_ref), outs = refs[:given], refs[given : given + 2], refs[given + 2 :]
    rows = q_ref.shape[0]
    info = info_ref[...]
    q = q_ref[...]
    masked_q = [head_mask(q, h) for h in range(3)]
    tops, sums, accs = [None] * 3, [None] * 3, [None] * 3
    for e, kv in enumerate((kv0, kv1, kv2, kv3)):
        bias = allowed_pairs(starts_ref, info, e, rows)
        keys = kv[:, :LANES]
        values_t = kv[:, LANES:].T
        for h in range(3):
            scores = mm_nt(keys, masked_q[h]) + bias
            top = jnp.max(scores, axis=0, keepdims=True)
            if e:
                top = jnp.maximum(tops[h], top)
            probs = jnp.exp(scores - top)
            total = jnp.sum(probs, axis=0, keepdims=True)
            part = mm(values_t[h * HEAD_DIM : (h + 1) * HEAD_DIM, :], probs.astype(BF))
            if e:
                shrink = jnp.exp(tops[h] - top)
                total = total + sums[h] * shrink
                part = part + accs[h] * shrink
            tops[h], sums[h], accs[h] = top, total, part
    mids = [accs[h] / sums[h] for h in range(3)] + [jnp.zeros((HEAD_DIM, rows), F32)]
    mid = jnp.concatenate(mids, axis=0).T.astype(BF)
    mid_ref[...] = mid
    for h in range(3):
        lse_ref[h : h + 1, :] = tops[h] + jnp.log(sums[h])
    lse_ref[3:, :] = jnp.zeros((5, rows), F32)
    if others:
        rows_ref, mlp_ref = others
        store_parts(mm(mid, out_rows(rows_ref)) + mlp_ref[...], outs)


def attend_back_body(
    starts_ref, info_ref, q_ref, a0, a1, a2, a3, rows_ref, mid_ref, lse_ref, cos, sin,
    kv0, kv1, kv2, kv3, dq_ref, g0, g1, g2, g3
):
    rows = q_ref.shape[0]
    info = info_ref[...]
    q = q_ref[...]
    g_all = jnp.concatenate([a0[...], a1[...], a2[...], a3[...]], axis=0)
    do = mm_nt(g_all, out_rows(rows_ref)).astype(BF)
    lse = lse_ref[...]
    lane = lax.broadcasted_iota(jnp.int32, (8, LANES), 1)
    head = lax.broadcasted_iota(jnp.int32, (8, LANES), 0)
    pick = jnp.where(lane // HEAD_DIM == head, 1.0, 0.0)
    products = do.astype(F32) * mid_ref[...].astype(F32)
    delta = lax.dot_general(
        pick,
        products,
        (((1,), (1,)), ((), ())),
        precision=lax.Precision.HIGHEST,
        preferred_element_type=F32,
    )
    masked_q = [head_mask(q, h) for h in range(3)]
    masked_do = [head_mask(do, h) for h in range(3)]
    dq = [None] * 3
    for e, (kv, grad) in enumerate(zip((kv0, kv1, kv2, kv3), (g0, g1, g2, g3))):
        bias = allowed_pairs(starts_ref, info, e, rows)
        keys = kv[:, :LANES]
        keys_t = keys.T
        values = kv[:, LANES:]
        dk = jnp.zeros((rows, LANES), F32)
        dv = jnp.zeros((rows, LANES), F32)
        for h in range(3):
            scores = mm_nt(keys, masked_q[h]) + bias
            probs = jnp.exp(scores - lse[h : h + 1, :])
            dprobs = mm_nt(values, masked_do[h])
            dscores = (probs * (dprobs - delta[h : h + 1, :])).astype(BF)
            dv = dv + mm(probs.astype(BF), masked_do[h])
            dk = dk + mm(dscores, masked_q[h])
            part = mm(keys_t[h * HEAD_DIM : (h + 1) * HEAD_DIM, :], dscores)
            dq[h] = part if e == 0 else dq[h] + part
        grad[:, :LANES] = dk.astype(BF)
        grad[:, LANES:] = dv.astype(BF)
    dq_all = jnp.concatenate(dq + [jnp.zeros((HEAD_DIM, rows), F32)], axis=0).T * 0.125
    dq_ref[...] = rotate(dq_all, cos[...], -sin[...]).astype(BF)


def mlp_back_body(a0, a1, a2, a3, slope, w_up, rows, grad_ref, dx_ref):
    g_all = jnp.concatenate([a0[...], a1[...], a2[...], a3[...]], axis=0)
    grad_up = (mm_nt(g_all, down_rows(rows)) * slope[...].astype(F32)).astype(BF)
    grad_ref[...] = grad_up
    dx_ref[...] = mm_nt(grad_up, w_up[...])


def weight_grads_body(a0, a1, a2, a3, hidden, mid, x_ref, grad_qkv, grad_up, out_ref):
    step = pl.program_id(0)

    @pl.when(step == 0)
    def rows_part():
        g_all = jnp.concatenate([a0[...], a1[...], a2[...], a3[...]], axis=0)
        down_grad = mm_tn(hidden[...], g_all).astype(BF)
        out_grad = mm_tn(mid[...], g_all).astype(BF)
        sums = jnp.sum(g_all.astype(F32), axis=0, keepdims=True)
        sums = jnp.broadcast_to(sums, (PACK - OWN_ROWS, WIDTH)).astype(BF)
        for j in range(RING):
            at = j * LANES
            out_ref[at : at + OWN_ROWS, :] = out_grad[j * OWN_ROWS : (j + 1) * OWN_ROWS]
            out_ref[at + OWN_ROWS : at + OWN_ROWS + SPOT, :] = down_grad[j * SPOT : (j + 1) * SPOT]
            out_ref[at + OWN_ROWS + SPOT : at + LANES, :] = sums

    @pl.when(step == 1)
    def up_part():
        out_ref[...] = mm_tn(x_ref[...], grad_up[...]).astype(BF)

    @pl.when(step == 2)
    def qkv_part():
        out_ref[...] = mm_tn(x_ref[...], grad_qkv[...]).astype(BF)


def qkv_back_body(
    dq, g0, g1, g2, g3, cos, sin, w_qkv, dx_up, feature, grad_ref, d0, d1, d2, d3
):
    dkv = g0[...].astype(F32)
    for part in (g1, g2, g3):
        dkv = dkv + part[...].astype(F32)
    dk = rotate(dkv[:, :LANES], cos[...], -sin[...])
    grad = jnp.concatenate([dq[...], dk.astype(BF), dkv[:, LANES:].astype(BF)], axis=1)
    grad_ref[...] = grad
    dx = (mm_nt(grad, w_qkv[...]) + dx_up[...]).astype(BF)
    store_parts(mm_nt(dx, places(feature)), (d0, d1, d2, d3))


def own_piece(row, place):
    size = row.shape[1] // (RING * RING)
    return sum(
        jnp.where(place == f, row[:, f * size : (f + 1) * size], 0.0) for f in range(RING * RING)
    )


def finish_body(
    first_ref, place_ref, l0, l1, r0, r1, sums, gain1, bias1, gain2, bias2, w_qkv, w_up,
    gain1_ref, bias1_ref, gain2_ref, bias2_ref, qkv_ref, b_qkv_ref, out_ref, b_out_ref, up_ref, b_up_ref, down_ref
):
    first = first_ref[0] == 1
    place = place_ref[0]

    def total(low, high):
        value = jnp.concatenate(
            [
                one[:, low:high].astype(F32) + two[:, low:high].astype(F32)
                for one, two in ((l0, r0), (l1, r1))
            ],
            axis=0,
        )
        return jnp.where(first, value, sums[:, low:high].astype(F32))

    m = total(0, WIDTH)
    m_qkv = jnp.concatenate(
        [
            m[t * PACK : (t + 1) * PACK, i * LANES : i * LANES + SPOT]
            for i in range(3)
            for t in range(RING)
        ],
        axis=1,
    )
    m = total(WIDTH, 2 * WIDTH)
    m_up = jnp.concatenate([m[t * PACK : (t + 1) * PACK] for t in range(RING)], axis=1)
    rows = total(2 * WIDTH, 3 * WIDTH)
    out_ref[...] = rows[:OWN_ROWS]
    down_ref[...] = rows[OWN_ROWS : OWN_ROWS + SPOT]
    b_out_ref[...] = own_piece(rows[OWN_ROWS + SPOT : OWN_ROWS + SPOT + 1], place)
    for m, w_ref, gain, bias, gain_ref, bias_ref, grad_ref in (
        (m_qkv, w_qkv, gain1, bias1, gain1_ref, bias1_ref, qkv_ref),
        (m_up, w_up, gain2, bias2, gain2_ref, bias2_ref, up_ref),
    ):
        ends = m[OWN_ROWS : OWN_ROWS + 1]
        m = m[:OWN_ROWS]
        weight = w_ref[...].astype(F32)
        all_ones = jnp.ones((8, m.shape[1]), F32)
        gain_ref[...] = mm_exact(all_ones, weight * m)[0:1]
        bias_ref[...] = mm_exact(all_ones, weight * ends)[0:1]
        grad_ref[...] = as_column(gain[...].astype(F32)) * m + as_column(bias[...].astype(F32)) * ends
    ends = m_qkv[OWN_ROWS : OWN_ROWS + 1]
    b_qkv_ref[...] = jnp.concatenate(
        [own_piece(ends[:, i * WIDTH : (i + 1) * WIDTH], place) for i in range(3)], axis=0
    )
    b_up_ref[...] = own_piece(m_up[OWN_ROWS : OWN_ROWS + 1], place)


def unit_rows_of(rows):
    centered = rows - jnp.mean(rows, axis=-1, keepdims=True)
    inv_std = lax.rsqrt(jnp.mean(centered * centered, axis=-1, keepdims=True) + EPSILON)
    return centered * inv_std, inv_std


def forward_layer(tok_rows, xs, weights, geometry, order, mlp_first):
    w_qkv, w_up, w_rows = weights
    starts, info, tables = geometry
    own = tok_rows.shape[0]
    rows = RING * own
    x_all, q, kv = vmem_call(
        project_body,
        (
            like((rows, RING * LANES), BF),
            like((rows, LANES), BF),
            like((rows, 2 * LANES), BF),
        ),
        1_600_000_000,
        (),
        *xs,
        *order,
        w_qkv,
        *tables,
    )
    kvs = in_order([kv] + [send(kv, along_tokens(-by)) for by in (1, 3, 2)])
    whole = (like((rows, WIDTH), F32),)
    cut = (like((own, WIDTH), F32),) + (like((own, WIDTH), BF),) * (RING - 1)

    def mlp(attended, outs):
        return vmem_call(
            mlp_body,
            (like((rows, WIDTH), BF), like((rows, WIDTH), BF)) + outs,
            2_000_000_000,
            (),
            x_all,
            w_up,
            w_rows,
            *attended,
        )

    def attention(others, outs):
        return vmem_call(
            attend_body,
            (like((rows, LANES), BF), like((8, rows), F32)) + outs,
            6_000_000_000,
            (starts,),
            info,
            q,
            *kvs,
            *others,
        )

    if mlp_first:
        hidden, slope, partial = mlp((), whole)
        mid, lse, *parts = attention((w_rows, partial), cut)
    else:
        mid, lse = attention((), ())
        hidden, slope, *parts = mlp((mid,), cut)
    total = tok_rows + parts[0]
    for by in (1, 3, 2):
        total = total + send(parts[by], along_weights(by)).astype(F32)
    return total, (x_all, q, kvs, hidden, slope, mid, lse)


def backward_layer(
    grad_rows, gs, unit, inv_std, weights, stored, geometry, order, tie=()
):
    w_qkv, w_up, w_rows = weights
    starts, info, tables = geometry
    x_all, q, kvs, hidden, slope, mid, lse = stored
    own = grad_rows.shape[0]
    rows = RING * own

    def attention_back(gs):
        return vmem_call(
            attend_back_body,
            (like((rows, LANES), BF),) + (like((rows, 2 * LANES), BF),) * RING,
            16_000_000_000,
            (starts,),
            info,
            q,
            *gs,
            w_rows,
            mid,
            lse,
            *tables,
            *kvs,
        )

    dq, *dkvs = attention_back(gs)
    received = [send(dkvs[by], along_tokens(by)) for by in (1, 3, 2)]
    grad_up, dx_up = vmem_call(
        mlp_back_body,
        (like((rows, WIDTH), BF), like((rows, RING * LANES), F32)),
        1_600_000_000,
        (),
        *([after(gs[0], *tie)] + gs[1:]),
        slope,
        w_up,
        w_rows,
    )
    grad_qkv, *dxs = vmem_call(
        qkv_back_body,
        (like((rows, WIDTH), BF),) + (like((own, WIDTH), BF),) * RING,
        2_000_000_000,
        (),
        dq,
        dkvs[0],
        *received,
        *tables,
        w_qkv,
        dx_up,
        order[0],
    )
    total = dxs[0].astype(F32)
    for by in (1, 3, 2):
        total = total + send(dxs[by], along_weights(by)).astype(F32)
    grad_in = grad_rows.astype(F32) + inv_std * (
        total
        - jnp.mean(total, axis=-1, keepdims=True)
        - unit * jnp.mean(total * unit, axis=-1, keepdims=True)
    )
    grad_in = grad_in.astype(BF)
    cuts = vmem_call(
        weight_grads_body,
        like((RING * LANES, 3 * WIDTH), BF),
        3_000_000_000,
        (),
        *gs,
        hidden,
        mid,
        x_all,
        after(grad_qkv, *((grad_in,) if tie else ())),
        grad_up,
        steps=3,
    )
    return grad_in, scatter_tokens_axis(cuts), cuts


def over_weights(total, tp):
    parts = [total[:PACK]] + [
        send(total[by * PACK : (by + 1) * PACK], along_weights(by)) for by in (1, 3, 2)
    ]
    near = in_order(parts)
    return turned([near[0], near[3], near[2], near[1]], tp)


def to_core(value, core):
    return send(value, moves(lambda s, a, b: flat(core, a, b) if s != core else None))


def over_replicas(low, core):
    rest = lax.axis_size("replica")

    def swapped(value, partner):
        pairs = [(core * rest + i, core * rest + partner(i)) for i in range(rest)]
        return lax.ppermute(value, ("section", "replica"), pairs)

    def inner(i):
        return i ^ 1

    def outer(i):
        return rest - 1 - i

    half = low.shape[0] // 2
    left, right = low[:half], low[half:]
    left = (left.astype(F32) + swapped(left, inner).astype(F32)).astype(BF)
    right = (right.astype(F32) + swapped(right, outer).astype(F32)).astype(BF)
    return left, right, swapped(left, outer), swapped(right, inner)


def on_device(
    pipe_ends,
    seq_lengths,
    norm1_gain,
    norm1_bias,
    norm2_gain,
    norm2_bias,
    qkv_weight,
    qkv_bias,
    out_weight,
    out_bias,
    up_weight,
    up_bias,
    down_weight,
    down_bias,
):
    core = lax.axis_index("section")
    first = core == 0
    place = lax.axis_index("fsdp")
    a_at, b_at = place // RING, place % RING
    tp = jnp.where(first, a_at, b_at)
    sq = jnp.where(first, b_at, a_at)
    rows_dev = pipe_ends.shape[3]

    def block_of(weight_at, token_at):
        weight_at, token_at = weight_at % RING, token_at % RING
        return jnp.where(first, RING * weight_at + token_at, RING * token_at + weight_at)

    ring = jnp.arange(RING, dtype=jnp.int32)
    dest = block_of(tp + ring[None, :], sq + ring[:, None]).reshape(-1).astype(jnp.int32)
    kept = block_of(tp + ring[None, :], ring[:, None]).reshape(-1).astype(jnp.int32)
    spare = jnp.arange(PACK, dtype=jnp.int32)[None, :]
    feature = jnp.where(spare < OWN_ROWS, kept[:, None] * OWN_ROWS + spare, -1).reshape(1, -1)
    ones = np.tile((np.arange(PACK) // 2 == OWN_ROWS // 2).astype(np.float32), RING * RING)
    order = (jnp.broadcast_to(feature, (8, RING * LANES)), ones[None, :])

    flags = (first.astype(jnp.int32)[None], place.astype(jnp.int32)[None])
    pack = like((RING, PACK, 2 * WIDTH), BF)
    own_pack, sent_pack, pack_down = vmem_call(
        pack_body,
        (pack, pack, like((SPOT + PACK - OWN_ROWS, WIDTH), BF)),
        1_000_000,
        flags,
        norm1_gain,
        norm1_bias,
        norm2_gain,
        norm2_bias,
        qkv_weight[0],
        qkv_bias[0],
        up_weight[0],
        up_bias,
        down_weight[0],
        out_bias,
        down_bias,
    )
    swap = moves(lambda s, a, b: flat(1 - s, a, b))

    def both(own, other):
        return jnp.where(first, own, other), jnp.where(first, other, own)

    early_pack, late_pack = both(own_pack, send(sent_pack, swap))
    other_ends = send(
        jnp.where(first, pipe_ends[0, 1, 0], pipe_ends[0, 0, 0]), swap
    )
    own_end = jnp.where(first, pipe_ends[0, 0, 0], pipe_ends[0, 1, 0])
    tokens_in = jnp.where(first, own_end, other_ends)
    cotangent = jnp.where(first, other_ends, own_end)

    lens = lax.dynamic_index_in_dim(seq_lengths[:, 0], core, 0, keepdims=False)
    starts = (dest * rows_dev).astype(jnp.int32)
    rows_at = (starts[:RING, None] + jnp.arange(rows_dev, dtype=jnp.int32)[None, :]).reshape(-1)
    finish = jnp.cumsum(lens)
    begin = jnp.sum(
        jnp.where(rows_at[None, :] >= finish[:, None], lens[:, None], 0), axis=0
    ).astype(jnp.int32)
    info = jnp.concatenate(
        [begin[None, :], rows_at[None, :], jnp.zeros((6, rows_at.shape[0]), jnp.int32)], axis=0
    )
    in_head = np.arange(2 * HEAD_DIM) % HEAD_DIM
    inv_freq = (10000.0 ** (-(in_head % 8) / 8.0)).astype(np.float32)
    inv_freq = np.where(in_head < 16, inv_freq, np.float32(0))
    angles = (rows_at - begin).astype(F32)[:, None] * inv_freq[None, :]
    tables = (jnp.cos(angles), jnp.sin(angles))
    geometry = (starts, info, tables)

    def to_columns(pack):
        def block_for(by):
            return lax.dynamic_index_in_dim(pack, (tp + by) % RING, 0, keepdims=False)

        parts = [block_for(0)] + [
            send(block_for(-by), along_weights(-by)) for by in (1, 3, 2)
        ]
        return jnp.concatenate(in_order(parts), axis=0)

    down_layers = both(pack_down, send(pack_down, swap))
    turn = moves(lambda s, a, b: flat(1, b, a) if s == 0 else flat(0, a, b))
    stay = moves(lambda s, a, b: None if s == 0 else flat(s, b, a))
    out_other = send(out_weight[0], turn)
    out_turned = send(out_weight[0], stay)
    out_layers = jnp.where(first, out_weight[0], out_other), jnp.where(first, out_other, out_turned)
    row_packs = [jnp.concatenate([out_layers[i], down_layers[i]], axis=0) for i in range(2)]

    unit0, inv_std0 = unit_rows_of(tokens_in.astype(F32))
    xs0 = in_order(gathered_weights_axis(unit0.astype(BF)))
    columns = to_columns(jnp.concatenate([early_pack, late_pack], axis=2))
    columns = after(columns, *xs0, info, *tables)
    qkv0 = columns[:, :WIDTH]
    qkv0 = turned(
        in_order([qkv0] + [send(qkv0, along_tokens(-by)) for by in (1, 3, 2)]), sq
    )
    mlp0 = gather_tokens_axis(
        jnp.concatenate([columns[:, WIDTH : 2 * WIDTH], row_packs[0]], axis=1)
    )
    weights0 = (qkv0, (mlp0, 0), (mlp0, 1))

    out0, stored0 = forward_layer(
        tokens_in.astype(F32), xs0, weights0, geometry, order, False
    )
    gs1 = in_order(gathered_weights_axis(after(cotangent, stored0[1])))
    later = jnp.concatenate([columns[:, 2 * WIDTH :], row_packs[1]], axis=1)
    all1 = gather_tokens_axis(after(later, *stored0[2]))
    weights1 = ((all1, 0), (all1, 1), (all1, 2))
    low0 = out0.astype(BF)
    unit1, inv_std1 = unit_rows_of(low0.astype(F32))
    xs1 = in_order(gathered_weights_axis(unit1.astype(BF)))
    out1, stored1 = forward_layer(
        low0.astype(F32), xs1, weights1, geometry, order, True
    )
    low1 = out1.astype(BF)

    def up_swapped(value):
        value = value.reshape(RING, PACK, RING, SPOT)
        return value.transpose(2, 1, 0, 3).reshape(RING * PACK, WIDTH)

    def rows_turned(rows):
        out_part = jnp.where(first, rows[:OWN_ROWS], send(rows[:OWN_ROWS], stay))
        return jnp.concatenate([out_part, rows[OWN_ROWS:]], axis=0)

    def joined(part, layer):
        return (part.astype(F32) + to_core(part, layer).astype(F32)).astype(BF)

    def joined_up(part, layer):
        return joined(jnp.where(first, part, up_swapped(part)), layer)

    grad1, scattered1, unused = backward_layer(
        cotangent,
        gs1,
        unit1,
        inv_std1,
        weights1,
        stored1,
        geometry,
        order,
        (low1,),
    )
    gs0 = in_order(gathered_weights_axis(grad1))

    def swapped_rows(early, late):
        other = send(jnp.where(first, late, early), swap)
        mine = jnp.where(first, early, late)
        stacked = jnp.stack([jnp.where(first, mine, other), jnp.where(first, other, mine)])
        return stacked[None, :, None]

    layer_out = swapped_rows(low0, low1)

    def to_owner(scattered, columns, layer):
        return jnp.concatenate(
            [
                joined(columns[:, :WIDTH], layer),
                joined_up(columns[:, WIDTH:], layer),
                joined(rows_turned(scattered[:, 2 * WIDTH :]), layer),
            ],
            axis=1,
        )

    grad0, scattered0, cuts0 = backward_layer(
        grad1, gs0, unit0, inv_std0, weights0, stored0, geometry, order
    )
    scattered1 = after(scattered1, cuts0)
    columns1 = over_weights(scattered1[:, : 2 * WIDTH], tp)
    left, right, left_rest, right_rest = over_replicas(to_owner(scattered1, columns1, 1), 1)
    total1 = jnp.concatenate(
        [
            (one.astype(F32) + two.astype(F32)).astype(BF)
            for one, two in ((left, left_rest), (right, right_rest))
        ],
        axis=0,
    )
    input_grad = swapped_rows(grad0, grad1)
    scattered0 = after(scattered0, total1, input_grad)
    columns0 = over_weights(scattered0[:, : 2 * WIDTH], tp)
    parts0 = over_replicas(to_owner(scattered0, columns0, 0), 0)


    vector = like((1, OWN_ROWS), F32)
    gain1_grad, bias1_grad, gain2_grad, bias2_grad, *grads = vmem_call(
        finish_body,
        (
            vector,
            vector,
            vector,
            vector,
            like((OWN_ROWS, 3 * WIDTH), F32),
            like((3, OWN_ROWS), F32),
            like((OWN_ROWS, WIDTH), F32),
            vector,
            like((OWN_ROWS, RING * WIDTH), F32),
            like((1, SPOT), F32),
            like((SPOT, WIDTH), F32),
        ),
        10_000_000,
        flags,
        *parts0,
        total1,
        norm1_gain,
        norm1_bias,
        norm2_gain,
        norm2_bias,
        qkv_weight[0],
        up_weight[0],
    )
    qkv_grad, qkv_bias_grad, out_grad, end_grad, up_grad, up_bias_grad, down_grad = grads
    return (
        layer_out,
        input_grad,
        gain1_grad,
        bias1_grad,
        gain2_grad,
        bias2_grad,
        qkv_grad[None],
        qkv_bias_grad[None],
        out_grad[None],
        end_grad,
        up_grad[None],
        up_bias_grad,
        down_grad[None],
        end_grad,
    )


def solution(mesh):
    tokens = P("section", None, "replica", "fsdp", None)
    vector = P("section", "fsdp")
    matrix = P("section", "fsdp", None)
    three = P("section", None, "fsdp")
    params = (
        vector,
        vector,
        vector,
        vector,
        matrix,
        three,
        matrix,
        vector,
        matrix,
        vector,
        matrix,
        vector,
    )
    return jax.shard_map(
        on_device,
        mesh=mesh,
        in_specs=(tokens, P(None, "replica", None)) + params,
        out_specs=(tokens, tokens) + params,
        check_vma=False,
    )
```

```python
import jax
import jax.numpy as jnp
import numpy as np
from jax import lax
from jax.experimental import pallas as pl
from jax.experimental.pallas import tpu as pltpu
from jax.sharding import PartitionSpec as P

HEADS = 12
HEAD_DIM = 64
EPSILON = 1e-05
NEG_FILL = -1e30
WIDTH = 768
RING = 4
OWN_ROWS = 48
PACK = 64
LANES = 256
SPOT = 192
BF = jnp.bfloat16
F32 = jnp.float32
CORES = ("section", "fsdp")


def flat(core, a, b):
    return core * RING * RING + (a % RING) * RING + b % RING


def moves(step):
    return [
        (flat(core, a, b), step(core, a, b))
        for core in range(2)
        for a in range(RING)
        for b in range(RING)
        if step(core, a, b) is not None
    ]


def along_weights(by):
    return moves(lambda core, a, b: flat(core, a + by, b) if core == 0 else flat(core, a, b + by))


def along_tokens(by):
    return moves(lambda core, a, b: flat(core, a, b + by) if core == 0 else flat(core, a + by, b))


def token_groups():
    return [[flat(0, a, b) for b in range(RING)] for a in range(RING)] + [
        [flat(1, a, b) for a in range(RING)] for b in range(RING)
    ]


def send(value, pairs):
    return lax.ppermute(value, CORES, pairs)


def gather_tokens_axis(block):
    return lax.all_gather(block, CORES, axis=0, tiled=True, axis_index_groups=token_groups())


def scatter_tokens_axis(total):
    return lax.psum_scatter(
        total, CORES, scatter_dimension=0, tiled=True, axis_index_groups=token_groups()
    )


def gathered_weights_axis(block):
    return [block] + [send(block, along_weights(-by)) for by in (1, 3, 2)]


ORDER = (0, 1, 3, 2)


def turned(blocks, by):
    rows = blocks[0].shape[0]
    twice = jnp.concatenate(list(blocks) + list(blocks), axis=0)
    return lax.dynamic_slice_in_dim(twice, ((RING - by) % RING) * rows, RING * rows, 0)


def in_order(blocks):
    found = dict(zip(ORDER, blocks))
    return [found[i] for i in range(RING)]


def after(value, *others):
    return lax.optimization_barrier((value,) + others)[0]


def vmem_call(body, out_shapes, flops, scalars, *arrays, steps=1):
    specs, operands = [], []
    for item in arrays:
        array, column = item if isinstance(item, tuple) else (item, None)
        block = array.shape if column is None else (array.shape[0], WIDTH)
        place = (0,) * array.ndim if column is None else (0, column)
        specs.append(pl.BlockSpec(block, lambda i, place=place: place))
        operands.append(array)
    return pl.pallas_call(
        body,
        grid=(steps,),
        out_shape=out_shapes,
        in_specs=[pl.BlockSpec(memory_space=pltpu.SMEM)] * len(scalars) + specs,
        out_specs=pl.BlockSpec(
            (out_shapes.shape[0], out_shapes.shape[1] // steps), lambda i: (0, steps - 1 - i)
        )
        if steps > 1
        else jax.tree.map(
            lambda shape: pl.BlockSpec(shape.shape, lambda i, n=len(shape.shape): (0,) * n),
            out_shapes,
        ),
        compiler_params=pltpu.CompilerParams(vmem_limit_bytes=56 * 1024 * 1024),
        cost_estimate=pl.CostEstimate(flops=flops, bytes_accessed=4_000_000, transcendentals=0),
    )(*scalars, *operands)


def like(shape, dtype):
    return jax.ShapeDtypeStruct(shape, dtype)


def mm(left, right):
    return lax.dot_general(left, right, (((1,), (0,)), ((), ())), preferred_element_type=F32)


def mm_nt(left, right):
    return lax.dot_general(left, right, (((1,), (1,)), ((), ())), preferred_element_type=F32)


def mm_exact(left, right):
    return lax.dot_general(
        left,
        right,
        (((1,), (1,)), ((), ())),
        precision=lax.Precision.HIGHEST,
        preferred_element_type=F32,
    )


def mm_tn(left, right):
    return lax.dot_general(left, right, (((0,), (0,)), ((), ())), preferred_element_type=F32)


def bias_rows(bias, weight, row):
    row = row + jnp.sum(bias * weight, axis=0, keepdims=True)
    high = row.astype(BF)
    low = (row - high.astype(F32)).astype(BF)
    return jnp.concatenate(
        [high, low, jnp.zeros((PACK - OWN_ROWS - 2, row.shape[1]), BF)], axis=0
    )


def as_column(row):
    size = row.shape[1]
    at = lax.broadcasted_iota(jnp.int32, (size, size), 0)
    lane = lax.broadcasted_iota(jnp.int32, (size, size), 1)
    return jnp.sum(jnp.where(at == lane, row, 0.0), axis=1, keepdims=True)


def spread(piece, place):
    size = piece.shape[1]
    whole = jnp.concatenate([piece] * (RING * RING), axis=1)
    lane = lax.broadcasted_iota(jnp.int32, whole.shape, 1)
    return jnp.where((lane >= place * size) & (lane < (place + 1) * size), whole, 0.0)


def pack_body(
    first_ref, place_ref, gain1, bias1, gain2, bias2, w_qkv, b_qkv, w_up, b_up, w_down, b_out, b_down,
    own_ref, sent_ref, down_ref
):
    first = first_ref[0] == 1
    place = place_ref[0]
    weight = w_qkv[...].astype(F32)
    scaled = (weight * as_column(gain1[...].astype(F32))).astype(BF)
    three = spread(b_qkv[...].astype(F32), place)
    row = jnp.concatenate([three[i : i + 1] for i in range(3)], axis=1)
    extra = bias_rows(as_column(bias1[...].astype(F32)), weight, row)
    whole = jnp.concatenate([scaled, extra], axis=0)
    spare = jnp.zeros((PACK, LANES - SPOT), BF)
    for t in range(RING):
        for i in range(3):
            at = i * WIDTH + t * SPOT
            part = jnp.concatenate([whole[:, at : at + SPOT], spare], axis=1)
            own_ref[t, :, i * LANES : (i + 1) * LANES] = part
            sent_ref[t, :, i * LANES : (i + 1) * LANES] = part
    weight = w_up[...].astype(F32)
    scaled = (weight * as_column(gain2[...].astype(F32))).astype(BF)
    extra = bias_rows(
        as_column(bias2[...].astype(F32)), weight, spread(b_up[...].astype(F32), place)
    )
    whole = jnp.concatenate([scaled, extra], axis=0)
    for t in range(RING):
        by_a = whole[:, t * WIDTH : (t + 1) * WIDTH]
        by_b = jnp.concatenate(
            [whole[:, a * WIDTH + t * SPOT : a * WIDTH + (t + 1) * SPOT] for a in range(RING)],
            axis=1,
        )
        own_ref[t, :, WIDTH:] = jnp.where(first, by_a, by_b)
        sent_ref[t, :, WIDTH:] = jnp.where(first, by_b, by_a)
    down_ref[:SPOT] = w_down[...]
    rows = [spread(b[...].astype(F32), place).astype(BF) for b in (b_out, b_down)]
    rows.append(jnp.zeros((PACK - OWN_ROWS - 2, WIDTH), BF))
    down_ref[SPOT:] = jnp.concatenate(rows, axis=0)


def out_rows(rows):
    parts = [rows[j * LANES : j * LANES + OWN_ROWS, :] for j in range(RING)]
    return jnp.concatenate(parts + [jnp.zeros((LANES - SPOT, WIDTH), BF)], axis=0)


def down_rows(rows):
    parts = [rows[j * LANES + OWN_ROWS : j * LANES + OWN_ROWS + SPOT, :] for j in range(RING)]
    return jnp.concatenate(parts, axis=0)


def out_bias_row(rows):
    total = jnp.zeros((1, WIDTH), F32)
    for j in range(RING):
        extra = rows[j * LANES + OWN_ROWS + SPOT : (j + 1) * LANES, :].astype(F32)
        total = total + extra[0:1, :] + extra[1:2, :]
    return total


def rotate(value, cos, sin):
    cos = jnp.concatenate([cos, cos], axis=1)
    sin = jnp.concatenate([sin, sin], axis=1)
    lanes = value.shape[1]
    lane = lax.broadcasted_iota(jnp.int32, value.shape, 1)
    other = jnp.where(
        (lane & (HEAD_DIM - 1)) < 8,
        -pltpu.roll(value, lanes - 8, 1),
        pltpu.roll(value, 8, 1),
    )
    return value * cos + other * sin


def places(feature):
    row = lax.broadcasted_iota(jnp.int32, (WIDTH, feature.shape[1]), 0)
    return jnp.where(row == feature[0:1, :], 1.0, 0.0).astype(BF)


def project_turned_body(at_ref, x0, x1, x2, x3, feature, ones, w0, w1, w2, w3, cos, sin,
                        x_ref, q_ref, kv_ref, w_ref):
    for e, block in enumerate((w0, w1, w2, w3)):
        at = pl.multiple_of(lax.rem(at_ref[0] + e, RING) * LANES, LANES)
        w_ref[pl.ds(at, LANES), :] = block[...]
    project_body(x0, x1, x2, x3, feature, ones, w_ref, cos, sin, x_ref, q_ref, kv_ref)


def project_body(x0, x1, x2, x3, feature, ones, w, cos, sin, x_ref, q_ref, kv_ref):
    x = jnp.concatenate([x0[...], x1[...], x2[...], x3[...]], axis=0)
    x_all = (mm(x, places(feature)) + ones[...]).astype(BF)
    x_ref[...] = x_all
    qkv = mm(x_all, w[...])
    tables = cos[...], sin[...]
    q_ref[...] = (rotate(qkv[:, :LANES], *tables) * 0.125).astype(BF)
    kv_ref[:, :LANES] = rotate(qkv[:, LANES : 2 * LANES], *tables).astype(BF)
    kv_ref[:, LANES:] = qkv[:, 2 * LANES :].astype(BF)


def store_parts(partial, outs):
    block = partial.shape[0] // len(outs)
    for i, out in enumerate(outs):
        out[...] = partial[i * block : (i + 1) * block].astype(out.dtype)


def mlp_body(x_ref, w_up, rows, *refs):
    given = 0 if len(refs) == 3 else 1
    mids, (hidden_ref, slope_ref), outs = refs[:given], refs[given : given + 2], refs[given + 2 :]
    up_proj = mm(x_ref[...], w_up[...])
    cdf = 0.5 * (1.0 + lax.erf(up_proj * 0.7071067811865476))
    hidden = (up_proj * cdf).astype(BF)
    hidden_ref[...] = hidden
    density = jnp.exp(-0.5 * up_proj * up_proj) * 0.3989422804014327
    slope_ref[...] = (cdf + up_proj * density).astype(BF)
    partial = mm(hidden, down_rows(rows)) + out_bias_row(rows)
    for mid in mids:
        partial = partial + mm(mid[...], out_rows(rows))
    store_parts(partial, outs)


def head_mask(value, head):
    lane = lax.broadcasted_iota(jnp.int32, value.shape, 1)
    return jnp.where((lane >= head * HEAD_DIM) & (lane < (head + 1) * HEAD_DIM), value, 0)


def allowed_pairs(starts_ref, info, e, rows):
    part = rows // RING
    pieces = []
    for d in range(RING):
        base = lax.broadcasted_iota(jnp.int32, (part, rows), 0) + starts_ref[e * RING + d]
        pieces.append(jnp.where((base >= info[0:1, :]) & (base <= info[1:2, :]), 0.0, NEG_FILL))
    return jnp.concatenate(pieces, axis=0)


def attend_body(starts_ref, info_ref, q_ref, kv0, kv1, kv2, kv3, *refs):
    given = 0 if len(refs) == 2 else 2
    others, (mid_ref, lse_ref), outs = refs[:given], refs[given : given + 2], refs[given + 2 :]
    rows = q_ref.shape[0]
    info = info_ref[...]
    q = q_ref[...]
    masked_q = [head_mask(q, h) for h in range(3)]
    tops, sums, accs = [None] * 3, [None] * 3, [None] * 3
    for e, kv in enumerate((kv0, kv1, kv2, kv3)):
        bias = allowed_pairs(starts_ref, info, e, rows)
        keys = kv[:, :LANES]
        values_t = kv[:, LANES:].T
        for h in range(3):
            scores = mm_nt(keys, masked_q[h]) + bias
            top = jnp.max(scores, axis=0, keepdims=True)
            if e:
                top = jnp.maximum(tops[h], top)
            probs = jnp.exp(scores - top)
            total = jnp.sum(probs, axis=0, keepdims=True)
            part = mm(values_t[h * HEAD_DIM : (h + 1) * HEAD_DIM, :], probs.astype(BF))
            if e:
                shrink = jnp.exp(tops[h] - top)
                total = total + sums[h] * shrink
                part = part + accs[h] * shrink
            tops[h], sums[h], accs[h] = top, total, part
    mids = [accs[h] / sums[h] for h in range(3)] + [jnp.zeros((HEAD_DIM, rows), F32)]
    mid = jnp.concatenate(mids, axis=0).T.astype(BF)
    mid_ref[...] = mid
    for h in range(3):
        lse_ref[h : h + 1, :] = tops[h] + jnp.log(sums[h])
    lse_ref[3:, :] = jnp.zeros((5, rows), F32)
    if others:
        rows_ref, mlp_ref = others
        store_parts(mm(mid, out_rows(rows_ref)) + mlp_ref[...], outs)


def attend_back_body(
    starts_ref, info_ref, q_ref, a0, a1, a2, a3, rows_ref, mid_ref, lse_ref, cos, sin,
    kv0, kv1, kv2, kv3, dq_ref, g0, g1, g2, g3
):
    rows = q_ref.shape[0]
    info = info_ref[...]
    q = q_ref[...]
    g_all = jnp.concatenate([a0[...], a1[...], a2[...], a3[...]], axis=0)
    do = mm_nt(g_all, out_rows(rows_ref)).astype(BF)
    lse = lse_ref[...]
    lane = lax.broadcasted_iota(jnp.int32, (8, LANES), 1)
    head = lax.broadcasted_iota(jnp.int32, (8, LANES), 0)
    pick = jnp.where(lane // HEAD_DIM == head, 1.0, 0.0)
    products = do.astype(F32) * mid_ref[...].astype(F32)
    delta = lax.dot_general(
        pick,
        products,
        (((1,), (1,)), ((), ())),
        precision=lax.Precision.HIGHEST,
        preferred_element_type=F32,
    )
    masked_q = [head_mask(q, h) for h in range(3)]
    masked_do = [head_mask(do, h) for h in range(3)]
    dq = [None] * 3
    for e, (kv, grad) in enumerate(zip((kv0, kv1, kv2, kv3), (g0, g1, g2, g3))):
        bias = allowed_pairs(starts_ref, info, e, rows)
        keys = kv[:, :LANES]
        keys_t = keys.T
        values = kv[:, LANES:]
        dk = jnp.zeros((rows, LANES), F32)
        dv = jnp.zeros((rows, LANES), F32)
        for h in range(3):
            scores = mm_nt(keys, masked_q[h]) + bias
            probs = jnp.exp(scores - lse[h : h + 1, :])
            dprobs = mm_nt(values, masked_do[h])
            dscores = (probs * (dprobs - delta[h : h + 1, :])).astype(BF)
            dv = dv + mm(probs.astype(BF), masked_do[h])
            dk = dk + mm(dscores, masked_q[h])
            part = mm(keys_t[h * HEAD_DIM : (h + 1) * HEAD_DIM, :], dscores)
            dq[h] = part if e == 0 else dq[h] + part
        grad[:, :LANES] = dk.astype(BF)
        grad[:, LANES:] = dv.astype(BF)
    dq_all = jnp.concatenate(dq + [jnp.zeros((HEAD_DIM, rows), F32)], axis=0).T * 0.125
    dq_ref[...] = rotate(dq_all, cos[...], -sin[...]).astype(BF)


def mlp_back_body(a0, a1, a2, a3, slope, w_up, rows, grad_ref, dx_ref):
    g_all = jnp.concatenate([a0[...], a1[...], a2[...], a3[...]], axis=0)
    grad_up = (mm_nt(g_all, down_rows(rows)) * slope[...].astype(F32)).astype(BF)
    grad_ref[...] = grad_up
    dx_ref[...] = mm_nt(grad_up, w_up[...])


def weight_grads_body(a0, a1, a2, a3, hidden, mid, x_ref, grad_qkv, grad_up, out_ref):
    step = pl.program_id(0)

    @pl.when(step == 0)
    def rows_part():
        g_all = jnp.concatenate([a0[...], a1[...], a2[...], a3[...]], axis=0)
        down_grad = mm_tn(hidden[...], g_all).astype(BF)
        out_grad = mm_tn(mid[...], g_all).astype(BF)
        sums = jnp.sum(g_all.astype(F32), axis=0, keepdims=True)
        sums = jnp.broadcast_to(sums, (PACK - OWN_ROWS, WIDTH)).astype(BF)
        for j in range(RING):
            at = j * LANES
            out_ref[at : at + OWN_ROWS, :] = out_grad[j * OWN_ROWS : (j + 1) * OWN_ROWS]
            out_ref[at + OWN_ROWS : at + OWN_ROWS + SPOT, :] = down_grad[j * SPOT : (j + 1) * SPOT]
            out_ref[at + OWN_ROWS + SPOT : at + LANES, :] = sums

    @pl.when(step == 1)
    def up_part():
        out_ref[...] = mm_tn(x_ref[...], grad_up[...]).astype(BF)

    @pl.when(step == 2)
    def qkv_part():
        out_ref[...] = mm_tn(x_ref[...], grad_qkv[...]).astype(BF)


def qkv_back_body(
    dq, g0, g1, g2, g3, cos, sin, w_qkv, dx_up, feature, grad_ref, d0, d1, d2, d3
):
    dkv = g0[...].astype(F32)
    for part in (g1, g2, g3):
        dkv = dkv + part[...].astype(F32)
    dk = rotate(dkv[:, :LANES], cos[...], -sin[...])
    grad = jnp.concatenate([dq[...], dk.astype(BF), dkv[:, LANES:].astype(BF)], axis=1)
    grad_ref[...] = grad
    dx = (mm_nt(grad, w_qkv[...]) + dx_up[...]).astype(BF)
    store_parts(mm_nt(dx, places(feature)), (d0, d1, d2, d3))


def own_piece(row, place):
    size = row.shape[1] // (RING * RING)
    return sum(
        jnp.where(place == f, row[:, f * size : (f + 1) * size], 0.0) for f in range(RING * RING)
    )


def finish_body(
    place_ref, l0, l1, r0, r1, gain1, bias1, gain2, bias2, w_qkv, w_up,
    gain1_ref, bias1_ref, gain2_ref, bias2_ref, qkv_ref, b_qkv_ref, out_ref, b_out_ref, up_ref, b_up_ref, down_ref
):
    place = place_ref[0]

    def total(low, high):
        return jnp.concatenate(
            [
                one[:, low:high].astype(F32) + two[:, low:high].astype(F32)
                for one, two in ((l0, r0), (l1, r1))
            ],
            axis=0,
        )

    m = total(0, WIDTH)
    m_qkv = jnp.concatenate(
        [
            m[t * PACK : (t + 1) * PACK, i * LANES : i * LANES + SPOT]
            for i in range(3)
            for t in range(RING)
        ],
        axis=1,
    )
    m = total(WIDTH, 2 * WIDTH)
    m_up = jnp.concatenate([m[t * PACK : (t + 1) * PACK] for t in range(RING)], axis=1)
    rows = total(2 * WIDTH, 3 * WIDTH)
    out_ref[...] = rows[:OWN_ROWS]
    down_ref[...] = rows[OWN_ROWS : OWN_ROWS + SPOT]
    b_out_ref[...] = own_piece(rows[OWN_ROWS + SPOT : OWN_ROWS + SPOT + 1], place)
    for m, w_ref, gain, bias, gain_ref, bias_ref, grad_ref in (
        (m_qkv, w_qkv, gain1, bias1, gain1_ref, bias1_ref, qkv_ref),
        (m_up, w_up, gain2, bias2, gain2_ref, bias2_ref, up_ref),
    ):
        ends = m[OWN_ROWS : OWN_ROWS + 1]
        m = m[:OWN_ROWS]
        weight = w_ref[...].astype(F32)
        all_ones = jnp.ones((8, m.shape[1]), F32)
        gain_ref[...] = mm_exact(all_ones, weight * m)[0:1]
        bias_ref[...] = mm_exact(all_ones, weight * ends)[0:1]
        grad_ref[...] = as_column(gain[...].astype(F32)) * m + as_column(bias[...].astype(F32)) * ends
    ends = m_qkv[OWN_ROWS : OWN_ROWS + 1]
    b_qkv_ref[...] = jnp.concatenate(
        [own_piece(ends[:, i * WIDTH : (i + 1) * WIDTH], place) for i in range(3)], axis=0
    )
    b_up_ref[...] = own_piece(m_up[OWN_ROWS : OWN_ROWS + 1], place)


def unit_rows_of(rows):
    centered = rows - jnp.mean(rows, axis=-1, keepdims=True)
    inv_std = lax.rsqrt(jnp.mean(centered * centered, axis=-1, keepdims=True) + EPSILON)
    return centered * inv_std, inv_std


def forward_layer(tok_rows, xs, weights, geometry, order, mlp_first):
    w_qkv, w_up, w_rows = weights
    starts, info, tables = geometry
    own = tok_rows.shape[0]
    rows = RING * own
    outs = (like((rows, RING * LANES), BF), like((rows, LANES), BF), like((rows, 2 * LANES), BF))
    if isinstance(w_qkv, list):
        at, *blocks = w_qkv
        x_all, q, kv, w_qkv = vmem_call(
            project_turned_body,
            outs + (like((RING * LANES, WIDTH), BF),),
            1_600_000_000,
            (at,),
            *xs,
            *order,
            *blocks,
            *tables,
        )
    else:
        x_all, q, kv = vmem_call(
            project_body, outs, 1_600_000_000, (), *xs, *order, w_qkv, *tables
        )
    kvs = in_order([kv] + [send(kv, along_tokens(-by)) for by in (1, 3, 2)])
    whole = (like((rows, WIDTH), F32),)
    cut = (like((own, WIDTH), F32),) + (like((own, WIDTH), BF),) * (RING - 1)

    def mlp(attended, outs):
        return vmem_call(
            mlp_body,
            (like((rows, WIDTH), BF), like((rows, WIDTH), BF)) + outs,
            2_000_000_000,
            (),
            x_all,
            w_up,
            w_rows,
            *attended,
        )

    def attention(others, outs):
        return vmem_call(
            attend_body,
            (like((rows, LANES), BF), like((8, rows), F32)) + outs,
            6_000_000_000,
            (starts,),
            info,
            q,
            *kvs,
            *others,
        )

    if mlp_first:
        hidden, slope, partial = mlp((), whole)
        mid, lse, *parts = attention((w_rows, partial), cut)
    else:
        mid, lse = attention((), ())
        hidden, slope, *parts = mlp((mid,), cut)
    total = tok_rows + parts[0]
    for by in (1, 3, 2):
        total = total + send(parts[by], along_weights(by)).astype(F32)
    return total, (x_all, q, kvs, hidden, slope, mid, lse), w_qkv


def backward_layer(
    grad_rows, gs, unit, inv_std, weights, stored, geometry, order, tie, late
):
    w_qkv, w_up, w_rows = weights
    starts, info, tables = geometry
    x_all, q, kvs, hidden, slope, mid, lse = stored
    own = grad_rows.shape[0]
    rows = RING * own

    def attention_back(gs):
        return vmem_call(
            attend_back_body,
            (like((rows, LANES), BF),) + (like((rows, 2 * LANES), BF),) * RING,
            16_000_000_000,
            (starts,),
            info,
            q,
            *gs,
            w_rows,
            mid,
            lse,
            *tables,
            *kvs,
        )

    dq, *dkvs = attention_back(gs)
    received = [send(dkvs[by], along_tokens(by)) for by in (1, 3, 2)]
    grad_up, dx_up = vmem_call(
        mlp_back_body,
        (like((rows, WIDTH), BF), like((rows, RING * LANES), F32)),
        1_600_000_000,
        (),
        *([after(gs[0], *tie)] + gs[1:]),
        slope,
        w_up,
        w_rows,
    )
    grad_qkv, *dxs = vmem_call(
        qkv_back_body,
        (like((rows, WIDTH), BF),) + (like((own, WIDTH), BF),) * RING,
        2_000_000_000,
        (),
        dq,
        dkvs[0],
        *received,
        *tables,
        w_qkv,
        dx_up,
        order[0],
    )
    total = dxs[0].astype(F32)
    for by in (1, 3, 2):
        total = total + send(dxs[by], along_weights(by)).astype(F32)
    grad_in = grad_rows.astype(F32) + inv_std * (
        total
        - jnp.mean(total, axis=-1, keepdims=True)
        - unit * jnp.mean(total * unit, axis=-1, keepdims=True)
    )
    grad_in = grad_in.astype(BF)
    cuts = vmem_call(
        weight_grads_body,
        like((RING * LANES, 3 * WIDTH), BF),
        3_000_000_000,
        (),
        *gs,
        hidden,
        mid,
        x_all,
        after(grad_qkv, *((grad_in,) if late else ())),
        grad_up,
        steps=3,
    )
    return grad_in, scatter_tokens_axis(cuts), cuts


def over_weights(total, tp):
    parts = [total[:PACK]] + [
        send(total[by * PACK : (by + 1) * PACK], along_weights(by)) for by in (1, 3, 2)
    ]
    near = in_order(parts)
    return turned([near[0], near[3], near[2], near[1]], tp)


def to_core(value, core):
    return send(value, moves(lambda s, a, b: flat(core, a, b) if s != core else None))


def over_replicas(low):
    rest = lax.axis_size("replica")

    def swapped(value, partner):
        return lax.ppermute(value, "replica", [(i, partner(i)) for i in range(rest)])

    def inner(i):
        return i ^ 1

    def outer(i):
        return rest - 1 - i

    half = low.shape[0] // 2
    left, right = low[:half], low[half:]
    left = (left.astype(F32) + swapped(left, inner).astype(F32)).astype(BF)
    right = (right.astype(F32) + swapped(right, outer).astype(F32)).astype(BF)
    return left, right, swapped(left, outer), swapped(right, inner)


def on_device(
    pipe_ends,
    seq_lengths,
    norm1_gain,
    norm1_bias,
    norm2_gain,
    norm2_bias,
    qkv_weight,
    qkv_bias,
    out_weight,
    out_bias,
    up_weight,
    up_bias,
    down_weight,
    down_bias,
):
    core = lax.axis_index("section")
    first = core == 0
    place = lax.axis_index("fsdp")
    a_at, b_at = place // RING, place % RING
    tp = jnp.where(first, a_at, b_at)
    sq = jnp.where(first, b_at, a_at)
    rows_dev = pipe_ends.shape[3]

    def block_of(weight_at, token_at):
        weight_at, token_at = weight_at % RING, token_at % RING
        return jnp.where(first, RING * weight_at + token_at, RING * token_at + weight_at)

    ring = jnp.arange(RING, dtype=jnp.int32)
    dest = block_of(tp + ring[None, :], sq + ring[:, None]).reshape(-1).astype(jnp.int32)
    kept = block_of(tp + ring[None, :], ring[:, None]).reshape(-1).astype(jnp.int32)
    spare = jnp.arange(PACK, dtype=jnp.int32)[None, :]
    feature = jnp.where(spare < OWN_ROWS, kept[:, None] * OWN_ROWS + spare, -1).reshape(1, -1)
    ones = np.tile((np.arange(PACK) // 2 == OWN_ROWS // 2).astype(np.float32), RING * RING)
    order = (jnp.broadcast_to(feature, (8, RING * LANES)), ones[None, :])

    flags = (first.astype(jnp.int32)[None], place.astype(jnp.int32)[None])
    pack = like((RING, PACK, 2 * WIDTH), BF)
    own_pack, sent_pack, pack_down = vmem_call(
        pack_body,
        (pack, pack, like((SPOT + PACK - OWN_ROWS, WIDTH), BF)),
        1_000_000,
        flags,
        norm1_gain,
        norm1_bias,
        norm2_gain,
        norm2_bias,
        qkv_weight[0],
        qkv_bias[0],
        up_weight[0],
        up_bias,
        down_weight[0],
        out_bias,
        down_bias,
    )
    swap = moves(lambda s, a, b: flat(1 - s, a, b))

    def both(own, other):
        return jnp.where(first, own, other), jnp.where(first, other, own)

    early_pack, late_pack = both(own_pack, send(sent_pack, swap))
    other_ends = send(
        jnp.where(first, pipe_ends[0, 1, 0], pipe_ends[0, 0, 0]), swap
    )
    own_end = jnp.where(first, pipe_ends[0, 0, 0], pipe_ends[0, 1, 0])
    tokens_in = jnp.where(first, own_end, other_ends)
    cotangent = jnp.where(first, other_ends, own_end)

    lens = lax.dynamic_index_in_dim(seq_lengths[:, 0], core, 0, keepdims=False)
    starts = (dest * rows_dev).astype(jnp.int32)
    rows_at = (starts[:RING, None] + jnp.arange(rows_dev, dtype=jnp.int32)[None, :]).reshape(-1)
    finish = jnp.cumsum(lens)
    begin = jnp.sum(
        jnp.where(rows_at[None, :] >= finish[:, None], lens[:, None], 0), axis=0
    ).astype(jnp.int32)
    info = jnp.concatenate(
        [begin[None, :], rows_at[None, :], jnp.zeros((6, rows_at.shape[0]), jnp.int32)], axis=0
    )
    in_head = np.arange(2 * HEAD_DIM) % HEAD_DIM
    inv_freq = (10000.0 ** (-(in_head % 8) / 8.0)).astype(np.float32)
    inv_freq = np.where(in_head < 16, inv_freq, np.float32(0))
    angles = (rows_at - begin).astype(F32)[:, None] * inv_freq[None, :]
    tables = (jnp.cos(angles), jnp.sin(angles))
    geometry = (starts, info, tables)

    def to_columns(pack):
        def block_for(by):
            return lax.dynamic_index_in_dim(pack, (tp + by) % RING, 0, keepdims=False)

        parts = [block_for(0)] + [
            send(block_for(-by), along_weights(-by)) for by in (1, 3, 2)
        ]
        return jnp.concatenate(in_order(parts), axis=0)

    down_layers = both(pack_down, send(pack_down, swap))
    turn = moves(lambda s, a, b: flat(1, b, a) if s == 0 else flat(0, a, b))
    stay = moves(lambda s, a, b: None if s == 0 else flat(s, b, a))
    out_other = send(out_weight[0], turn)
    out_turned = send(out_weight[0], stay)
    out_layers = jnp.where(first, out_weight[0], out_other), jnp.where(first, out_other, out_turned)
    row_packs = [jnp.concatenate([out_layers[i], down_layers[i]], axis=0) for i in range(2)]

    unit0, inv_std0 = unit_rows_of(tokens_in.astype(F32))
    xs0 = in_order(gathered_weights_axis(unit0.astype(BF)))
    columns = to_columns(jnp.concatenate([early_pack, late_pack], axis=2))
    columns = after(columns, *xs0, info, *tables)
    qkv0 = columns[:, :WIDTH]
    qkv0 = in_order([qkv0] + [send(qkv0, along_tokens(-by)) for by in (1, 3, 2)])
    qkv0 = [sq.astype(jnp.int32)[None]] + qkv0
    mlp0 = gather_tokens_axis(
        jnp.concatenate([columns[:, WIDTH : 2 * WIDTH], row_packs[0]], axis=1)
    )
    weights0 = (qkv0, (mlp0, 0), (mlp0, 1))

    out0, stored0, qkv0 = forward_layer(
        tokens_in.astype(F32), xs0, weights0, geometry, order, False
    )
    weights0 = (qkv0, (mlp0, 0), (mlp0, 1))
    gs1 = in_order(gathered_weights_axis(after(cotangent, stored0[1])))
    later = jnp.concatenate([columns[:, 2 * WIDTH :], row_packs[1]], axis=1)
    all1 = gather_tokens_axis(after(later, *stored0[2]))
    weights1 = ((all1, 0), (all1, 1), (all1, 2))
    low0 = out0.astype(BF)
    unit1, inv_std1 = unit_rows_of(low0.astype(F32))
    xs1 = in_order(gathered_weights_axis(unit1.astype(BF)))
    out1, stored1, unused = forward_layer(
        low0.astype(F32), xs1, weights1, geometry, order, True
    )
    low1 = out1.astype(BF)

    def up_swapped(value):
        value = value.reshape(RING, PACK, RING, SPOT)
        return value.transpose(2, 1, 0, 3).reshape(RING * PACK, WIDTH)

    def rows_turned(rows):
        out_part = jnp.where(first, rows[:OWN_ROWS], send(rows[:OWN_ROWS], stay))
        return jnp.concatenate([out_part, rows[OWN_ROWS:]], axis=0)

    def joined(part, layer):
        return (part.astype(F32) + to_core(part, layer).astype(F32)).astype(BF)

    def joined_up(part, layer):
        return joined(jnp.where(first, part, up_swapped(part)), layer)

    grad1, scattered1, unused = backward_layer(
        cotangent,
        gs1,
        unit1,
        inv_std1,
        weights1,
        stored1,
        geometry,
        order,
        (low1,),
        True,
    )
    gs0 = in_order(gathered_weights_axis(grad1))

    def swapped_rows(early, late):
        other = send(jnp.where(first, late, early), swap)
        mine = jnp.where(first, early, late)
        stacked = jnp.stack([jnp.where(first, mine, other), jnp.where(first, other, mine)])
        return stacked[None, :, None], other

    layer_out, out_other = swapped_rows(low0, low1)

    def to_owner(scattered, columns, layer):
        return jnp.concatenate(
            [
                joined(columns[:, :WIDTH], layer),
                joined_up(columns[:, WIDTH:], layer),
                joined(rows_turned(scattered[:, 2 * WIDTH :]), layer),
            ],
            axis=1,
        )

    grad0, scattered0, cuts0 = backward_layer(
        grad1,
        gs0,
        unit0,
        inv_std0,
        weights0,
        stored0,
        geometry,
        order,
        (out_other,),
        False,
    )
    scattered1 = after(scattered1, cuts0, grad0)
    columns1 = over_weights(scattered1[:, : 2 * WIDTH], tp)
    owned1 = to_owner(scattered1, columns1, 1)
    input_grad, grad_other = swapped_rows(grad0, grad1)
    scattered0 = after(scattered0, owned1, grad_other)
    columns0 = over_weights(scattered0[:, : 2 * WIDTH], tp)
    parts = over_replicas(jnp.where(first, to_owner(scattered0, columns0, 0), owned1))

    vector = like((1, OWN_ROWS), F32)
    gain1_grad, bias1_grad, gain2_grad, bias2_grad, *grads = vmem_call(
        finish_body,
        (
            vector,
            vector,
            vector,
            vector,
            like((OWN_ROWS, 3 * WIDTH), F32),
            like((3, OWN_ROWS), F32),
            like((OWN_ROWS, WIDTH), F32),
            vector,
            like((OWN_ROWS, RING * WIDTH), F32),
            like((1, SPOT), F32),
            like((SPOT, WIDTH), F32),
        ),
        10_000_000,
        flags[1:],
        *parts,
        norm1_gain,
        norm1_bias,
        norm2_gain,
        norm2_bias,
        qkv_weight[0],
        up_weight[0],
    )
    qkv_grad, qkv_bias_grad, out_grad, end_grad, up_grad, up_bias_grad, down_grad = grads
    return (
        layer_out,
        input_grad,
        gain1_grad,
        bias1_grad,
        gain2_grad,
        bias2_grad,
        qkv_grad[None],
        qkv_bias_grad[None],
        out_grad[None],
        end_grad,
        up_grad[None],
        up_bias_grad,
        down_grad[None],
        end_grad,
    )


def solution(mesh):
    tokens = P("section", None, "replica", "fsdp", None)
    vector = P("section", "fsdp")
    matrix = P("section", "fsdp", None)
    three = P("section", None, "fsdp")
    params = (
        vector,
        vector,
        vector,
        vector,
        matrix,
        three,
        matrix,
        vector,
        matrix,
        vector,
        matrix,
        vector,
    )
    return jax.shard_map(
        on_device,
        mesh=mesh,
        in_specs=(tokens, P(None, "replica", None)) + params,
        out_specs=(tokens, tokens) + params,
        check_vma=False,
    )
```

```python
import jax
import jax.numpy as jnp
import numpy as np
from jax import lax
from jax.experimental import pallas as pl
from jax.experimental.pallas import tpu as pltpu
from jax.sharding import PartitionSpec as P

HEADS = 12
HEAD_DIM = 64
EPSILON = 1e-05
NEG_FILL = -1e30
WIDTH = 768
RING = 4
OWN_ROWS = 48
PACK = 64
LANES = 256
SPOT = 192
BF = jnp.bfloat16
F32 = jnp.float32
CORES = ("section", "fsdp")


def flat(core, a, b):
    return core * RING * RING + (a % RING) * RING + b % RING


def moves(step):
    return [
        (flat(core, a, b), step(core, a, b))
        for core in range(2)
        for a in range(RING)
        for b in range(RING)
        if step(core, a, b) is not None
    ]


def along_weights(by):
    return moves(lambda core, a, b: flat(core, a + by, b) if core == 0 else flat(core, a, b + by))


def along_tokens(by):
    return moves(lambda core, a, b: flat(core, a, b + by) if core == 0 else flat(core, a + by, b))


def token_groups():
    return [[flat(0, a, b) for b in range(RING)] for a in range(RING)] + [
        [flat(1, a, b) for a in range(RING)] for b in range(RING)
    ]


def send(value, pairs):
    return lax.ppermute(value, CORES, pairs)


def gather_tokens_axis(block):
    return lax.all_gather(block, CORES, axis=0, tiled=True, axis_index_groups=token_groups())


def scatter_tokens_axis(total):
    return lax.psum_scatter(
        total, CORES, scatter_dimension=0, tiled=True, axis_index_groups=token_groups()
    )


def gathered_weights_axis(block):
    return [block] + [send(block, along_weights(-by)) for by in (1, 3, 2)]


ORDER = (0, 1, 3, 2)


def turned(blocks, by):
    rows = blocks[0].shape[0]
    twice = jnp.concatenate(list(blocks) + list(blocks), axis=0)
    return lax.dynamic_slice_in_dim(twice, ((RING - by) % RING) * rows, RING * rows, 0)


def in_order(blocks):
    found = dict(zip(ORDER, blocks))
    return [found[i] for i in range(RING)]


def after(value, *others):
    return lax.optimization_barrier((value,) + others)[0]


def vmem_call(body, out_shapes, flops, scalars, *arrays, steps=1):
    specs, operands = [], []
    for item in arrays:
        array, column = item if isinstance(item, tuple) else (item, None)
        block = array.shape if column is None else (array.shape[0], WIDTH)
        place = (0,) * array.ndim if column is None else (0, column)
        specs.append(pl.BlockSpec(block, lambda i, place=place: place))
        operands.append(array)
    return pl.pallas_call(
        body,
        grid=(steps,),
        out_shape=out_shapes,
        in_specs=[pl.BlockSpec(memory_space=pltpu.SMEM)] * len(scalars) + specs,
        out_specs=pl.BlockSpec(
            (out_shapes.shape[0], out_shapes.shape[1] // steps), lambda i: (0, steps - 1 - i)
        )
        if steps > 1
        else jax.tree.map(
            lambda shape: pl.BlockSpec(shape.shape, lambda i, n=len(shape.shape): (0,) * n),
            out_shapes,
        ),
        compiler_params=pltpu.CompilerParams(vmem_limit_bytes=56 * 1024 * 1024),
        cost_estimate=pl.CostEstimate(flops=flops, bytes_accessed=4_000_000, transcendentals=0),
    )(*scalars, *operands)


def like(shape, dtype):
    return jax.ShapeDtypeStruct(shape, dtype)


def mm(left, right):
    return lax.dot_general(left, right, (((1,), (0,)), ((), ())), preferred_element_type=F32)


def mm_nt(left, right):
    return lax.dot_general(left, right, (((1,), (1,)), ((), ())), preferred_element_type=F32)


def mm_exact(left, right):
    return lax.dot_general(
        left,
        right,
        (((1,), (1,)), ((), ())),
        precision=lax.Precision.HIGHEST,
        preferred_element_type=F32,
    )


def mm_tn(left, right):
    return lax.dot_general(left, right, (((0,), (0,)), ((), ())), preferred_element_type=F32)


def bias_rows(bias, weight, row):
    row = row + jnp.sum(bias * weight, axis=0, keepdims=True)
    high = row.astype(BF)
    low = (row - high.astype(F32)).astype(BF)
    return jnp.concatenate(
        [high, low, jnp.zeros((PACK - OWN_ROWS - 2, row.shape[1]), BF)], axis=0
    )


def as_column(row):
    size = row.shape[1]
    at = lax.broadcasted_iota(jnp.int32, (size, size), 0)
    lane = lax.broadcasted_iota(jnp.int32, (size, size), 1)
    return jnp.sum(jnp.where(at == lane, row, 0.0), axis=1, keepdims=True)


def spread(piece, place):
    size = piece.shape[1]
    whole = jnp.concatenate([piece] * (RING * RING), axis=1)
    lane = lax.broadcasted_iota(jnp.int32, whole.shape, 1)
    return jnp.where((lane >= place * size) & (lane < (place + 1) * size), whole, 0.0)


def pack_body(
    first_ref, place_ref, gain1, bias1, gain2, bias2, w_qkv, b_qkv, w_up, b_up, w_down, b_out, b_down,
    own_ref, sent_ref, down_ref
):
    first = first_ref[0] == 1
    place = place_ref[0]
    weight = w_qkv[...].astype(F32)
    scaled = (weight * as_column(gain1[...].astype(F32))).astype(BF)
    three = spread(b_qkv[...].astype(F32), place)
    row = jnp.concatenate([three[i : i + 1] for i in range(3)], axis=1)
    extra = bias_rows(as_column(bias1[...].astype(F32)), weight, row)
    whole = jnp.concatenate([scaled, extra], axis=0)
    spare = jnp.zeros((PACK, LANES - SPOT), BF)
    for t in range(RING):
        for i in range(3):
            at = i * WIDTH + t * SPOT
            part = jnp.concatenate([whole[:, at : at + SPOT], spare], axis=1)
            own_ref[t, :, i * LANES : (i + 1) * LANES] = part
            sent_ref[t, :, i * LANES : (i + 1) * LANES] = part
    weight = w_up[...].astype(F32)
    scaled = (weight * as_column(gain2[...].astype(F32))).astype(BF)
    extra = bias_rows(
        as_column(bias2[...].astype(F32)), weight, spread(b_up[...].astype(F32), place)
    )
    whole = jnp.concatenate([scaled, extra], axis=0)
    for t in range(RING):
        by_a = whole[:, t * WIDTH : (t + 1) * WIDTH]
        by_b = jnp.concatenate(
            [whole[:, a * WIDTH + t * SPOT : a * WIDTH + (t + 1) * SPOT] for a in range(RING)],
            axis=1,
        )
        own_ref[t, :, WIDTH:] = jnp.where(first, by_a, by_b)
        sent_ref[t, :, WIDTH:] = jnp.where(first, by_b, by_a)
    down_ref[:SPOT] = w_down[...]
    rows = [spread(b[...].astype(F32), place).astype(BF) for b in (b_out, b_down)]
    rows.append(jnp.zeros((PACK - OWN_ROWS - 2, WIDTH), BF))
    down_ref[SPOT:] = jnp.concatenate(rows, axis=0)


def out_rows(rows):
    parts = [rows[j * LANES : j * LANES + OWN_ROWS, :] for j in range(RING)]
    return jnp.concatenate(parts + [jnp.zeros((LANES - SPOT, WIDTH), BF)], axis=0)


def down_rows(rows):
    parts = [rows[j * LANES + OWN_ROWS : j * LANES + OWN_ROWS + SPOT, :] for j in range(RING)]
    return jnp.concatenate(parts, axis=0)


def out_bias_row(rows):
    total = jnp.zeros((1, WIDTH), F32)
    for j in range(RING):
        extra = rows[j * LANES + OWN_ROWS + SPOT : (j + 1) * LANES, :].astype(F32)
        total = total + extra[0:1, :] + extra[1:2, :]
    return total


def rotate(value, cos, sin):
    cos = jnp.concatenate([cos, cos], axis=1)
    sin = jnp.concatenate([sin, sin], axis=1)
    lanes = value.shape[1]
    lane = lax.broadcasted_iota(jnp.int32, value.shape, 1)
    other = jnp.where(
        (lane & (HEAD_DIM - 1)) < 8,
        -pltpu.roll(value, lanes - 8, 1),
        pltpu.roll(value, 8, 1),
    )
    return value * cos + other * sin


def places(feature):
    row = lax.broadcasted_iota(jnp.int32, (WIDTH, feature.shape[1]), 0)
    return jnp.where(row == feature[0:1, :], 1.0, 0.0).astype(BF)


def project_turned_body(at_ref, x0, x1, x2, x3, feature, ones, w0, w1, w2, w3, cos, sin,
                        x_ref, q_ref, kv_ref, w_ref):
    for e, block in enumerate((w0, w1, w2, w3)):
        at = pl.multiple_of(lax.rem(at_ref[0] + e, RING) * LANES, LANES)
        w_ref[pl.ds(at, LANES), :] = block[...]
    project_body(x0, x1, x2, x3, feature, ones, w_ref, cos, sin, x_ref, q_ref, kv_ref)


def project_body(x0, x1, x2, x3, feature, ones, w, cos, sin, x_ref, q_ref, kv_ref):
    x = jnp.concatenate([x0[...], x1[...], x2[...], x3[...]], axis=0)
    x_all = (mm(x, places(feature)) + ones[...]).astype(BF)
    x_ref[...] = x_all
    qkv = mm(x_all, w[...])
    tables = cos[...], sin[...]
    q_ref[...] = (rotate(qkv[:, :LANES], *tables) * 0.125).astype(BF)
    kv_ref[:, :LANES] = rotate(qkv[:, LANES : 2 * LANES], *tables).astype(BF)
    kv_ref[:, LANES:] = qkv[:, 2 * LANES :].astype(BF)


def store_parts(partial, outs):
    block = partial.shape[0] // len(outs)
    for i, out in enumerate(outs):
        out[...] = partial[i * block : (i + 1) * block].astype(out.dtype)


def mlp_body(x_ref, w_up, rows, *refs):
    given = 0 if len(refs) == 3 else 1
    mids, (hidden_ref, slope_ref), outs = refs[:given], refs[given : given + 2], refs[given + 2 :]
    up_proj = mm(x_ref[...], w_up[...])
    cdf = 0.5 * (1.0 + lax.erf(up_proj * 0.7071067811865476))
    hidden = (up_proj * cdf).astype(BF)
    hidden_ref[...] = hidden
    density = jnp.exp(-0.5 * up_proj * up_proj) * 0.3989422804014327
    slope_ref[...] = (cdf + up_proj * density).astype(BF)
    partial = mm(hidden, down_rows(rows)) + out_bias_row(rows)
    for mid in mids:
        partial = partial + mm(mid[...], out_rows(rows))
    store_parts(partial, outs)


def head_mask(value, head):
    lane = lax.broadcasted_iota(jnp.int32, value.shape, 1)
    return jnp.where((lane >= head * HEAD_DIM) & (lane < (head + 1) * HEAD_DIM), value, 0)


def block_at(where_ref, j):
    return pl.multiple_of(lax.rem(j - where_ref[0] + RING, RING) * 128, 128)


def in_place_order(ref, where_ref):
    return jnp.concatenate([ref[pl.ds(block_at(where_ref, j), 128), :] for j in range(RING)], axis=0)


def allowed_pairs(where_ref, info, j):
    columns = (RING - j) * 128
    low, high = info[0:1, j * 128 :], info[1:2, j * 128 :]
    pieces = []
    for e in range(RING):
        start = (RING * j + lax.rem(where_ref[1] + e, RING)) * 128
        row = lax.broadcasted_iota(jnp.int32, (128, columns), 0) + start
        pieces.append(jnp.where((row >= low) & (row <= high), 0.0, NEG_FILL))
    return jnp.concatenate(pieces, axis=0)


def attend_body(where_ref, info_ref, q_ref, kv0, kv1, kv2, kv3, *refs):
    given = 0 if len(refs) == 2 else 2
    others, (mid_ref, lse_ref), outs = refs[:given], refs[given : given + 2], refs[given + 2 :]
    rows = q_ref.shape[0]
    info = info_ref[...]
    q = in_place_order(q_ref, where_ref)
    masked_q = [head_mask(q, h) for h in range(3)]
    tops, sums, accs = [None] * 3, [None] * 3, [None] * 3
    for j in range(RING):
        bias = allowed_pairs(where_ref, info, j)
        at = block_at(where_ref, j)
        kv = jnp.concatenate([ref[pl.ds(at, 128), :] for ref in (kv0, kv1, kv2, kv3)], axis=0)
        keys = kv[:, :LANES]
        values_t = kv[:, LANES:].T
        low = j * 128
        for h in range(3):
            scores = mm_nt(keys, masked_q[h][low:]) + bias
            top = jnp.max(scores, axis=0, keepdims=True)
            if j:
                top = jnp.maximum(tops[h][:, low:], top)
            probs = jnp.exp(scores - top)
            total = jnp.sum(probs, axis=0, keepdims=True)
            part = mm(values_t[h * HEAD_DIM : (h + 1) * HEAD_DIM, :], probs.astype(BF))
            if j:
                shrink = jnp.exp(tops[h][:, low:] - top)
                total = total + sums[h][:, low:] * shrink
                part = part + accs[h][:, low:] * shrink
                top = jnp.concatenate([tops[h][:, :low], top], axis=1)
                total = jnp.concatenate([sums[h][:, :low], total], axis=1)
                part = jnp.concatenate([accs[h][:, :low], part], axis=1)
            tops[h], sums[h], accs[h] = top, total, part
    mids = [accs[h] / sums[h] for h in range(3)] + [jnp.zeros((HEAD_DIM, rows), F32)]
    mid = jnp.concatenate(mids, axis=0).T.astype(BF)
    for j in range(RING):
        mid_ref[pl.ds(block_at(where_ref, j), 128), :] = mid[j * 128 : (j + 1) * 128]
    for h in range(3):
        lse_ref[h : h + 1, :] = tops[h] + jnp.log(sums[h])
    lse_ref[3:, :] = jnp.zeros((5, rows), F32)
    if others:
        rows_ref, mlp_ref = others
        store_parts(mm(mid_ref[...], out_rows(rows_ref)) + mlp_ref[...], outs)


def attend_back_body(
    where_ref, info_ref, q_ref, a0, a1, a2, a3, rows_ref, mid_ref, lse_ref, cos, sin,
    kv0, kv1, kv2, kv3, dq_ref, g0, g1, g2, g3
):
    rows = q_ref.shape[0]
    info = info_ref[...]
    q = in_place_order(q_ref, where_ref)
    g_all = jnp.concatenate([a0[...], a1[...], a2[...], a3[...]], axis=0)
    dq_ref[...] = mm_nt(g_all, out_rows(rows_ref)).astype(BF)
    do = in_place_order(dq_ref, where_ref)
    mid = in_place_order(mid_ref, where_ref)
    lse = lse_ref[...]
    lane = lax.broadcasted_iota(jnp.int32, (8, LANES), 1)
    head = lax.broadcasted_iota(jnp.int32, (8, LANES), 0)
    pick = jnp.where(lane // HEAD_DIM == head, 1.0, 0.0)
    delta = mm_exact(pick, do.astype(F32) * mid.astype(F32))
    masked_q = [head_mask(q, h) for h in range(3)]
    masked_do = [head_mask(do, h) for h in range(3)]
    dq = [None] * 3
    for j in range(RING):
        bias = allowed_pairs(where_ref, info, j)
        at = block_at(where_ref, j)
        kv = jnp.concatenate([ref[pl.ds(at, 128), :] for ref in (kv0, kv1, kv2, kv3)], axis=0)
        keys = kv[:, :LANES]
        keys_t = keys.T
        values = kv[:, LANES:]
        low = j * 128
        dk = jnp.zeros((rows, LANES), F32)
        dv = jnp.zeros((rows, LANES), F32)
        for h in range(3):
            queries, grads = masked_q[h][low:], masked_do[h][low:]
            scores = mm_nt(keys, queries) + bias
            probs = jnp.exp(scores - lse[h : h + 1, low:])
            dprobs = mm_nt(values, grads)
            dscores = (probs * (dprobs - delta[h : h + 1, low:])).astype(BF)
            dv = dv + mm(probs.astype(BF), grads)
            dk = dk + mm(dscores, queries)
            part = mm(keys_t[h * HEAD_DIM : (h + 1) * HEAD_DIM, :], dscores)
            if j:
                part = jnp.concatenate([dq[h][:, :low], dq[h][:, low:] + part], axis=1)
            dq[h] = part
        for e, grad in enumerate((g0, g1, g2, g3)):
            grad[pl.ds(at, 128), :LANES] = dk[e * 128 : (e + 1) * 128].astype(BF)
            grad[pl.ds(at, 128), LANES:] = dv[e * 128 : (e + 1) * 128].astype(BF)
    dq_all = jnp.concatenate(dq + [jnp.zeros((HEAD_DIM, rows), F32)], axis=0).T * 0.125
    dq_all = rotate(dq_all, in_place_order(cos, where_ref), -in_place_order(sin, where_ref))
    for j in range(RING):
        dq_ref[pl.ds(block_at(where_ref, j), 128), :] = dq_all[j * 128 : (j + 1) * 128].astype(BF)


def mlp_back_body(a0, a1, a2, a3, slope, w_up, rows, grad_ref, dx_ref):
    g_all = jnp.concatenate([a0[...], a1[...], a2[...], a3[...]], axis=0)
    grad_up = (mm_nt(g_all, down_rows(rows)) * slope[...].astype(F32)).astype(BF)
    grad_ref[...] = grad_up
    dx_ref[...] = mm_nt(grad_up, w_up[...])


def weight_grads_body(a0, a1, a2, a3, hidden, mid, x_ref, grad_qkv, grad_up, out_ref):
    step = pl.program_id(0)

    @pl.when(step == 0)
    def rows_part():
        g_all = jnp.concatenate([a0[...], a1[...], a2[...], a3[...]], axis=0)
        down_grad = mm_tn(hidden[...], g_all).astype(BF)
        out_grad = mm_tn(mid[...], g_all).astype(BF)
        sums = jnp.sum(g_all.astype(F32), axis=0, keepdims=True)
        sums = jnp.broadcast_to(sums, (PACK - OWN_ROWS, WIDTH)).astype(BF)
        for j in range(RING):
            at = j * LANES
            out_ref[at : at + OWN_ROWS, :] = out_grad[j * OWN_ROWS : (j + 1) * OWN_ROWS]
            out_ref[at + OWN_ROWS : at + OWN_ROWS + SPOT, :] = down_grad[j * SPOT : (j + 1) * SPOT]
            out_ref[at + OWN_ROWS + SPOT : at + LANES, :] = sums

    @pl.when(step == 1)
    def up_part():
        out_ref[...] = mm_tn(x_ref[...], grad_up[...]).astype(BF)

    @pl.when(step == 2)
    def qkv_part():
        out_ref[...] = mm_tn(x_ref[...], grad_qkv[...]).astype(BF)


def qkv_back_body(
    dq, g0, g1, g2, g3, cos, sin, w_qkv, dx_up, feature, grad_ref, d0, d1, d2, d3
):
    dkv = g0[...].astype(F32)
    for part in (g1, g2, g3):
        dkv = dkv + part[...].astype(F32)
    dk = rotate(dkv[:, :LANES], cos[...], -sin[...])
    grad = jnp.concatenate([dq[...], dk.astype(BF), dkv[:, LANES:].astype(BF)], axis=1)
    grad_ref[...] = grad
    dx = (mm_nt(grad, w_qkv[...]) + dx_up[...]).astype(BF)
    store_parts(mm_nt(dx, places(feature)), (d0, d1, d2, d3))


def own_piece(row, place):
    size = row.shape[1] // (RING * RING)
    return sum(
        jnp.where(place == f, row[:, f * size : (f + 1) * size], 0.0) for f in range(RING * RING)
    )


def finish_body(
    place_ref, l0, l1, r0, r1, gain1, bias1, gain2, bias2, w_qkv, w_up,
    gain1_ref, bias1_ref, gain2_ref, bias2_ref, qkv_ref, b_qkv_ref, out_ref, b_out_ref, up_ref, b_up_ref, down_ref
):
    place = place_ref[0]

    def total(low, high):
        return jnp.concatenate(
            [
                one[:, low:high].astype(F32) + two[:, low:high].astype(F32)
                for one, two in ((l0, r0), (l1, r1))
            ],
            axis=0,
        )

    m = total(0, WIDTH)
    m_qkv = jnp.concatenate(
        [
            m[t * PACK : (t + 1) * PACK, i * LANES : i * LANES + SPOT]
            for i in range(3)
            for t in range(RING)
        ],
        axis=1,
    )
    m = total(WIDTH, 2 * WIDTH)
    m_up = jnp.concatenate([m[t * PACK : (t + 1) * PACK] for t in range(RING)], axis=1)
    rows = total(2 * WIDTH, 3 * WIDTH)
    out_ref[...] = rows[:OWN_ROWS]
    down_ref[...] = rows[OWN_ROWS : OWN_ROWS + SPOT]
    b_out_ref[...] = own_piece(rows[OWN_ROWS + SPOT : OWN_ROWS + SPOT + 1], place)
    for m, w_ref, gain, bias, gain_ref, bias_ref, grad_ref in (
        (m_qkv, w_qkv, gain1, bias1, gain1_ref, bias1_ref, qkv_ref),
        (m_up, w_up, gain2, bias2, gain2_ref, bias2_ref, up_ref),
    ):
        ends = m[OWN_ROWS : OWN_ROWS + 1]
        m = m[:OWN_ROWS]
        weight = w_ref[...].astype(F32)
        all_ones = jnp.ones((8, m.shape[1]), F32)
        gain_ref[...] = mm_exact(all_ones, weight * m)[0:1]
        bias_ref[...] = mm_exact(all_ones, weight * ends)[0:1]
        grad_ref[...] = as_column(gain[...].astype(F32)) * m + as_column(bias[...].astype(F32)) * ends
    ends = m_qkv[OWN_ROWS : OWN_ROWS + 1]
    b_qkv_ref[...] = jnp.concatenate(
        [own_piece(ends[:, i * WIDTH : (i + 1) * WIDTH], place) for i in range(3)], axis=0
    )
    b_up_ref[...] = own_piece(m_up[OWN_ROWS : OWN_ROWS + 1], place)


def unit_rows_of(rows):
    centered = rows - jnp.mean(rows, axis=-1, keepdims=True)
    inv_std = lax.rsqrt(jnp.mean(centered * centered, axis=-1, keepdims=True) + EPSILON)
    return centered * inv_std, inv_std


def forward_layer(tok_rows, xs, weights, geometry, order, mlp_first):
    w_qkv, w_up, w_rows = weights
    where, info, tables = geometry
    own = tok_rows.shape[0]
    rows = RING * own
    outs = (like((rows, RING * LANES), BF), like((rows, LANES), BF), like((rows, 2 * LANES), BF))
    if isinstance(w_qkv, list):
        at, *blocks = w_qkv
        x_all, q, kv, w_qkv = vmem_call(
            project_turned_body,
            outs + (like((RING * LANES, WIDTH), BF),),
            1_600_000_000,
            (at,),
            *xs,
            *order,
            *blocks,
            *tables,
        )
    else:
        x_all, q, kv = vmem_call(
            project_body, outs, 1_600_000_000, (), *xs, *order, w_qkv, *tables
        )
    kvs = in_order([kv] + [send(kv, along_tokens(-by)) for by in (1, 3, 2)])
    whole = (like((rows, WIDTH), F32),)
    cut = (like((own, WIDTH), F32),) + (like((own, WIDTH), BF),) * (RING - 1)

    def mlp(attended, outs):
        return vmem_call(
            mlp_body,
            (like((rows, WIDTH), BF), like((rows, WIDTH), BF)) + outs,
            2_000_000_000,
            (),
            x_all,
            w_up,
            w_rows,
            *attended,
        )

    def attention(others, outs):
        return vmem_call(
            attend_body,
            (like((rows, LANES), BF), like((8, rows), F32)) + outs,
            6_000_000_000,
            (where,),
            info,
            q,
            *kvs,
            *others,
        )

    if mlp_first:
        hidden, slope, partial = mlp((), whole)
        mid, lse, *parts = attention((w_rows, partial), cut)
    else:
        mid, lse = attention((), ())
        hidden, slope, *parts = mlp((mid,), cut)
    total = tok_rows + parts[0]
    for by in (1, 3, 2):
        total = total + send(parts[by], along_weights(by)).astype(F32)
    return total, (x_all, q, kvs, hidden, slope, mid, lse), w_qkv


def backward_layer(
    grad_rows, gs, unit, inv_std, weights, stored, geometry, order, tie, late
):
    w_qkv, w_up, w_rows = weights
    where, info, tables = geometry
    x_all, q, kvs, hidden, slope, mid, lse = stored
    own = grad_rows.shape[0]
    rows = RING * own

    def attention_back(gs):
        return vmem_call(
            attend_back_body,
            (like((rows, LANES), BF),) + (like((rows, 2 * LANES), BF),) * RING,
            16_000_000_000,
            (where,),
            info,
            q,
            *gs,
            w_rows,
            mid,
            lse,
            *tables,
            *kvs,
        )

    dq, *dkvs = attention_back(gs)
    received = [send(dkvs[by], along_tokens(by)) for by in (1, 3, 2)]
    grad_up, dx_up = vmem_call(
        mlp_back_body,
        (like((rows, WIDTH), BF), like((rows, RING * LANES), F32)),
        1_600_000_000,
        (),
        *([after(gs[0], *tie)] + gs[1:]),
        slope,
        w_up,
        w_rows,
    )
    grad_qkv, *dxs = vmem_call(
        qkv_back_body,
        (like((rows, WIDTH), BF),) + (like((own, WIDTH), BF),) * RING,
        2_000_000_000,
        (),
        dq,
        dkvs[0],
        *received,
        *tables,
        w_qkv,
        dx_up,
        order[0],
    )
    total = dxs[0].astype(F32)
    for by in (1, 3, 2):
        total = total + send(dxs[by], along_weights(by)).astype(F32)
    grad_in = grad_rows.astype(F32) + inv_std * (
        total
        - jnp.mean(total, axis=-1, keepdims=True)
        - unit * jnp.mean(total * unit, axis=-1, keepdims=True)
    )
    grad_in = grad_in.astype(BF)
    cuts = vmem_call(
        weight_grads_body,
        like((RING * LANES, 3 * WIDTH), BF),
        3_000_000_000,
        (),
        *gs,
        hidden,
        mid,
        x_all,
        after(grad_qkv, *((grad_in,) if late else ())),
        grad_up,
        steps=3,
    )
    return grad_in, scatter_tokens_axis(cuts), cuts


def over_weights(total, tp):
    parts = [total[:PACK]] + [
        send(total[by * PACK : (by + 1) * PACK], along_weights(by)) for by in (1, 3, 2)
    ]
    near = in_order(parts)
    return turned([near[0], near[3], near[2], near[1]], tp)


def to_core(value, core):
    return send(value, moves(lambda s, a, b: flat(core, a, b) if s != core else None))


def over_replicas(low):
    rest = lax.axis_size("replica")

    def swapped(value, partner):
        return lax.ppermute(value, "replica", [(i, partner(i)) for i in range(rest)])

    def inner(i):
        return i ^ 1

    def outer(i):
        return rest - 1 - i

    half = low.shape[0] // 2
    left, right = low[:half], low[half:]
    left = (left.astype(F32) + swapped(left, inner).astype(F32)).astype(BF)
    right = (right.astype(F32) + swapped(right, outer).astype(F32)).astype(BF)
    return left, right, swapped(left, outer), swapped(right, inner)


def on_device(
    pipe_ends,
    seq_lengths,
    norm1_gain,
    norm1_bias,
    norm2_gain,
    norm2_bias,
    qkv_weight,
    qkv_bias,
    out_weight,
    out_bias,
    up_weight,
    up_bias,
    down_weight,
    down_bias,
):
    core = lax.axis_index("section")
    first = core == 0
    place = lax.axis_index("fsdp")
    a_at, b_at = place // RING, place % RING
    tp = jnp.where(first, a_at, b_at)
    sq = jnp.where(first, b_at, a_at)
    rows_dev = pipe_ends.shape[3]

    def block_of(weight_at, token_at):
        weight_at, token_at = weight_at % RING, token_at % RING
        return jnp.where(first, RING * weight_at + token_at, RING * token_at + weight_at)

    ring = jnp.arange(RING, dtype=jnp.int32)
    kept = block_of(tp + ring[None, :], ring[:, None]).reshape(-1).astype(jnp.int32)
    spare = jnp.arange(PACK, dtype=jnp.int32)[None, :]
    feature = jnp.where(spare < OWN_ROWS, kept[:, None] * OWN_ROWS + spare, -1).reshape(1, -1)
    ones = np.tile((np.arange(PACK) // 2 == OWN_ROWS // 2).astype(np.float32), RING * RING)
    order = (jnp.broadcast_to(feature, (8, RING * LANES)), ones[None, :])

    flags = (first.astype(jnp.int32)[None], place.astype(jnp.int32)[None])
    pack = like((RING, PACK, 2 * WIDTH), BF)
    own_pack, sent_pack, pack_down = vmem_call(
        pack_body,
        (pack, pack, like((SPOT + PACK - OWN_ROWS, WIDTH), BF)),
        1_000_000,
        flags,
        norm1_gain,
        norm1_bias,
        norm2_gain,
        norm2_bias,
        qkv_weight[0],
        qkv_bias[0],
        up_weight[0],
        up_bias,
        down_weight[0],
        out_bias,
        down_bias,
    )
    swap = moves(lambda s, a, b: flat(1 - s, a, b))

    def both(own, other):
        return jnp.where(first, own, other), jnp.where(first, other, own)

    early_pack, late_pack = both(own_pack, send(sent_pack, swap))
    turn = moves(lambda s, a, b: flat(1, b, a) if s == 0 else flat(0, a, b))
    back = moves(lambda s, a, b: flat(1, a, b) if s == 0 else flat(0, b, a))
    stay = moves(lambda s, a, b: None if s == 0 else flat(s, b, a))
    other_ends = send(jnp.where(first, pipe_ends[0, 1, 0], pipe_ends[0, 0, 0]), turn)
    tokens_in = jnp.where(first, pipe_ends[0, 0, 0], other_ends)
    cotangent = jnp.where(first, other_ends, send(pipe_ends[0, 1, 0], stay))

    lens = lax.dynamic_index_in_dim(seq_lengths[:, 0], core, 0, keepdims=False)
    where = jnp.stack([tp, sq]).astype(jnp.int32)

    def rows_of(places):
        blocks = RING * (places % RING) + sq
        return (blocks[:, None] * rows_dev + jnp.arange(rows_dev)[None, :]).reshape(-1).astype(
            jnp.int32
        )

    def begin_of(rows_at):
        return jnp.sum(
            jnp.where(rows_at[None, :] >= finish[:, None], lens[:, None], 0), axis=0
        ).astype(jnp.int32)

    finish = jnp.cumsum(lens)
    ordered = rows_of(ring)
    rows_at = rows_of(tp + ring)
    begin = begin_of(rows_at)
    info = jnp.concatenate(
        [begin_of(ordered)[None, :], ordered[None, :], jnp.zeros((6, ordered.shape[0]), jnp.int32)],
        axis=0,
    )
    in_head = np.arange(2 * HEAD_DIM) % HEAD_DIM
    inv_freq = (10000.0 ** (-(in_head % 8) / 8.0)).astype(np.float32)
    inv_freq = np.where(in_head < 16, inv_freq, np.float32(0))
    angles = (rows_at - begin).astype(F32)[:, None] * inv_freq[None, :]
    tables = (jnp.cos(angles), jnp.sin(angles))
    geometry = (where, info, tables)

    def to_columns(pack):
        def block_for(by):
            return lax.dynamic_index_in_dim(pack, (tp + by) % RING, 0, keepdims=False)

        parts = [block_for(0)] + [
            send(block_for(-by), along_weights(-by)) for by in (1, 3, 2)
        ]
        return jnp.concatenate(in_order(parts), axis=0)

    down_layers = both(pack_down, send(pack_down, swap))
    out_other = send(out_weight[0], turn)
    out_turned = send(out_weight[0], stay)
    out_layers = jnp.where(first, out_weight[0], out_other), jnp.where(first, out_other, out_turned)
    row_packs = [jnp.concatenate([out_layers[i], down_layers[i]], axis=0) for i in range(2)]

    unit0, inv_std0 = unit_rows_of(tokens_in.astype(F32))
    xs0 = in_order(gathered_weights_axis(unit0.astype(BF)))
    columns = to_columns(jnp.concatenate([early_pack, late_pack], axis=2))
    columns = after(columns, *xs0, info, *tables)
    qkv0 = columns[:, :WIDTH]
    qkv0 = in_order([qkv0] + [send(qkv0, along_tokens(-by)) for by in (1, 3, 2)])
    qkv0 = [sq.astype(jnp.int32)[None]] + qkv0
    mlp0 = gather_tokens_axis(
        jnp.concatenate([columns[:, WIDTH : 2 * WIDTH], row_packs[0]], axis=1)
    )
    weights0 = (qkv0, (mlp0, 0), (mlp0, 1))

    out0, stored0, qkv0 = forward_layer(
        tokens_in.astype(F32), xs0, weights0, geometry, order, False
    )
    weights0 = (qkv0, (mlp0, 0), (mlp0, 1))
    gs1 = in_order(gathered_weights_axis(after(cotangent, stored0[1])))
    later = jnp.concatenate([columns[:, 2 * WIDTH :], row_packs[1]], axis=1)
    all1 = gather_tokens_axis(after(later, *stored0[2]))
    weights1 = ((all1, 0), (all1, 1), (all1, 2))
    low0 = out0.astype(BF)
    unit1, inv_std1 = unit_rows_of(low0.astype(F32))
    xs1 = in_order(gathered_weights_axis(unit1.astype(BF)))
    out1, stored1, unused = forward_layer(
        low0.astype(F32), xs1, weights1, geometry, order, True
    )
    low1 = out1.astype(BF)

    def up_swapped(value):
        value = value.reshape(RING, PACK, RING, SPOT)
        return value.transpose(2, 1, 0, 3).reshape(RING * PACK, WIDTH)

    def rows_turned(rows):
        out_part = jnp.where(first, rows[:OWN_ROWS], send(rows[:OWN_ROWS], stay))
        return jnp.concatenate([out_part, rows[OWN_ROWS:]], axis=0)

    def joined(part, layer):
        return (part.astype(F32) + to_core(part, layer).astype(F32)).astype(BF)

    def joined_up(part, layer):
        return joined(jnp.where(first, part, up_swapped(part)), layer)

    grad1, scattered1, unused = backward_layer(
        cotangent,
        gs1,
        unit1,
        inv_std1,
        weights1,
        stored1,
        geometry,
        order,
        (low1,),
        True,
    )
    gs0 = in_order(gathered_weights_axis(grad1))

    def swapped_rows(early, late):
        other = send(jnp.where(first, late, early), back)
        mine = jnp.where(first, early, send(late, stay))
        stacked = jnp.stack([jnp.where(first, mine, other), jnp.where(first, other, mine)])
        return stacked[None, :, None], other

    layer_out, out_other = swapped_rows(low0, low1)

    def to_owner(scattered, columns, layer):
        return jnp.concatenate(
            [
                joined(columns[:, :WIDTH], layer),
                joined_up(columns[:, WIDTH:], layer),
                joined(rows_turned(scattered[:, 2 * WIDTH :]), layer),
            ],
            axis=1,
        )

    grad0, scattered0, cuts0 = backward_layer(
        grad1,
        gs0,
        unit0,
        inv_std0,
        weights0,
        stored0,
        geometry,
        order,
        (out_other,),
        False,
    )
    scattered1 = after(scattered1, cuts0, grad0)
    columns1 = over_weights(scattered1[:, : 2 * WIDTH], tp)
    owned1 = to_owner(scattered1, columns1, 1)
    input_grad, grad_other = swapped_rows(grad0, grad1)
    scattered0 = after(scattered0, owned1, grad_other)
    columns0 = over_weights(scattered0[:, : 2 * WIDTH], tp)
    parts = over_replicas(jnp.where(first, to_owner(scattered0, columns0, 0), owned1))

    vector = like((1, OWN_ROWS), F32)
    gain1_grad, bias1_grad, gain2_grad, bias2_grad, *grads = vmem_call(
        finish_body,
        (
            vector,
            vector,
            vector,
            vector,
            like((OWN_ROWS, 3 * WIDTH), F32),
            like((3, OWN_ROWS), F32),
            like((OWN_ROWS, WIDTH), F32),
            vector,
            like((OWN_ROWS, RING * WIDTH), F32),
            like((1, SPOT), F32),
            like((SPOT, WIDTH), F32),
        ),
        10_000_000,
        flags[1:],
        *parts,
        norm1_gain,
        norm1_bias,
        norm2_gain,
        norm2_bias,
        qkv_weight[0],
        up_weight[0],
    )
    qkv_grad, qkv_bias_grad, out_grad, end_grad, up_grad, up_bias_grad, down_grad = grads
    return (
        layer_out,
        input_grad,
        gain1_grad,
        bias1_grad,
        gain2_grad,
        bias2_grad,
        qkv_grad[None],
        qkv_bias_grad[None],
        out_grad[None],
        end_grad,
        up_grad[None],
        up_bias_grad,
        down_grad[None],
        end_grad,
    )


def solution(mesh):
    tokens = P("section", None, "replica", "fsdp", None)
    vector = P("section", "fsdp")
    matrix = P("section", "fsdp", None)
    three = P("section", None, "fsdp")
    params = (
        vector,
        vector,
        vector,
        vector,
        matrix,
        three,
        matrix,
        vector,
        matrix,
        vector,
        matrix,
        vector,
    )
    return jax.shard_map(
        on_device,
        mesh=mesh,
        in_specs=(tokens, P(None, "replica", None)) + params,
        out_specs=(tokens, tokens) + params,
        check_vma=False,
    )
```

```python
import jax
import jax.numpy as jnp
import numpy as np
from jax import lax
from jax.experimental import pallas as pl
from jax.experimental.pallas import tpu as pltpu
from jax.sharding import PartitionSpec as P

HEADS = 12
HEAD_DIM = 64
EPSILON = 1e-05
NEG_FILL = -1e30
WIDTH = 768
RING = 4
OWN_ROWS = 48
PACK = 64
LANES = 256
SPOT = 192
BF = jnp.bfloat16
F32 = jnp.float32
CORES = ("section", "fsdp")


def flat(core, a, b):
    return core * RING * RING + (a % RING) * RING + b % RING


def moves(step):
    return [
        (flat(core, a, b), step(core, a, b))
        for core in range(2)
        for a in range(RING)
        for b in range(RING)
        if step(core, a, b) is not None
    ]


def along_weights(by):
    return moves(lambda core, a, b: flat(core, a + by, b) if core == 0 else flat(core, a, b + by))


def along_tokens(by):
    return moves(lambda core, a, b: flat(core, a, b + by) if core == 0 else flat(core, a + by, b))


def token_groups():
    return [[flat(0, a, b) for b in range(RING)] for a in range(RING)] + [
        [flat(1, a, b) for a in range(RING)] for b in range(RING)
    ]


def send(value, pairs):
    return lax.ppermute(value, CORES, pairs)


def gather_tokens_axis(block):
    return lax.all_gather(block, CORES, axis=0, tiled=True, axis_index_groups=token_groups())


def scatter_tokens_axis(total):
    return lax.psum_scatter(
        total, CORES, scatter_dimension=0, tiled=True, axis_index_groups=token_groups()
    )


def gathered_weights_axis(block):
    return [block] + [send(block, along_weights(-by)) for by in (1, 3, 2)]


ORDER = (0, 1, 3, 2)


def turned(blocks, by):
    rows = blocks[0].shape[0]
    twice = jnp.concatenate(list(blocks) + list(blocks), axis=0)
    return lax.dynamic_slice_in_dim(twice, ((RING - by) % RING) * rows, RING * rows, 0)


def in_order(blocks):
    found = dict(zip(ORDER, blocks))
    return [found[i] for i in range(RING)]


def after(value, *others):
    return lax.optimization_barrier((value,) + others)[0]


def vmem_call(body, out_shapes, flops, scalars, *arrays, steps=1):
    specs, operands = [], []
    for item in arrays:
        array, column = item if isinstance(item, tuple) else (item, None)
        block = array.shape if column is None else (array.shape[0], WIDTH)
        place = (0,) * array.ndim if column is None else (0, column)
        specs.append(pl.BlockSpec(block, lambda i, place=place: place))
        operands.append(array)
    return pl.pallas_call(
        body,
        grid=(steps,),
        out_shape=out_shapes,
        in_specs=[pl.BlockSpec(memory_space=pltpu.SMEM)] * len(scalars) + specs,
        out_specs=pl.BlockSpec(
            (out_shapes.shape[0], out_shapes.shape[1] // steps), lambda i: (0, steps - 1 - i)
        )
        if steps > 1
        else jax.tree.map(
            lambda shape: pl.BlockSpec(shape.shape, lambda i, n=len(shape.shape): (0,) * n),
            out_shapes,
        ),
        compiler_params=pltpu.CompilerParams(vmem_limit_bytes=56 * 1024 * 1024),
        cost_estimate=pl.CostEstimate(flops=flops, bytes_accessed=4_000_000, transcendentals=0),
    )(*scalars, *operands)


def like(shape, dtype):
    return jax.ShapeDtypeStruct(shape, dtype)


def mm(left, right):
    return lax.dot_general(left, right, (((1,), (0,)), ((), ())), preferred_element_type=F32)


def mm_nt(left, right):
    return lax.dot_general(left, right, (((1,), (1,)), ((), ())), preferred_element_type=F32)


def mm_exact(left, right):
    return lax.dot_general(
        left,
        right,
        (((1,), (1,)), ((), ())),
        precision=lax.Precision.HIGHEST,
        preferred_element_type=F32,
    )


def mm_tn(left, right):
    return lax.dot_general(left, right, (((0,), (0,)), ((), ())), preferred_element_type=F32)


def bias_rows(bias, weight, row):
    row = row + jnp.sum(bias * weight, axis=0, keepdims=True)
    high = row.astype(BF)
    low = (row - high.astype(F32)).astype(BF)
    return jnp.concatenate(
        [high, low, jnp.zeros((PACK - OWN_ROWS - 2, row.shape[1]), BF)], axis=0
    )


def as_column(row):
    size = row.shape[1]
    at = lax.broadcasted_iota(jnp.int32, (size, size), 0)
    lane = lax.broadcasted_iota(jnp.int32, (size, size), 1)
    return jnp.sum(jnp.where(at == lane, row, 0.0), axis=1, keepdims=True)


def spread(piece, place):
    size = piece.shape[1]
    whole = jnp.concatenate([piece] * (RING * RING), axis=1)
    lane = lax.broadcasted_iota(jnp.int32, whole.shape, 1)
    return jnp.where((lane >= place * size) & (lane < (place + 1) * size), whole, 0.0)


def pack_body(
    first_ref, place_ref, gain1, bias1, gain2, bias2, w_qkv, b_qkv, w_up, b_up, w_down, b_out, b_down,
    own_ref, sent_ref, down_ref
):
    first = first_ref[0] == 1
    place = place_ref[0]
    weight = w_qkv[...].astype(F32)
    scaled = (weight * as_column(gain1[...].astype(F32))).astype(BF)
    three = spread(b_qkv[...].astype(F32), place)
    row = jnp.concatenate([three[i : i + 1] for i in range(3)], axis=1)
    extra = bias_rows(as_column(bias1[...].astype(F32)), weight, row)
    whole = jnp.concatenate([scaled, extra], axis=0)
    spare = jnp.zeros((PACK, LANES - SPOT), BF)
    for t in range(RING):
        for i in range(3):
            at = i * WIDTH + t * SPOT
            part = jnp.concatenate([whole[:, at : at + SPOT], spare], axis=1)
            own_ref[t, :, i * LANES : (i + 1) * LANES] = part
            sent_ref[t, :, i * LANES : (i + 1) * LANES] = part
    weight = w_up[...].astype(F32)
    scaled = (weight * as_column(gain2[...].astype(F32))).astype(BF)
    extra = bias_rows(
        as_column(bias2[...].astype(F32)), weight, spread(b_up[...].astype(F32), place)
    )
    whole = jnp.concatenate([scaled, extra], axis=0)
    for t in range(RING):
        by_a = whole[:, t * WIDTH : (t + 1) * WIDTH]
        by_b = jnp.concatenate(
            [whole[:, a * WIDTH + t * SPOT : a * WIDTH + (t + 1) * SPOT] for a in range(RING)],
            axis=1,
        )
        own_ref[t, :, WIDTH:] = jnp.where(first, by_a, by_b)
        sent_ref[t, :, WIDTH:] = jnp.where(first, by_b, by_a)
    down_ref[:SPOT] = w_down[...]
    rows = [spread(b[...].astype(F32), place).astype(BF) for b in (b_out, b_down)]
    rows.append(jnp.zeros((PACK - OWN_ROWS - 2, WIDTH), BF))
    down_ref[SPOT:] = jnp.concatenate(rows, axis=0)


def out_rows(rows):
    parts = [rows[j * LANES : j * LANES + OWN_ROWS, :] for j in range(RING)]
    return jnp.concatenate(parts + [jnp.zeros((LANES - SPOT, WIDTH), BF)], axis=0)


def down_rows(rows):
    parts = [rows[j * LANES + OWN_ROWS : j * LANES + OWN_ROWS + SPOT, :] for j in range(RING)]
    return jnp.concatenate(parts, axis=0)


def out_bias_row(rows):
    total = jnp.zeros((1, WIDTH), F32)
    for j in range(RING):
        extra = rows[j * LANES + OWN_ROWS + SPOT : (j + 1) * LANES, :].astype(F32)
        total = total + extra[0:1, :] + extra[1:2, :]
    return total


def rotate(value, cos, sin):
    cos = jnp.concatenate([cos, cos], axis=1)
    sin = jnp.concatenate([sin, sin], axis=1)
    lanes = value.shape[1]
    lane = lax.broadcasted_iota(jnp.int32, value.shape, 1)
    other = jnp.where(
        (lane & (HEAD_DIM - 1)) < 8,
        -pltpu.roll(value, lanes - 8, 1),
        pltpu.roll(value, 8, 1),
    )
    return value * cos + other * sin


def places(feature):
    row = lax.broadcasted_iota(jnp.int32, (WIDTH, feature.shape[1]), 0)
    return jnp.where(row == feature[0:1, :], 1.0, 0.0).astype(BF)


def project_turned_body(at_ref, x0, x1, x2, x3, feature, ones, w0, w1, w2, w3, cos, sin,
                        x_ref, q_ref, kv_ref, w_ref):
    for e, block in enumerate((w0, w1, w2, w3)):
        at = pl.multiple_of(lax.rem(at_ref[0] + e, RING) * LANES, LANES)
        w_ref[pl.ds(at, LANES), :] = block[...]
    project_body(x0, x1, x2, x3, feature, ones, w_ref, cos, sin, x_ref, q_ref, kv_ref)


def project_body(x0, x1, x2, x3, feature, ones, w, cos, sin, x_ref, q_ref, kv_ref):
    x = jnp.concatenate([x0[...], x1[...], x2[...], x3[...]], axis=0)
    x_all = (mm(x, places(feature)) + ones[...]).astype(BF)
    x_ref[...] = x_all
    qkv = mm(x_all, w[...])
    tables = cos[...], sin[...]
    q_ref[...] = (rotate(qkv[:, :LANES], *tables) * 0.125).astype(BF)
    kv_ref[:, :LANES] = rotate(qkv[:, LANES : 2 * LANES], *tables).astype(BF)
    kv_ref[:, LANES:] = qkv[:, 2 * LANES :].astype(BF)


def store_parts(partial, outs):
    block = partial.shape[0] // len(outs)
    for i, out in enumerate(outs):
        out[...] = partial[i * block : (i + 1) * block].astype(out.dtype)


def mlp_body(x_ref, w_up, rows, *refs):
    given = 0 if len(refs) == 3 else 1
    mids, (hidden_ref, slope_ref), outs = refs[:given], refs[given : given + 2], refs[given + 2 :]
    up_proj = mm(x_ref[...], w_up[...])
    cdf = 0.5 * (1.0 + lax.erf(up_proj * 0.7071067811865476))
    hidden = (up_proj * cdf).astype(BF)
    hidden_ref[...] = hidden
    density = jnp.exp(-0.5 * up_proj * up_proj) * 0.3989422804014327
    slope_ref[...] = (cdf + up_proj * density).astype(BF)
    partial = mm(hidden, down_rows(rows)) + out_bias_row(rows)
    for mid in mids:
        partial = partial + mm(mid[...], out_rows(rows))
    store_parts(partial, outs)


def head_mask(value, head):
    lane = lax.broadcasted_iota(jnp.int32, value.shape, 1)
    return jnp.where((lane >= head * HEAD_DIM) & (lane < (head + 1) * HEAD_DIM), value, 0)


def allowed_pairs(starts_ref, info, e, rows):
    part = rows // RING
    pieces = []
    for d in range(RING):
        base = lax.broadcasted_iota(jnp.int32, (part, rows), 0) + starts_ref[e * RING + d]
        pieces.append(jnp.where((base >= info[0:1, :]) & (base <= info[1:2, :]), 0.0, NEG_FILL))
    return jnp.concatenate(pieces, axis=0)


def attend_body(starts_ref, info_ref, q_ref, kv0, kv1, kv2, kv3, *refs):
    given = 0 if len(refs) == 2 else 2
    others, (mid_ref, lse_ref), outs = refs[:given], refs[given : given + 2], refs[given + 2 :]
    rows = q_ref.shape[0]
    info = info_ref[...]
    q = q_ref[...]
    masked_q = [head_mask(q, h) for h in range(3)]
    tops, sums, accs = [None] * 3, [None] * 3, [None] * 3
    for e, kv in enumerate((kv0, kv1, kv2, kv3)):
        bias = allowed_pairs(starts_ref, info, e, rows)
        keys = kv[:, :LANES]
        values_t = kv[:, LANES:].T
        for h in range(3):
            scores = mm_nt(keys, masked_q[h]) + bias
            top = jnp.max(scores, axis=0, keepdims=True)
            if e:
                top = jnp.maximum(tops[h], top)
            probs = jnp.exp(scores - top)
            total = jnp.sum(probs, axis=0, keepdims=True)
            part = mm(values_t[h * HEAD_DIM : (h + 1) * HEAD_DIM, :], probs.astype(BF))
            if e:
                shrink = jnp.exp(tops[h] - top)
                total = total + sums[h] * shrink
                part = part + accs[h] * shrink
            tops[h], sums[h], accs[h] = top, total, part
    mids = [accs[h] / sums[h] for h in range(3)] + [jnp.zeros((HEAD_DIM, rows), F32)]
    mid = jnp.concatenate(mids, axis=0).T.astype(BF)
    mid_ref[...] = mid
    for h in range(3):
        lse_ref[h : h + 1, :] = tops[h] + jnp.log(sums[h])
    lse_ref[3:, :] = jnp.zeros((5, rows), F32)
    if others:
        rows_ref, mlp_ref = others
        store_parts(mm(mid, out_rows(rows_ref)) + mlp_ref[...], outs)


def attend_back_body(
    starts_ref, info_ref, q_ref, a0, a1, a2, a3, rows_ref, mid_ref, lse_ref, cos, sin,
    kv0, kv1, kv2, kv3, dq_ref, g0, g1, g2, g3
):
    rows = q_ref.shape[0]
    info = info_ref[...]
    q = q_ref[...]
    g_all = jnp.concatenate([a0[...], a1[...], a2[...], a3[...]], axis=0)
    do = mm_nt(g_all, out_rows(rows_ref)).astype(BF)
    lse = lse_ref[...]
    lane = lax.broadcasted_iota(jnp.int32, (8, LANES), 1)
    head = lax.broadcasted_iota(jnp.int32, (8, LANES), 0)
    pick = jnp.where(lane // HEAD_DIM == head, 1.0, 0.0)
    products = do.astype(F32) * mid_ref[...].astype(F32)
    delta = lax.dot_general(
        pick,
        products,
        (((1,), (1,)), ((), ())),
        precision=lax.Precision.HIGHEST,
        preferred_element_type=F32,
    )
    masked_q = [head_mask(q, h) for h in range(3)]
    masked_do = [head_mask(do, h) for h in range(3)]
    dq = [None] * 3
    for e, (kv, grad) in enumerate(zip((kv0, kv1, kv2, kv3), (g0, g1, g2, g3))):
        bias = allowed_pairs(starts_ref, info, e, rows)
        keys = kv[:, :LANES]
        keys_t = keys.T
        values = kv[:, LANES:]
        dk = jnp.zeros((rows, LANES), F32)
        dv = jnp.zeros((rows, LANES), F32)
        for h in range(3):
            scores = mm_nt(keys, masked_q[h]) + bias
            probs = jnp.exp(scores - lse[h : h + 1, :])
            dprobs = mm_nt(values, masked_do[h])
            dscores = (probs * (dprobs - delta[h : h + 1, :])).astype(BF)
            dv = dv + mm(probs.astype(BF), masked_do[h])
            dk = dk + mm(dscores, masked_q[h])
            part = mm(keys_t[h * HEAD_DIM : (h + 1) * HEAD_DIM, :], dscores)
            dq[h] = part if e == 0 else dq[h] + part
        grad[:, :LANES] = dk.astype(BF)
        grad[:, LANES:] = dv.astype(BF)
    dq_all = jnp.concatenate(dq + [jnp.zeros((HEAD_DIM, rows), F32)], axis=0).T * 0.125
    dq_ref[...] = rotate(dq_all, cos[...], -sin[...]).astype(BF)


def mlp_back_body(a0, a1, a2, a3, slope, w_up, rows, grad_ref, dx_ref):
    g_all = jnp.concatenate([a0[...], a1[...], a2[...], a3[...]], axis=0)
    grad_up = (mm_nt(g_all, down_rows(rows)) * slope[...].astype(F32)).astype(BF)
    grad_ref[...] = grad_up
    dx_ref[...] = mm_nt(grad_up, w_up[...])


def weight_grads_body(a0, a1, a2, a3, hidden, mid, x_ref, grad_qkv, grad_up, out_ref):
    step = pl.program_id(0)

    @pl.when(step == 0)
    def rows_part():
        g_all = jnp.concatenate([a0[...], a1[...], a2[...], a3[...]], axis=0)
        down_grad = mm_tn(hidden[...], g_all).astype(BF)
        out_grad = mm_tn(mid[...], g_all).astype(BF)
        sums = jnp.sum(g_all.astype(F32), axis=0, keepdims=True)
        sums = jnp.broadcast_to(sums, (PACK - OWN_ROWS, WIDTH)).astype(BF)
        for j in range(RING):
            at = j * LANES
            out_ref[at : at + OWN_ROWS, :] = out_grad[j * OWN_ROWS : (j + 1) * OWN_ROWS]
            out_ref[at + OWN_ROWS : at + OWN_ROWS + SPOT, :] = down_grad[j * SPOT : (j + 1) * SPOT]
            out_ref[at + OWN_ROWS + SPOT : at + LANES, :] = sums

    @pl.when(step == 1)
    def up_part():
        out_ref[...] = mm_tn(x_ref[...], grad_up[...]).astype(BF)

    @pl.when(step == 2)
    def qkv_part():
        out_ref[...] = mm_tn(x_ref[...], grad_qkv[...]).astype(BF)


def qkv_back_body(
    dq, g0, g1, g2, g3, cos, sin, w_qkv, dx_up, feature, grad_ref, d0, d1, d2, d3
):
    dkv = g0[...].astype(F32)
    for part in (g1, g2, g3):
        dkv = dkv + part[...].astype(F32)
    dk = rotate(dkv[:, :LANES], cos[...], -sin[...])
    grad = jnp.concatenate([dq[...], dk.astype(BF), dkv[:, LANES:].astype(BF)], axis=1)
    grad_ref[...] = grad
    dx = (mm_nt(grad, w_qkv[...]) + dx_up[...]).astype(BF)
    store_parts(mm_nt(dx, places(feature)), (d0, d1, d2, d3))


def own_piece(row, place):
    size = row.shape[1] // (RING * RING)
    return sum(
        jnp.where(place == f, row[:, f * size : (f + 1) * size], 0.0) for f in range(RING * RING)
    )


def finish_body(
    place_ref, l0, l1, r0, r1, gain1, bias1, gain2, bias2, w_qkv, w_up,
    gain1_ref, bias1_ref, gain2_ref, bias2_ref, qkv_ref, b_qkv_ref, out_ref, b_out_ref, up_ref, b_up_ref, down_ref
):
    place = place_ref[0]

    def total(low, high):
        return jnp.concatenate(
            [
                one[:, low:high].astype(F32) + two[:, low:high].astype(F32)
                for one, two in ((l0, r0), (l1, r1))
            ],
            axis=0,
        )

    m = total(0, WIDTH)
    m_qkv = jnp.concatenate(
        [
            m[t * PACK : (t + 1) * PACK, i * LANES : i * LANES + SPOT]
            for i in range(3)
            for t in range(RING)
        ],
        axis=1,
    )
    m = total(WIDTH, 2 * WIDTH)
    m_up = jnp.concatenate([m[t * PACK : (t + 1) * PACK] for t in range(RING)], axis=1)
    rows = total(2 * WIDTH, 3 * WIDTH)
    out_ref[...] = rows[:OWN_ROWS]
    down_ref[...] = rows[OWN_ROWS : OWN_ROWS + SPOT]
    b_out_ref[...] = own_piece(rows[OWN_ROWS + SPOT : OWN_ROWS + SPOT + 1], place)
    for m, w_ref, gain, bias, gain_ref, bias_ref, grad_ref in (
        (m_qkv, w_qkv, gain1, bias1, gain1_ref, bias1_ref, qkv_ref),
        (m_up, w_up, gain2, bias2, gain2_ref, bias2_ref, up_ref),
    ):
        ends = m[OWN_ROWS : OWN_ROWS + 1]
        m = m[:OWN_ROWS]
        weight = w_ref[...].astype(F32)
        all_ones = jnp.ones((8, m.shape[1]), F32)
        gain_ref[...] = mm_exact(all_ones, weight * m)[0:1]
        bias_ref[...] = mm_exact(all_ones, weight * ends)[0:1]
        grad_ref[...] = as_column(gain[...].astype(F32)) * m + as_column(bias[...].astype(F32)) * ends
    ends = m_qkv[OWN_ROWS : OWN_ROWS + 1]
    b_qkv_ref[...] = jnp.concatenate(
        [own_piece(ends[:, i * WIDTH : (i + 1) * WIDTH], place) for i in range(3)], axis=0
    )
    b_up_ref[...] = own_piece(m_up[OWN_ROWS : OWN_ROWS + 1], place)


def unit_rows_of(rows):
    centered = rows - jnp.mean(rows, axis=-1, keepdims=True)
    inv_std = lax.rsqrt(jnp.mean(centered * centered, axis=-1, keepdims=True) + EPSILON)
    return centered * inv_std, inv_std


def forward_layer(tok_rows, xs, weights, geometry, order, mlp_first):
    w_qkv, w_up, w_rows = weights
    starts, info, tables = geometry
    own = tok_rows.shape[0]
    rows = RING * own
    outs = (like((rows, RING * LANES), BF), like((rows, LANES), BF), like((rows, 2 * LANES), BF))
    if isinstance(w_qkv, list):
        at, *blocks = w_qkv
        x_all, q, kv, w_qkv = vmem_call(
            project_turned_body,
            outs + (like((RING * LANES, WIDTH), BF),),
            1_600_000_000,
            (at,),
            *xs,
            *order,
            *blocks,
            *tables,
        )
    else:
        x_all, q, kv = vmem_call(
            project_body, outs, 1_600_000_000, (), *xs, *order, w_qkv, *tables
        )
    kvs = in_order([kv] + [send(kv, along_tokens(-by)) for by in (1, 3, 2)])
    whole = (like((rows, WIDTH), F32),)
    cut = (like((own, WIDTH), F32),) + (like((own, WIDTH), BF),) * (RING - 1)

    def mlp(attended, outs):
        return vmem_call(
            mlp_body,
            (like((rows, WIDTH), BF), like((rows, WIDTH), BF)) + outs,
            2_000_000_000,
            (),
            x_all,
            w_up,
            w_rows,
            *attended,
        )

    def attention(others, outs):
        return vmem_call(
            attend_body,
            (like((rows, LANES), BF), like((8, rows), F32)) + outs,
            6_000_000_000,
            (starts,),
            info,
            q,
            *kvs,
            *others,
        )

    if mlp_first:
        hidden, slope, partial = mlp((), whole)
        mid, lse, *parts = attention((w_rows, partial), cut)
    else:
        mid, lse = attention((), ())
        hidden, slope, *parts = mlp((mid,), cut)
    total = tok_rows + parts[0]
    for by in (1, 3, 2):
        total = total + send(parts[by], along_weights(by)).astype(F32)
    return total, (x_all, q, kvs, hidden, slope, mid, lse), w_qkv


def backward_layer(
    grad_rows, gs, unit, inv_std, weights, stored, geometry, order, tie, late
):
    w_qkv, w_up, w_rows = weights
    starts, info, tables = geometry
    x_all, q, kvs, hidden, slope, mid, lse = stored
    own = grad_rows.shape[0]
    rows = RING * own

    def attention_back(gs):
        return vmem_call(
            attend_back_body,
            (like((rows, LANES), BF),) + (like((rows, 2 * LANES), BF),) * RING,
            16_000_000_000,
            (starts,),
            info,
            q,
            *gs,
            w_rows,
            mid,
            lse,
            *tables,
            *kvs,
        )

    dq, *dkvs = attention_back(gs)
    received = [send(dkvs[by], along_tokens(by)) for by in (1, 3, 2)]
    grad_up, dx_up = vmem_call(
        mlp_back_body,
        (like((rows, WIDTH), BF), like((rows, RING * LANES), F32)),
        1_600_000_000,
        (),
        *([after(gs[0], *tie)] + gs[1:]),
        slope,
        w_up,
        w_rows,
    )
    grad_qkv, *dxs = vmem_call(
        qkv_back_body,
        (like((rows, WIDTH), BF),) + (like((own, WIDTH), BF),) * RING,
        2_000_000_000,
        (),
        dq,
        dkvs[0],
        *received,
        *tables,
        w_qkv,
        dx_up,
        order[0],
    )
    total = dxs[0].astype(F32)
    for by in (1, 3, 2):
        total = total + send(dxs[by], along_weights(by)).astype(F32)
    grad_in = grad_rows.astype(F32) + inv_std * (
        total
        - jnp.mean(total, axis=-1, keepdims=True)
        - unit * jnp.mean(total * unit, axis=-1, keepdims=True)
    )
    grad_in = grad_in.astype(BF)
    cuts = vmem_call(
        weight_grads_body,
        like((RING * LANES, 3 * WIDTH), BF),
        3_000_000_000,
        (),
        *gs,
        hidden,
        mid,
        x_all,
        after(grad_qkv, *((grad_in,) if late else ())),
        grad_up,
        steps=3,
    )
    return grad_in, scatter_tokens_axis(cuts), cuts


def over_weights(total, tp):
    parts = [total[:PACK]] + [
        send(total[by * PACK : (by + 1) * PACK], along_weights(by)) for by in (1, 3, 2)
    ]
    near = in_order(parts)
    return turned([near[0], near[3], near[2], near[1]], tp)


def to_core(value, core):
    return send(value, moves(lambda s, a, b: flat(core, a, b) if s != core else None))


def over_replicas(low):
    rest = lax.axis_size("replica")

    def swapped(value, partner):
        return lax.ppermute(value, "replica", [(i, partner(i)) for i in range(rest)])

    def inner(i):
        return i ^ 1

    def outer(i):
        return rest - 1 - i

    half = low.shape[0] // 2
    left, right = low[:half], low[half:]
    left = (left.astype(F32) + swapped(left, inner).astype(F32)).astype(BF)
    right = (right.astype(F32) + swapped(right, outer).astype(F32)).astype(BF)
    return left, right, swapped(left, outer), swapped(right, inner)


def on_device(
    pipe_ends,
    seq_lengths,
    norm1_gain,
    norm1_bias,
    norm2_gain,
    norm2_bias,
    qkv_weight,
    qkv_bias,
    out_weight,
    out_bias,
    up_weight,
    up_bias,
    down_weight,
    down_bias,
):
    core = lax.axis_index("section")
    first = core == 0
    place = lax.axis_index("fsdp")
    a_at, b_at = place // RING, place % RING
    tp = jnp.where(first, a_at, b_at)
    sq = jnp.where(first, b_at, a_at)
    rows_dev = pipe_ends.shape[3]

    def block_of(weight_at, token_at):
        weight_at, token_at = weight_at % RING, token_at % RING
        return jnp.where(first, RING * weight_at + token_at, RING * token_at + weight_at)

    ring = jnp.arange(RING, dtype=jnp.int32)
    dest = block_of(tp + ring[None, :], sq + ring[:, None]).reshape(-1).astype(jnp.int32)
    kept = block_of(tp + ring[None, :], ring[:, None]).reshape(-1).astype(jnp.int32)
    spare = jnp.arange(PACK, dtype=jnp.int32)[None, :]
    feature = jnp.where(spare < OWN_ROWS, kept[:, None] * OWN_ROWS + spare, -1).reshape(1, -1)
    ones = np.tile((np.arange(PACK) // 2 == OWN_ROWS // 2).astype(np.float32), RING * RING)
    order = (jnp.broadcast_to(feature, (8, RING * LANES)), ones[None, :])

    flags = (first.astype(jnp.int32)[None], place.astype(jnp.int32)[None])
    pack = like((RING, PACK, 2 * WIDTH), BF)
    own_pack, sent_pack, pack_down = vmem_call(
        pack_body,
        (pack, pack, like((SPOT + PACK - OWN_ROWS, WIDTH), BF)),
        1_000_000,
        flags,
        norm1_gain,
        norm1_bias,
        norm2_gain,
        norm2_bias,
        qkv_weight[0],
        qkv_bias[0],
        up_weight[0],
        up_bias,
        down_weight[0],
        out_bias,
        down_bias,
    )
    swap = moves(lambda s, a, b: flat(1 - s, a, b))

    def both(own, other):
        return jnp.where(first, own, other), jnp.where(first, other, own)

    early_pack, late_pack = both(own_pack, send(sent_pack, swap))
    other_ends = send(
        jnp.where(first, pipe_ends[0, 1, 0], pipe_ends[0, 0, 0]), swap
    )
    own_end = jnp.where(first, pipe_ends[0, 0, 0], pipe_ends[0, 1, 0])
    tokens_in = jnp.where(first, own_end, other_ends)
    cotangent = jnp.where(first, other_ends, own_end)

    lens = lax.dynamic_index_in_dim(seq_lengths[:, 0], core, 0, keepdims=False)
    starts = (dest * rows_dev).astype(jnp.int32)
    rows_at = (starts[:RING, None] + jnp.arange(rows_dev, dtype=jnp.int32)[None, :]).reshape(-1)
    finish = jnp.cumsum(lens)
    begin = jnp.sum(
        jnp.where(rows_at[None, :] >= finish[:, None], lens[:, None], 0), axis=0
    ).astype(jnp.int32)
    info = jnp.concatenate(
        [begin[None, :], rows_at[None, :], jnp.zeros((6, rows_at.shape[0]), jnp.int32)], axis=0
    )
    in_head = np.arange(2 * HEAD_DIM) % HEAD_DIM
    inv_freq = (10000.0 ** (-(in_head % 8) / 8.0)).astype(np.float32)
    inv_freq = np.where(in_head < 16, inv_freq, np.float32(0))
    angles = (rows_at - begin).astype(F32)[:, None] * inv_freq[None, :]
    tables = (jnp.cos(angles), jnp.sin(angles))
    geometry = (starts, info, tables)

    def to_columns(pack):
        def block_for(by):
            return lax.dynamic_index_in_dim(pack, (tp + by) % RING, 0, keepdims=False)

        parts = [block_for(0)] + [
            send(block_for(-by), along_weights(-by)) for by in (1, 3, 2)
        ]
        return jnp.concatenate(in_order(parts), axis=0)

    down_layers = both(pack_down, send(pack_down, swap))
    turn = moves(lambda s, a, b: flat(1, b, a) if s == 0 else flat(0, a, b))
    stay = moves(lambda s, a, b: None if s == 0 else flat(s, b, a))
    out_other = send(out_weight[0], turn)
    out_turned = send(out_weight[0], stay)
    out_layers = jnp.where(first, out_weight[0], out_other), jnp.where(first, out_other, out_turned)
    row_packs = [jnp.concatenate([out_layers[i], down_layers[i]], axis=0) for i in range(2)]

    rows = gather_tokens_axis(jnp.concatenate(row_packs, axis=1))
    unit0, inv_std0 = unit_rows_of(tokens_in.astype(F32))
    xs0 = in_order(gathered_weights_axis(unit0.astype(BF)))
    columns = jnp.concatenate([early_pack, late_pack], axis=2)
    columns = to_columns(after(columns, *row_packs))
    columns = after(columns, *xs0, info, *tables, rows)
    qkv0 = columns[:, :WIDTH]
    qkv0 = in_order([qkv0] + [send(qkv0, along_tokens(-by)) for by in (1, 3, 2)])
    qkv0 = [sq.astype(jnp.int32)[None]] + qkv0
    up0 = gather_tokens_axis(columns[:, WIDTH : 2 * WIDTH])
    weights0 = (qkv0, up0, (rows, 0))

    out0, stored0, qkv0 = forward_layer(
        tokens_in.astype(F32), xs0, weights0, geometry, order, False
    )
    weights0 = (qkv0, up0, (rows, 0))
    gs1 = in_order(gathered_weights_axis(after(cotangent, stored0[1])))
    all1 = gather_tokens_axis(after(columns[:, 2 * WIDTH :], *stored0[2]))
    weights1 = ((all1, 0), (all1, 1), (rows, 1))
    low0 = out0.astype(BF)
    unit1, inv_std1 = unit_rows_of(low0.astype(F32))
    xs1 = in_order(gathered_weights_axis(unit1.astype(BF)))
    out1, stored1, unused = forward_layer(
        low0.astype(F32), xs1, weights1, geometry, order, True
    )
    low1 = out1.astype(BF)

    def up_swapped(value):
        value = value.reshape(RING, PACK, RING, SPOT)
        return value.transpose(2, 1, 0, 3).reshape(RING * PACK, WIDTH)

    def rows_turned(rows):
        out_part = jnp.where(first, rows[:OWN_ROWS], send(rows[:OWN_ROWS], stay))
        return jnp.concatenate([out_part, rows[OWN_ROWS:]], axis=0)

    def joined(part, layer):
        return (part.astype(F32) + to_core(part, layer).astype(F32)).astype(BF)

    def joined_up(part, layer):
        return joined(jnp.where(first, part, up_swapped(part)), layer)

    grad1, scattered1, unused = backward_layer(
        cotangent,
        gs1,
        unit1,
        inv_std1,
        weights1,
        stored1,
        geometry,
        order,
        (low1,),
        True,
    )
    gs0 = in_order(gathered_weights_axis(grad1))

    def swapped_rows(early, late):
        other = send(jnp.where(first, late, early), swap)
        mine = jnp.where(first, early, late)
        stacked = jnp.stack([jnp.where(first, mine, other), jnp.where(first, other, mine)])
        return stacked[None, :, None], other

    layer_out, out_other = swapped_rows(low0, low1)

    def to_owner(scattered, columns, layer):
        return jnp.concatenate(
            [
                joined(columns[:, :WIDTH], layer),
                joined_up(columns[:, WIDTH:], layer),
                joined(rows_turned(scattered[:, 2 * WIDTH :]), layer),
            ],
            axis=1,
        )

    grad0, scattered0, cuts0 = backward_layer(
        grad1,
        gs0,
        unit0,
        inv_std0,
        weights0,
        stored0,
        geometry,
        order,
        (out_other,),
        False,
    )
    scattered1 = after(scattered1, cuts0, grad0)
    columns1 = over_weights(scattered1[:, : 2 * WIDTH], tp)
    owned1 = to_owner(scattered1, columns1, 1)
    input_grad, grad_other = swapped_rows(grad0, grad1)
    scattered0 = after(scattered0, owned1, grad_other)
    columns0 = over_weights(scattered0[:, : 2 * WIDTH], tp)
    parts = over_replicas(jnp.where(first, to_owner(scattered0, columns0, 0), owned1))

    vector = like((1, OWN_ROWS), F32)
    gain1_grad, bias1_grad, gain2_grad, bias2_grad, *grads = vmem_call(
        finish_body,
        (
            vector,
            vector,
            vector,
            vector,
            like((OWN_ROWS, 3 * WIDTH), F32),
            like((3, OWN_ROWS), F32),
            like((OWN_ROWS, WIDTH), F32),
            vector,
            like((OWN_ROWS, RING * WIDTH), F32),
            like((1, SPOT), F32),
            like((SPOT, WIDTH), F32),
        ),
        10_000_000,
        flags[1:],
        *parts,
        norm1_gain,
        norm1_bias,
        norm2_gain,
        norm2_bias,
        qkv_weight[0],
        up_weight[0],
    )
    qkv_grad, qkv_bias_grad, out_grad, end_grad, up_grad, up_bias_grad, down_grad = grads
    return (
        layer_out,
        input_grad,
        gain1_grad,
        bias1_grad,
        gain2_grad,
        bias2_grad,
        qkv_grad[None],
        qkv_bias_grad[None],
        out_grad[None],
        end_grad,
        up_grad[None],
        up_bias_grad,
        down_grad[None],
        end_grad,
    )


def solution(mesh):
    tokens = P("section", None, "replica", "fsdp", None)
    vector = P("section", "fsdp")
    matrix = P("section", "fsdp", None)
    three = P("section", None, "fsdp")
    params = (
        vector,
        vector,
        vector,
        vector,
        matrix,
        three,
        matrix,
        vector,
        matrix,
        vector,
        matrix,
        vector,
    )
    return jax.shard_map(
        on_device,
        mesh=mesh,
        in_specs=(tokens, P(None, "replica", None)) + params,
        out_specs=(tokens, tokens) + params,
        check_vma=False,
    )
```
